32 devices in a mesh: leaf: 16 (over z, y, x), grp: 2 (over core).
Axes of the slice: x: 2, y: 2, z: 4, core: 2. Of those that a mesh axis runs over, the one named last changes fastest.
Arguments:
- points: bfloat16 [256, 32768], P(None, ('leaf', 'grp')), may hold values from -6 to 6
- charges: bfloat16 [64, 32768], P(None, ('leaf', 'grp')), may hold values from -6 to 6
- order: int32 [32768], P(('leaf', 'grp')), may hold values from 0 to 1023, as said below
- near_mask: int32 [32, 5], P(('leaf', 'grp')), may hold values from 0 to 1, as said below
- skeletons: int32 [32, 5, 128], P(('leaf', 'grp')), may hold values from 0 to 1023, as said below
- leaf_interp: bfloat16 [128, 32768], P(None, ('leaf', 'grp')), may hold values from -0.5 to 0.5
- transfer: bfloat16 [32, 4, 128, 128], P(('leaf', 'grp')), as said below
Outputs:
- potentials: float32 [64, 32768], P(None, ('leaf', 'grp'))
The draws below stay inside these ranges and needn't reach their ends.
Inputs may be any that keep to these rules, and one draw needn't show every extreme that they name: `order`: within each block of 1024 consecutive entries, a permutation of 0 to 1023. `near_mask`: entry 2 of every row is 1; an entry is 0 where it points outside the leaf coordinates; the pattern is symmetric: block b marks the block k leaf coordinates away exactly when that block marks b. Level 0 holds 128 different rows of the block; level j >= 1 holds 128 different positions of 0 to 255 in the two children's skeletons; the set of a node is the same on every block of that node. `transfer`: the matrix of a node is the same on every block of that node.
All inputs are finite; a program needn't handle non-finite values.
Results may differ from the reference program's by a relative error of at most 0.0019.
Values may be sent and summed in bfloat16 or wider, within the bound.
No kernel may reach another device: no remote copies, remote signals or barrier semaphores. Data moves between devices by JAX's collectives and lax.ppermute only.
A program may use at most 64 MiB of HBM per device.

```python
import jax
import jax.numpy as jnp
from jax import lax

DIM = 256
RHS = 64
SK = 128
LEAF = 1024
REACH = 2
LEVELS = 4
BLOCKS = 32
ROWS = 32768
N_LEAF = 16
N_GRP = 2


def draw_points(key, part):
    values = jnp.clip(jax.random.normal(key, (DIM, ROWS), jnp.float32), -6.0, 6.0)
    return values.astype(jnp.bfloat16)


def draw_order(key, part):
    subkeys = jax.random.split(key, BLOCKS)
    shuffled = jax.vmap(lambda subkey: jax.random.permutation(subkey, LEAF))(subkeys)
    return shuffled.reshape(-1).astype(jnp.int32)


def draw_near_mask(key, part):
    coin_flips = jax.random.randint(key, (N_LEAF, N_GRP, REACH), 0, 2, dtype=jnp.int32)
    leaf_coord = jnp.arange(N_LEAF, dtype=jnp.int32)[:, None]
    upward = []
    for distance in range(1, REACH + 1):
        inside = (leaf_coord + distance < N_LEAF).astype(jnp.int32)
        upward.append(coin_flips[:, :, distance - 1] * inside)
    downward = []
    for distance in range(1, REACH + 1):
        moved = jnp.pad(upward[distance - 1], ((distance, 0), (0, 0)))[:N_LEAF]
        downward.append(moved)
    columns = [downward[distance - 1] for distance in range(REACH, 0, -1)]
    columns = columns + [jnp.ones((N_LEAF, N_GRP), jnp.int32)] + upward
    return jnp.stack(columns, axis=2).reshape(BLOCKS, 2 * REACH + 1).astype(jnp.int32)


def draw_skeletons(key, part):
    per_level = []
    for level in range(LEVELS + 1):
        count = (N_LEAF >> level) * N_GRP
        span = LEAF if level == 0 else 2 * SK
        subkeys = jax.random.split(jax.random.fold_in(key, level), count)
        chosen = jax.vmap(lambda subkey: jax.random.permutation(subkey, span)[:SK])(subkeys)
        if level == 0:
            node_ids = jnp.arange(count, dtype=jnp.int32)
            wanted = jnp.where(node_ids == 0, span - 1, 0)
            moved_by = (wanted - chosen[:, 0]) % span
            chosen = jnp.where((node_ids < 2)[:, None], (chosen + moved_by[:, None]) % span, chosen)
        chosen = chosen.reshape(N_LEAF >> level, N_GRP, SK)
        per_level.append(jnp.repeat(chosen, 2 ** level, axis=0))
    return jnp.stack(per_level, axis=2).reshape(BLOCKS, LEVELS + 1, SK).astype(jnp.int32)


def draw_transfer(key, part):
    per_level = []
    for level in range(LEVELS):
        count = N_LEAF >> level
        level_key = jax.random.fold_in(key, 100 + level)
        values = jax.random.normal(level_key, (count, N_GRP, SK, SK), jnp.float32)
        values = values / jnp.sqrt(2.0 * SK)
        per_level.append(jnp.repeat(values, 2 ** level, axis=0))
    return jnp.stack(per_level, axis=2).reshape(BLOCKS, LEVELS, SK, SK).astype(jnp.bfloat16)


def level_of(key, extent, pieces, low, high):
    loudness, own = 1.0, jax.random.fold_in(key, 6)
    for position, blocks in pieces:
        heights = jnp.exp(jax.random.uniform(jax.random.fold_in(own, position), (blocks,), jnp.float32, low / len(pieces), high / len(pieces)))
        loudness = loudness * jnp.repeat(heights, extent[position] // blocks).reshape([-1 if axis == position else 1 for axis in range(len(extent))])
    return loudness


def noise(rng, extent, deviation, bound, shards=(), kind=jnp.bfloat16):
    entries = jax.random.normal(rng, extent, jnp.float32) * deviation
    if len(shards) > 0:
        entries = level_of(rng, extent, shards, -0.22, 0.18) * entries
    return jnp.clip(entries, min=-bound, max=bound).astype(kind)


def setup_inputs(seed: int = 0) -> dict:
    splits = jax.random.split(jax.random.key(seed), 8)
    points = draw_points(jax.random.fold_in(splits[7], 71), 0)
    charges = noise(splits[1], (RHS, ROWS), 1.0, 6.0, ((1, 32),))
    order = draw_order(jax.random.fold_in(splits[7], 71), 0)
    near_mask = draw_near_mask(jax.random.fold_in(splits[7], 71), 0)
    skeletons = draw_skeletons(jax.random.fold_in(splits[7], 71), 0)
    leaf_interp = noise(splits[5], (SK, ROWS), SK ** -0.5, 0.5, ((1, 32),))
    transfer = draw_transfer(jax.random.fold_in(splits[7], 71), 0)
    return dict(points=points, charges=charges, order=order, near_mask=near_mask, skeletons=skeletons, leaf_interp=leaf_interp, transfer=transfer)


def pair_kernel(source, target):
    source_wide = source.astype(jnp.float32)
    target_wide = target.astype(jnp.float32)
    source_square = jnp.sum(source_wide * source_wide, axis=0)
    target_square = jnp.sum(target_wide * target_wide, axis=0)
    inner = jnp.dot(source.T, target, preferred_element_type=jnp.float32)
    return jnp.exp(-2.0 * (source_square[:, None] + target_square[None, :] - 2.0 * inner) / DIM)


def reference(points, charges, order, near_mask, skeletons, leaf_interp, transfer):
    highest = lax.Precision.HIGHEST
    ordered = jnp.take_along_axis(charges.reshape(RHS, BLOCKS, LEAF), order.reshape(1, BLOCKS, LEAF), axis=2).reshape(RHS, BLOCKS * LEAF)

    def near_block(block_id):
        leaf_coord = block_id // N_GRP
        group_id = block_id % N_GRP
        target = lax.dynamic_slice_in_dim(points, block_id * LEAF, LEAF, axis=1)
        running = jnp.zeros((RHS, LEAF), jnp.float32)
        for offset in range(-REACH, REACH + 1):
            neighbour = leaf_coord + offset
            usable = (neighbour >= 0) & (neighbour < N_LEAF) & (near_mask[block_id, offset + REACH] == 1)
            source_id = (jnp.clip(neighbour, 0, N_LEAF - 1) * N_GRP + group_id).astype(jnp.int32)

            def add_tile(carry, source_id=source_id):
                source = lax.dynamic_slice_in_dim(points, source_id * LEAF, LEAF, axis=1)
                source_charges = lax.dynamic_slice_in_dim(ordered, source_id * LEAF, LEAF, axis=1)
                tile = pair_kernel(source, target).astype(jnp.bfloat16)
                return carry + jnp.dot(source_charges, tile, preferred_element_type=jnp.float32)

            running = lax.cond(usable, add_tile, lambda carry: carry, running)
        return running

    near_field = lax.map(near_block, jnp.arange(BLOCKS, dtype=jnp.int32))

    blocked_points = points.reshape(DIM, BLOCKS, LEAF)
    blocked_interp = leaf_interp.reshape(SK, BLOCKS, LEAF).astype(jnp.float32)
    blocked_ordered = ordered.reshape(RHS, BLOCKS, LEAF).astype(jnp.float32)
    weights_now = jnp.einsum("rbl,kbl->brk", blocked_ordered, blocked_interp, precision=highest)
    weights_now = weights_now.reshape(N_LEAF, N_GRP, RHS, SK)
    coords = jnp.take_along_axis(blocked_points, skeletons[:, 0, :][None], axis=2)
    coords = jnp.transpose(coords, (1, 0, 2)).reshape(N_LEAF, N_GRP, DIM, SK)
    skeleton_table = skeletons.reshape(N_LEAF, N_GRP, LEVELS + 1, SK)
    transfer_table = transfer.reshape(N_LEAF, N_GRP, LEVELS, SK, SK)
    history = []
    for level in range(1, LEVELS + 1):
        stride = 2 ** (level - 1)
        matrices = transfer_table[::stride, :, level - 1].astype(jnp.float32)
        contrib = jnp.einsum("lgrk,lgmk->lgrm", weights_now, matrices, precision=highest)
        history.append((weights_now, coords))
        joined = jnp.concatenate([coords[0::2], coords[1::2]], axis=3)
        chosen = skeleton_table[::2 * stride, :, level]
        coords = jnp.take_along_axis(joined, chosen[:, :, None, :], axis=3)
        weights_now = contrib[0::2] + contrib[1::2]

    top_coords = coords[0]
    top_weights = weights_now[0]
    kernels = jax.vmap(lambda source: jax.vmap(lambda target: pair_kernel(source, target))(top_coords))(top_coords)
    keep = (jnp.arange(N_GRP)[:, None] != jnp.arange(N_GRP)[None, :]).astype(jnp.float32)
    potential = jnp.einsum("hrk,hgkm->grm", top_weights, kernels * keep[:, :, None, None], precision=highest)[None]

    for level in range(LEVELS, 0, -1):
        child_weights, child_coords = history[level - 1]
        count = child_weights.shape[0]
        matrices = transfer_table[::2 ** (level - 1), :, level - 1].astype(jnp.float32)
        inherited = jnp.repeat(potential, 2, axis=0)
        sibling_weights = child_weights.reshape(count // 2, 2, N_GRP, RHS, SK)[:, ::-1].reshape(child_weights.shape)
        sibling_coords = child_coords.reshape(count // 2, 2, N_GRP, DIM, SK)[:, ::-1].reshape(child_coords.shape)
        sibling_kernels = jax.vmap(jax.vmap(pair_kernel))(sibling_coords, child_coords)
        potential = jnp.einsum("lgrk,lgkm->lgrm", inherited, matrices, precision=highest) + jnp.einsum("lgrk,lgkm->lgrm", sibling_weights, sibling_kernels, precision=highest)

    far_field = jnp.einsum("brk,kbl->rbl", potential.reshape(BLOCKS, RHS, SK), blocked_interp, precision=highest)
    near_moved = jnp.transpose(near_field, (1, 0, 2))
    return (near_moved + far_field).reshape(RHS, BLOCKS * LEAF)
```

```python
import functools

import jax
import jax.numpy as jnp
from jax import lax
from jax.experimental import pallas as pl
from jax.experimental.pallas import tpu as pltpu
from jax.sharding import PartitionSpec as P

REACH = 2
PIECES = 2
BF16 = jnp.bfloat16
F32 = jnp.float32
LOG2E = 1.4426950408889634
HIGHEST = lax.Precision.HIGHEST
PAD = 16
VMEM_LIMIT = 40 * 1024 * 1024

NN = ((1,), (0,))
NT = ((1,), (1,))
TN = ((0,), (0,))


def dot(left, right, contract=NN, precision=None):
    return lax.dot_general(
        left, right, (contract, ((), ())), preferred_element_type=F32, precision=precision
    )


def halves(value):
    high = value.astype(BF16)
    return high, (value - high.astype(F32)).astype(BF16)


def row_norms(points):
    wide = points.astype(F32)
    return jnp.sum(wide * wide, axis=0, keepdims=True)


def column_norms(points):
    wide = points.astype(F32)
    high, low = halves(wide * wide)
    ones = jnp.ones((points.shape[0], 128), BF16)
    return dot(high, ones, TN) + dot(low, ones, TN)


def one_hot(index, rows, first):
    place = lax.broadcasted_iota(jnp.int32, (rows, index.shape[1]), 0) + first
    return jnp.where(place == index, 1.0, 0.0).astype(BF16)


def small_kernel(source, target):
    scale = 2.0 * LOG2E / source.shape[0]
    inner = dot(source, target, TN)
    squares = column_norms(source)[:, : target.shape[1]] + row_norms(target)
    return jnp.exp2(scale * (2.0 * inner - squares))


def pick(first, second, index, bit):
    count = first.shape[1]
    table = jnp.concatenate(
        [one_hot(index, count, count * bit), one_hot(index, count, count * (1 - bit))], axis=0
    )
    return dot(jnp.concatenate([first, second], axis=1), table).astype(BF16)


def write_messages(weights, coords, transfers, index, near_ref, far_ref, sum_ref):
    dimension, sides = coords.shape[0], weights.shape[0]
    once = dot(weights, transfers[0].astype(F32), NT, HIGHEST)
    near_ref[:dimension] = coords
    near_ref[dimension : dimension + sides] = weights.astype(BF16)
    if len(transfers) == 1:
        near_ref[dimension + sides :] = once.astype(BF16)
        sum_ref[...] = once
        return
    twice = dot(once, transfers[1].astype(F32), NT, HIGHEST)
    near_ref[dimension + sides :] = twice.astype(BF16)
    far_ref[:dimension] = coords
    far_ref[dimension : dimension + sides] = once.astype(BF16)
    far_ref[dimension + sides : dimension + 2 * sides] = twice.astype(BF16)
    far_ref[dimension + 2 * sides :] = jnp.broadcast_to(
        index.astype(F32), (PAD, index.shape[1])
    ).astype(BF16)
    sum_ref[...] = twice


def start_kernel(bits, points, charges, order, skeletons, interp, transfer, *outs):
    pieces, (ordered_ref, coords_ref), messages = outs[:PIECES], outs[PIECES : PIECES + 2], outs[PIECES + 2 :]
    dimension, rows = points.shape
    sides = charges.shape[0]
    coords = dot(points[...], one_hot(skeletons[0:1, :], rows, 0)).astype(BF16)
    coords_ref[...] = coords
    width = rows // 4
    for column in range(0, rows, width):
        table = one_hot(order[:, column : column + width], rows, 0)
        ordered_ref[:, column : column + width] = dot(charges[...], table).astype(BF16)
    weights = dot(ordered_ref[...], interp[...], NT)
    far = messages[1] if bits == 2 else None
    write_messages(
        weights,
        coords,
        [transfer[level] for level in range(bits)],
        skeletons[1:2, :],
        messages[0],
        far,
        messages[-1],
    )
    size = rows // PIECES
    for piece in range(PIECES):
        pieces[piece][:dimension] = points[:, piece * size : (piece + 1) * size]
        pieces[piece][dimension:] = ordered_ref[:, piece * size : (piece + 1) * size]


def round_kernel(level, bits, later, skeletons, transfer, coords, total, *refs):
    position = lax.axis_index("leaf")
    dimension, count = coords.shape
    sides = total.shape[0]
    low = (position >> level) & 1
    if bits == 2:
        first, second, third = (ref[...] for ref in refs[:3])
        coords_up_ref, sibling_coords_ref, sibling_weights_ref = refs[3:6]
        outs = refs[6:]
        high = (position >> (level + 1)) & 1
        middle = pick(coords[...], first[:dimension], skeletons[level + 1 : level + 2, :], low)
        index = second[dimension + 2 * sides : dimension + 2 * sides + 1].astype(F32).astype(jnp.int32)
        sibling = pick(second[:dimension], third[:dimension], index, low)
        coords_up_ref[...] = middle
        sibling_coords_ref[...] = sibling
        span = slice(dimension, dimension + sides)
        sibling_weights_ref[...] = second[span].astype(F32) + third[span].astype(F32)
        top = pick(middle, sibling, skeletons[level + 2 : level + 3, :], high)
        span = slice(dimension + sides, dimension + 2 * sides)
        weights = (
            (total[...] + first[span].astype(F32))
            + (second[span].astype(F32) + third[span].astype(F32))
        )
    else:
        first = refs[0][...]
        outs = refs[1:]
        top = pick(coords[...], first[:dimension], skeletons[level + 1 : level + 2, :], low)
        weights = total[...] + first[dimension + sides :].astype(F32)
    level += bits
    if later == 0:
        outs[0][:dimension] = top
        outs[0][dimension:] = weights.astype(BF16)
        return
    outs[0][...] = top
    write_messages(
        weights,
        top,
        [transfer[level + step] for step in range(later)],
        skeletons[level + 1 : level + 2, :],
        outs[1],
        outs[2] if later == 2 else None,
        outs[-1],
    )


def sibling_kernel(bits, sides, coords, first, *refs):
    dimension = coords.shape[0]
    weights = first[dimension : dimension + sides].astype(F32)
    refs[-bits][...] = dot(weights, small_kernel(first[:dimension], coords[...]), NN, HIGHEST)
    if bits == 2:
        coords_up, sibling_coords, sibling_weights = refs[:3]
        refs[-1][...] = dot(
            sibling_weights[...], small_kernel(sibling_coords[...], coords_up[...]), NN, HIGHEST
        )


def self_kernel(points, ordered, transposed_ref, norms_ref, near_ref):
    dimension, rows = points.shape
    scale = 2.0 * LOG2E / dimension
    transposed_ref[...] = jnp.transpose(points[...].astype(F32)).astype(BF16)
    norms_ref[...] = column_norms(points[...]) * scale
    source_norms = row_norms(points[...]) * scale
    height = min(256, rows)
    for row in range(0, rows, height):
        band = slice(row, row + height)
        inner = dot(transposed_ref[band], points[...])
        squares = jnp.tile(norms_ref[band], (1, rows // 128)) + source_norms
        tile = jnp.exp2((2.0 * scale) * inner - squares).astype(BF16)
        near_ref[:, band] = dot(ordered[...], tile, NT)


def near_kernel(column, mask, piece, transposed, norms, ordered, total, near_ref, back_ref):
    rows, dimension = transposed.shape
    width = piece.shape[1]
    scale = 2.0 * LOG2E / dimension

    @pl.when(mask[0, column] > 0)
    def _():
        source_norms = row_norms(piece[:dimension]) * scale
        height = min(256, rows)
        back = None
        for row in range(0, rows, height):
            band = slice(row, row + height)
            inner = dot(transposed[band], piece[:dimension])
            squares = jnp.tile(norms[band], (1, width // 128)) + source_norms
            tile = jnp.exp2((2.0 * scale) * inner - squares).astype(BF16)
            near_ref[:, band] = total[:, band] + dot(piece[dimension:], tile, NT)
            part = dot(ordered[:, band], tile)
            back = part if back is None else back + part
        back_ref[...] = back.astype(BF16)

    @pl.when(mask[0, column] <= 0)
    def _():
        near_ref[...] = total[...]
        back_ref[...] = jnp.zeros_like(back_ref)


def final_kernel(levels, others, near, own_top, transfer, interp, *refs):
    tops, terms, returns, out_ref = (
        refs[:others],
        refs[others : others + levels],
        refs[others + levels : -1],
        refs[-1],
    )
    dimension = own_top.shape[0] - near.shape[0]
    potential = None
    for top in tops:
        part = dot(
            top[dimension:].astype(F32),
            small_kernel(top[:dimension], own_top[:dimension]),
            NN,
            HIGHEST,
        )
        potential = part if potential is None else potential + part
    for level in range(levels, 0, -1):
        term = terms[level - 1][...]
        if potential is not None:
            term = term + dot(potential, transfer[level - 1].astype(F32), NN, HIGHEST)
        potential = term
    high, low = halves(potential)
    total = near[...] + (dot(high, interp[...]) + dot(low, interp[...]))
    size = near.shape[1] // PIECES
    for piece in range(PIECES):
        span = slice(piece * size, (piece + 1) * size)
        part = total[:, span]
        for back in returns[piece::PIECES]:
            part = part + back[...].astype(F32)
        out_ref[:, span] = part


def call(kernel, outs, args, scalars=0, flops=0, exps=0, name=None):
    vmem = pl.BlockSpec(memory_space=pltpu.VMEM)
    smem = pl.BlockSpec(memory_space=pltpu.SMEM)
    specs = [smem] * scalars + [vmem] * (len(args) - scalars)
    moved = sum(a.size * a.dtype.itemsize for a in list(args) + list(outs))
    return pl.pallas_call(
        kernel,
        out_shape=outs,
        in_specs=specs,
        out_specs=[vmem] * len(outs),
        compiler_params=pltpu.CompilerParams(vmem_limit_bytes=VMEM_LIMIT),
        cost_estimate=pl.CostEstimate(flops=flops, bytes_accessed=moved, transcendentals=exps),
        name=name,
    )(*args)


def swapped(value, axis, flip):
    count = lax.axis_size(axis)
    return lax.ppermute(value, axis, [(place, place ^ flip) for place in range(count)])


def shape(dims, dtype):
    return jax.ShapeDtypeStruct(dims, dtype)


def local(points, charges, order, near_mask, skeletons, leaf_interp, transfer):
    dimension, rows = points.shape
    sides, count = charges.shape[0], leaf_interp.shape[0]
    leaves, groups = lax.axis_size("leaf"), lax.axis_size("grp")
    levels = leaves.bit_length() - 1
    skeletons, transfer = skeletons[0], transfer[0]
    size = rows // PIECES
    rounds = []
    level = 0
    while level < levels:
        rounds.append((level, min(2, levels - level)))
        level += rounds[-1][1]

    def message_shapes(bits):
        near = shape((dimension + 2 * sides, count), BF16)
        far = shape((dimension + 2 * sides + PAD, count), BF16)
        return [near] + [far] * (bits - 1) + [shape((sides, count), F32)]

    bits = rounds[0][1]
    *pieces_and, = call(
        functools.partial(start_kernel, bits),
        [shape((dimension + sides, size), BF16)] * PIECES
        + [shape((sides, rows), BF16), shape((dimension, count), BF16)]
        + message_shapes(bits),
        [points, charges, order.reshape(1, rows), skeletons, leaf_interp, transfer],
        flops=2 * sides * rows * rows,
        name="start",
    )
    pieces = pieces_and[:PIECES]
    ordered, coords = pieces_and[PIECES : PIECES + 2]
    messages, total = pieces_and[PIECES + 2 : -1], pieces_and[-1]

    def arrived(step):
        return [(place, place + step) for place in range(leaves - step)]

    two = [lax.ppermute(piece, "leaf", arrived(2)) for piece in pieces]
    one = []
    for piece in range(PIECES):
        if 2 * piece < PIECES and leaves > 2:
            even = lax.ppermute(pieces[piece], "leaf", arrived(1)[::2])
            odd = lax.ppermute(
                two[piece], "leaf", [(place + 1, place) for place in range(2, leaves, 2)]
            )
            keep = lax.axis_index("leaf") % 2 == 1
            one.append(jnp.where(keep, even, odd))
        else:
            one.append(lax.ppermute(pieces[piece], "leaf", arrived(1)))

    transposed, norms, near = call(
        self_kernel,
        [shape((rows, dimension), BF16), shape((rows, 128), F32), shape((sides, rows), F32)],
        [points, ordered],
        flops=2 * rows * rows * (dimension + sides),
        exps=rows * rows,
        name="self_tile",
    )
    returns = []
    for step, parts in ((2, two), (1, one)):
        for piece in range(PIECES):
            near, back = call(
                functools.partial(near_kernel, REACH - step),
                [shape((sides, rows), F32), shape((sides, size), BF16)],
                [near_mask, parts[piece], transposed, norms, ordered, near],
                scalars=1,
                flops=2 * rows * size * (dimension + 2 * sides),
                exps=rows * size,
                name="near_tile",
            )
            returns.append(
                lax.ppermute(back, "leaf", [(place + step, place) for place in range(leaves - step)])
            )

    terms = []
    for number, (level, bits) in enumerate(rounds):
        later = rounds[number + 1][1] if number + 1 < len(rounds) else 0
        received = [swapped(messages[0], "leaf", 1 << level)]
        if bits == 2:
            received.append(swapped(messages[1], "leaf", 2 << level))
            received.append(swapped(messages[1], "leaf", 3 << level))
        outs = []
        if bits == 2:
            outs += [shape((dimension, count), BF16)] * 2 + [shape((sides, count), F32)]
        if later == 0:
            outs += [shape((dimension + sides, count), BF16)]
        else:
            outs += [shape((dimension, count), BF16)] + message_shapes(later)
        results = call(
            functools.partial(round_kernel, level, bits, later),
            outs,
            [skeletons, transfer, coords, total] + received,
            flops=8 * dimension * count * count,
            name="join_round",
        )
        results = list(results)
        kept = results[:3] if bits == 2 else []
        terms += list(call(
            functools.partial(sibling_kernel, bits, sides),
            [shape((sides, count), F32)] * bits,
            [coords, received[0]] + kept,
            flops=8 * dimension * count * count,
            exps=2 * count * count,
            name="sibling_terms",
        ))
        results = results[len(kept) :]
        if later:
            coords, messages, total = results[0], results[1:-1], results[-1]
    own_top = results[0]
    tops = [
        lax.ppermute(own_top, "grp", [(place, (place + turn) % groups) for place in range(groups)])
        for turn in range(1, groups)
    ]
    (out,) = call(
        functools.partial(final_kernel, levels, len(tops)),
        [shape((sides, rows), F32)],
        [near, own_top, transfer, leaf_interp] + tops + terms + returns,
        flops=4 * sides * rows * count,
        name="downward",
    )
    return out


def solution(mesh):
    in_specs = (
        P(None, ("leaf", "grp")),
        P(None, ("leaf", "grp")),
        P(("leaf", "grp")),
        P(("leaf", "grp"), None),
        P(("leaf", "grp"), None, None),
        P(None, ("leaf", "grp")),
        P(("leaf", "grp"), None, None, None),
    )
    out_specs = P(None, ("leaf", "grp"))
    return jax.shard_map(local, mesh=mesh, in_specs=in_specs, out_specs=out_specs, check_vma=False)
```

```python
import functools

import jax
import jax.numpy as jnp
from jax import lax
from jax.experimental import pallas as pl
from jax.experimental.pallas import tpu as pltpu
from jax.sharding import PartitionSpec as P

REACH = 2
BF16 = jnp.bfloat16
F32 = jnp.float32
LOG2E = 1.4426950408889634
HIGHEST = lax.Precision.HIGHEST
PAD = 16
VMEM_LIMIT = 40 * 1024 * 1024
START_VMEM = 56 * 1024 * 1024

NN = ((1,), (0,))
NT = ((1,), (1,))
TN = ((0,), (0,))


def dot(left, right, contract=NN, precision=None):
    return lax.dot_general(
        left, right, (contract, ((), ())), preferred_element_type=F32, precision=precision
    )


def halves(value):
    high = value.astype(BF16)
    return high, (value - high.astype(F32)).astype(BF16)


def row_norms(points):
    wide = points.astype(F32)
    return jnp.sum(wide * wide, axis=0, keepdims=True)


def column_norms(points):
    wide = points.astype(F32)
    high, low = halves(wide * wide)
    ones = jnp.ones((points.shape[0], 128), BF16)
    return dot(high, ones, TN) + dot(low, ones, TN)


def one_hot(index, rows, first):
    place = lax.broadcasted_iota(jnp.int32, (rows, index.shape[1]), 0) + first
    return jnp.where(place == index, 1.0, 0.0).astype(BF16)


def small_kernel(source, target):
    scale = 2.0 * LOG2E / source.shape[0]
    inner = dot(source, target, TN)
    squares = column_norms(source)[:, : target.shape[1]] + row_norms(target)
    return jnp.exp2(scale * (2.0 * inner - squares))


def pick(first, second, index, bit):
    count = first.shape[1]
    table = jnp.concatenate(
        [one_hot(index, count, count * bit), one_hot(index, count, count * (1 - bit))], axis=0
    )
    return dot(jnp.concatenate([first, second], axis=1), table).astype(BF16)


def write_messages(weights, coords, transfers, index, near_row, near_ref, far_ref, sum_ref):
    dimension, (sides, count) = coords.shape[0], weights.shape
    first = transfers[0].astype(F32)
    once = dot(weights, first, NT, HIGHEST)
    summed = once
    if len(transfers) == 2:
        summed = dot(once, transfers[1].astype(F32), NT, HIGHEST)
    for ref, own, row in ((near_ref, weights, near_row), (far_ref, once, index)):
        if ref is not None:
            ref[:dimension] = coords
            ref[dimension : dimension + sides] = own.astype(BF16)
            ref[dimension + sides : dimension + 2 * sides] = summed.astype(BF16)
            ref[dimension + 2 * sides :] = jnp.broadcast_to(
                row.astype(F32), (PAD, count)
            ).astype(BF16)
    sum_ref[...] = summed


def start_kernel(bits, *refs):
    inputs, outs = refs[:7], refs[7 : 10 + bits]
    held, sems = refs[10 + bits : -1], refs[-1]
    copies = [
        pltpu.make_async_copy(source, target, sems.at[number])
        for number, (source, target) in enumerate(zip(inputs, held))
    ]
    for copy in copies:
        copy.start()
    order, skeletons, mask, charges, points, interp, transfer = held
    ordered_ref, coords_ref, messages = outs[0], outs[1], outs[2:]
    rows = points.shape[1]
    for copy in copies[:4]:
        copy.wait()
    width = rows // 4
    for column in range(0, rows, width):
        table = one_hot(order[:, column : column + width], rows, 0)
        ordered_ref[:, column : column + width] = dot(charges[...], table).astype(BF16)
    copies[4].wait()
    coords = dot(points[...], one_hot(skeletons[0], rows, 0)).astype(BF16)
    coords_ref[...] = coords
    copies[5].wait()
    weights = dot(ordered_ref[...], interp[...], NT)
    copies[6].wait()
    write_messages(
        weights,
        coords,
        [transfer[level] for level in range(bits)],
        skeletons[1],
        jnp.broadcast_to(mask[:, 1:2], (1, coords.shape[1])),
        messages[0],
        messages[1] if bits == 2 else None,
        messages[-1],
    )


def pack_kernel(points, ordered, tall_ref, wide_ref):
    dimension, rows = points.shape
    sides = ordered.shape[0]
    wide_ref[:dimension] = points[...]
    wide_ref[dimension:] = ordered[...]
    tall_ref[:rows] = jnp.transpose(points[...])
    for number in range(rows // dimension):
        tall_ref[rows + number * sides : rows + (number + 1) * sides] = ordered[
            :, number * dimension : (number + 1) * dimension
        ]


def round_kernel(level, bits, later, skeletons, transfer, coords, total, *refs):
    position = lax.axis_index("leaf")
    dimension, count = coords.shape
    sides = total.shape[0]
    low = (position >> level) & 1
    if bits == 2:
        first, second, third = (ref[...] for ref in refs[:3])
        coords_up_ref, sibling_coords_ref, sibling_weights_ref = refs[3:6]
        outs = refs[6:]
        high = (position >> (level + 1)) & 1
        middle = pick(coords[...], first[:dimension], skeletons[level + 1], low)
        row = dimension + 2 * sides
        index = second[row : row + 1].astype(F32).astype(jnp.int32)
        sibling = pick(second[:dimension], third[:dimension], index, low)
        coords_up_ref[...] = middle
        sibling_coords_ref[...] = sibling
        span = slice(dimension, dimension + sides)
        sibling_weights_ref[...] = second[span].astype(F32) + third[span].astype(F32)
        top = pick(middle, sibling, skeletons[level + 2], high)
        span = slice(dimension + sides, dimension + 2 * sides)
        weights = (
            (total[...] + first[span].astype(F32))
            + (second[span].astype(F32) + third[span].astype(F32))
        )
    else:
        first = refs[0][...]
        outs = refs[1:]
        top = pick(coords[...], first[:dimension], skeletons[level + 1], low)
        weights = total[...] + first[dimension + sides : dimension + 2 * sides].astype(F32)
    level += bits
    if later == 0:
        outs[0][:dimension] = top
        outs[0][dimension:] = weights.astype(BF16)
        return
    outs[0][...] = top
    write_messages(
        weights,
        top,
        [transfer[level + step] for step in range(later)],
        skeletons[level + 1],
        skeletons[level + 1],
        outs[1],
        outs[2] if later == 2 else None,
        outs[-1],
    )


def sibling_kernel(bits, sides, coords, first, *refs):
    dimension = coords.shape[0]
    weights = first[dimension : dimension + sides].astype(F32)
    refs[-bits][...] = dot(weights, small_kernel(first[:dimension], coords[...]), NN, HIGHEST)
    if bits == 2:
        coords_up, sibling_coords, sibling_weights = refs[:3]
        refs[-1][...] = dot(
            sibling_weights[...], small_kernel(sibling_coords[...], coords_up[...]), NN, HIGHEST
        )


def tall_norms(tall):
    high, low = halves(jnp.square(tall.astype(F32)))
    ones = jnp.ones((tall.shape[1], 128), BF16)
    return dot(high, ones) + dot(low, ones)


def tall_charges(tall, rows, start):
    dimension = tall.shape[1]
    sides = (tall.shape[0] - rows) * dimension // rows
    first = rows + start // dimension * sides
    return tall[first : first + sides]


def bands(tall, wide):
    dimension = tall.shape[1]
    rows = wide.shape[1]
    scale = 2.0 * LOG2E / dimension
    target_norms = row_norms(wide[:dimension]) * scale
    for row in range(0, rows, dimension):
        band = slice(row, row + dimension)
        source = tall[band]
        inner = dot(source, wide[:dimension])
        squares = jnp.tile(tall_norms(source) * scale, (1, rows // 128)) + target_norms
        yield band, jnp.exp2((2.0 * scale) * inner - squares).astype(BF16)


def self_kernel(tall, wide, near_ref):
    dimension = tall.shape[1]
    for band, tile in bands(tall, wide):
        near_ref[:, band] = dot(wide[dimension:], tile, NT)


def near_kernel(mask, own_tall, own_wide, tall, wide, message, near, near_ref, back_ref, side_ref, held):
    dimension = own_tall.shape[1]
    rows = near.shape[1]
    sides = near.shape[0]
    odd = lax.rem(lax.axis_index("leaf"), 2)
    near_ref[...] = near[...]
    held[...] = jnp.zeros_like(held)

    @pl.when(mask[0, 0] > 0)
    def _():
        total = near[...]
        for band, tile in bands(tall, own_wide):
            total = total + dot(tall_charges(tall, rows, band.start), tile)
            held[:, band] = dot(own_wide[dimension:], tile, NT)
        near_ref[...] = total

    def pair(source, sum_ref):
        total = None
        for band, tile in bands(source, wide):
            sum_ref[:, band] += dot(wide[dimension:], tile, NT)
            part = dot(tall_charges(source, rows, band.start), tile)
            total = part if total is None else total + part
        side_ref[...] = total.astype(BF16)

    first = dimension + 2 * sides
    across = jnp.max(message[first : first + PAD].astype(F32)) > 0.5
    with_next = mask[0, REACH + 1] > 0
    go_odd = jnp.logical_and(odd == 1, across)
    go_even = jnp.logical_and(odd == 0, with_next)

    @pl.when(go_odd)
    def _():
        pair(tall, held)

    @pl.when(go_even)
    def _():
        pair(own_tall, near_ref)

    @pl.when(jnp.logical_not(jnp.logical_or(go_odd, go_even)))
    def _():
        side_ref[...] = jnp.zeros_like(side_ref)

    back_ref[...] = held[...].astype(BF16)


def far_kernel(levels, others, own_top, transfer, interp, *refs):
    tops, terms, out_ref = refs[:others], refs[others:-1], refs[-1]
    sides = out_ref.shape[0]
    dimension = own_top.shape[0] - sides
    potential = None
    for top in tops:
        part = dot(
            top[dimension:].astype(F32),
            small_kernel(top[:dimension], own_top[:dimension]),
            NN,
            HIGHEST,
        )
        potential = part if potential is None else potential + part
    for level in range(levels, 0, -1):
        term = terms[level - 1][...]
        if potential is not None:
            term = term + dot(potential, transfer[level - 1].astype(F32), NN, HIGHEST)
        potential = term
    high, low = halves(potential)
    out_ref[...] = dot(high, interp[...]) + dot(low, interp[...])


def sum_kernel(near, far, back, side, out_ref):
    out_ref[...] = (near[...] + far[...]) + (back[...].astype(F32) + side[...].astype(F32))


def call(kernel, outs, args, scalars=0, scratch=(), anywhere=False, flops=0, exps=0, name=None):
    vmem = pl.BlockSpec(memory_space=pltpu.VMEM)
    smem = pl.BlockSpec(memory_space=pltpu.SMEM)
    rest = pl.BlockSpec(memory_space=pl.ANY) if anywhere else vmem
    specs = [smem] * scalars + [rest] * (len(args) - scalars)
    moved = 0 if anywhere else sum(a.size * a.dtype.itemsize for a in list(args) + list(outs))
    return pl.pallas_call(
        kernel,
        out_shape=outs,
        in_specs=specs,
        out_specs=[vmem] * len(outs),
        scratch_shapes=list(scratch),
        compiler_params=pltpu.CompilerParams(
            vmem_limit_bytes=START_VMEM if anywhere else VMEM_LIMIT
        ),
        cost_estimate=pl.CostEstimate(flops=flops, bytes_accessed=moved, transcendentals=exps),
        name=name,
    )(*args)


def swapped(value, axis, flip):
    count = lax.axis_size(axis)
    return lax.ppermute(value, axis, [(place, place ^ flip) for place in range(count)])


def rotated(value, axis, turn):
    count = lax.axis_size(axis)
    return lax.ppermute(value, axis, [(place, (place + turn) % count) for place in range(count)])


def shape(dims, dtype):
    return jax.ShapeDtypeStruct(dims, dtype)


def local(points, charges, order, near_mask, skeletons, leaf_interp, transfer):
    dimension, rows = points.shape
    sides, count = charges.shape[0], leaf_interp.shape[0]
    leaves, groups = lax.axis_size("leaf"), lax.axis_size("grp")
    levels = leaves.bit_length() - 1
    rounds = []
    level = 0
    while level < levels:
        rounds.append((level, min(2, levels - level)))
        level += rounds[-1][1]
    message = shape((dimension + 2 * sides + PAD, count), BF16)

    def message_shapes(bits):
        return [message] * bits + [shape((sides, count), F32)]

    bits = rounds[0][1]
    skeletons = jnp.transpose(skeletons, (1, 0, 2))
    transfer = transfer[0]
    inputs = [order.reshape(1, rows), skeletons, near_mask, charges, points, leaf_interp, transfer]
    ordered, coords, *messages, total = call(
        functools.partial(start_kernel, bits),
        [shape((sides, rows), BF16), shape((dimension, count), BF16)] + message_shapes(bits),
        inputs,
        scratch=[pltpu.VMEM(value.shape, value.dtype) for value in inputs]
        + [pltpu.SemaphoreType.DMA((len(inputs),))],
        anywhere=True,
        name="start",
    )

    def exchange(level, bits):
        received = [swapped(messages[0], "leaf", 1 << level)]
        if bits == 2:
            received.append(swapped(messages[1], "leaf", 2 << level))
            received.append(swapped(messages[1], "leaf", 3 << level))
        return received

    received = exchange(0, bits)

    own_tall, own_wide = call(
        pack_kernel,
        [
            shape((rows + sides * rows // dimension, dimension), BF16),
            shape((dimension + sides, rows), BF16),
        ],
        [points, ordered],
        flops=dimension * rows,
        name="pack",
    )
    (near,) = call(
        self_kernel,
        [shape((sides, rows), F32)],
        [own_tall, own_wide],
        flops=2 * rows * rows * (dimension + sides),
        exps=rows * rows,
        name="self_tile",
    )
    own_tall, own_wide, near, received = lax.optimization_barrier(
        (own_tall, own_wide, near, received)
    )
    first_message = received[0]
    tall = rotated(own_tall, "leaf", 2)
    wide = swapped(own_wide, "leaf", 1)
    near, back, side = call(
        near_kernel,
        [shape((sides, rows), F32), shape((sides, rows), BF16), shape((sides, rows), BF16)],
        [near_mask, own_tall, own_wide, tall, wide, first_message, near],
        scalars=1,
        scratch=[pltpu.VMEM((sides, rows), F32)],
        flops=4 * rows * rows * (dimension + 2 * sides),
        exps=2 * rows * rows,
        name="near_tiles",
    )
    back = rotated(back, "leaf", -2)
    side = swapped(side, "leaf", 1)

    terms = []
    for number, (level, bits) in enumerate(rounds):
        later = rounds[number + 1][1] if number + 1 < len(rounds) else 0
        if number:
            received = exchange(level, bits)
        outs = []
        if bits == 2:
            outs += [shape((dimension, count), BF16)] * 2 + [shape((sides, count), F32)]
        if later == 0:
            outs += [shape((dimension + sides, count), BF16)]
        else:
            outs += [shape((dimension, count), BF16)] + message_shapes(later)
        results = list(
            call(
                functools.partial(round_kernel, level, bits, later),
                outs,
                [skeletons, transfer, coords, total] + received,
                flops=8 * dimension * count * count,
                name="join_round",
            )
        )
        kept = results[:3] if bits == 2 else []
        terms += list(
            call(
                functools.partial(sibling_kernel, bits, sides),
                [shape((sides, count), F32)] * bits,
                [coords, received[0]] + kept,
                flops=8 * dimension * count * count,
                exps=2 * count * count,
                name="sibling_terms",
            )
        )
        results = results[len(kept) :]
        if later:
            coords, messages, total = results[0], results[1:-1], results[-1]
    own_top = results[0]
    tops = [rotated(own_top, "grp", turn) for turn in range(1, groups)]
    (far,) = call(
        functools.partial(far_kernel, levels, len(tops)),
        [shape((sides, rows), F32)],
        [own_top, transfer, leaf_interp] + tops + terms,
        flops=4 * sides * rows * count,
        name="far_field",
    )
    (out,) = call(
        sum_kernel,
        [shape((sides, rows), F32)],
        [near, far, back, side],
        flops=3 * sides * rows,
        name="total",
    )
    return out


def solution(mesh):
    in_specs = (
        P(None, ("leaf", "grp")),
        P(None, ("leaf", "grp")),
        P(("leaf", "grp")),
        P(("leaf", "grp"), None),
        P(("leaf", "grp"), None, None),
        P(None, ("leaf", "grp")),
        P(("leaf", "grp"), None, None, None),
    )
    out_specs = P(None, ("leaf", "grp"))
    return jax.shard_map(local, mesh=mesh, in_specs=in_specs, out_specs=out_specs, check_vma=False)
```

```python
import functools

import jax
import jax.numpy as jnp
from jax import lax
from jax.experimental import pallas as pl
from jax.experimental.pallas import tpu as pltpu
from jax.sharding import PartitionSpec as P

REACH = 2
BF16 = jnp.bfloat16
F32 = jnp.float32
LOG2E = 1.4426950408889634
HIGHEST = lax.Precision.HIGHEST
PAD = 16
VMEM_LIMIT = 40 * 1024 * 1024
START_VMEM = 56 * 1024 * 1024

NN = ((1,), (0,))
NT = ((1,), (1,))
TN = ((0,), (0,))


def dot(left, right, contract=NN, precision=None):
    return lax.dot_general(
        left, right, (contract, ((), ())), preferred_element_type=F32, precision=precision
    )


def halves(value):
    high = value.astype(BF16)
    return high, (value - high.astype(F32)).astype(BF16)


def row_norms(points):
    wide = points.astype(F32)
    return jnp.sum(wide * wide, axis=0, keepdims=True)


def column_norms(points):
    wide = points.astype(F32)
    high, low = halves(wide * wide)
    ones = jnp.ones((points.shape[0], 128), BF16)
    return dot(high, ones, TN) + dot(low, ones, TN)


def one_hot(index, rows, first):
    place = lax.broadcasted_iota(jnp.int32, (rows, index.shape[1]), 0) + first
    return jnp.where(place == index, 1.0, 0.0).astype(BF16)


def small_kernel(source, target):
    scale = 2.0 * LOG2E / source.shape[0]
    inner = dot(source, target, TN)
    squares = column_norms(source)[:, : target.shape[1]] + row_norms(target)
    return jnp.exp2(scale * (2.0 * inner - squares))


def pick(first, second, index, bit):
    count = first.shape[1]
    table = jnp.concatenate(
        [one_hot(index, count, count * bit), one_hot(index, count, count * (1 - bit))], axis=0
    )
    return dot(jnp.concatenate([first, second], axis=1), table).astype(BF16)


def write_messages(weights, coords, transfers, index, near_row, near_ref, far_ref, sum_ref):
    dimension, (sides, count) = coords.shape[0], weights.shape
    first = transfers[0].astype(F32)
    once = dot(weights, first, NT, HIGHEST)
    summed = once
    if len(transfers) == 2:
        summed = dot(once, transfers[1].astype(F32), NT, HIGHEST)
    for ref, own, row in ((near_ref, weights, near_row), (far_ref, once, index)):
        if ref is not None:
            ref[:dimension] = coords
            ref[dimension : dimension + sides] = own.astype(BF16)
            ref[dimension + sides : dimension + 2 * sides] = summed.astype(BF16)
            ref[dimension + 2 * sides :] = jnp.broadcast_to(
                row.astype(F32), (PAD, count)
            ).astype(BF16)
    sum_ref[...] = summed


def start_kernel(bits, *refs):
    inputs, outs = refs[:7], refs[7 : 10 + bits]
    held, sems = refs[10 + bits : -1], refs[-1]
    copies = [
        pltpu.make_async_copy(source, target, sems.at[number])
        for number, (source, target) in enumerate(zip(inputs, held))
    ]
    for copy in copies:
        copy.start()
    order, skeletons, mask, charges, points, interp, transfer = held
    ordered_ref, coords_ref, messages = outs[0], outs[1], outs[2:]
    rows = points.shape[1]
    for copy in copies[:4]:
        copy.wait()
    width = rows // 4
    for column in range(0, rows, width):
        table = one_hot(order[:, column : column + width], rows, 0)
        ordered_ref[:, column : column + width] = dot(charges[...], table).astype(BF16)
    copies[4].wait()
    coords = dot(points[...], one_hot(skeletons[0], rows, 0)).astype(BF16)
    coords_ref[...] = coords
    copies[5].wait()
    weights = dot(ordered_ref[...], interp[...], NT)
    copies[6].wait()
    write_messages(
        weights,
        coords,
        [transfer[level] for level in range(bits)],
        skeletons[1],
        jnp.broadcast_to(mask[:, 1:2], (1, coords.shape[1])),
        messages[0],
        messages[1] if bits == 2 else None,
        messages[-1],
    )


def round_kernel(level, bits, later, skeletons, transfer, coords, total, *refs):
    position = lax.axis_index("leaf")
    dimension, count = coords.shape
    sides = total.shape[0]
    low = (position >> level) & 1
    if bits == 2:
        first, second, third = (ref[...] for ref in refs[:3])
        coords_up_ref, sibling_coords_ref, sibling_weights_ref = refs[3:6]
        outs = refs[6:]
        high = (position >> (level + 1)) & 1
        middle = pick(coords[...], first[:dimension], skeletons[level + 1], low)
        row = dimension + 2 * sides
        index = second[row : row + 1].astype(F32).astype(jnp.int32)
        sibling = pick(second[:dimension], third[:dimension], index, low)
        coords_up_ref[...] = middle
        sibling_coords_ref[...] = sibling
        span = slice(dimension, dimension + sides)
        sibling_weights_ref[...] = second[span].astype(F32) + third[span].astype(F32)
        top = pick(middle, sibling, skeletons[level + 2], high)
        span = slice(dimension + sides, dimension + 2 * sides)
        weights = (
            (total[...] + first[span].astype(F32))
            + (second[span].astype(F32) + third[span].astype(F32))
        )
    else:
        first = refs[0][...]
        outs = refs[1:]
        top = pick(coords[...], first[:dimension], skeletons[level + 1], low)
        weights = total[...] + first[dimension + sides : dimension + 2 * sides].astype(F32)
    level += bits
    if later == 0:
        outs[0][:dimension] = top
        outs[0][dimension:] = weights.astype(BF16)
        return
    outs[0][...] = top
    write_messages(
        weights,
        top,
        [transfer[level + step] for step in range(later)],
        skeletons[level + 1],
        skeletons[level + 1],
        outs[1],
        outs[2] if later == 2 else None,
        outs[-1],
    )


def pair_terms(bits, sides, coords, first, refs):
    dimension = coords.shape[0]
    weights = first[dimension : dimension + sides].astype(F32)
    terms = [dot(weights, small_kernel(first[:dimension], coords[...]), NN, HIGHEST)]
    if bits == 2:
        coords_up, sibling_coords, sibling_weights = refs[:3]
        terms.append(
            dot(sibling_weights[...], small_kernel(sibling_coords[...], coords_up[...]), NN, HIGHEST)
        )
    return terms


def sibling_kernel(bits, sides, coords, first, *refs):
    for ref, term in zip(refs[-bits:], pair_terms(bits, sides, coords, first, refs)):
        ref[...] = term


def last_sibling_kernel(bits, sides, coords, first, transfer, *refs):
    earlier, (potential_ref, product_ref) = refs[3 * (bits - 1) : -2], refs[-2:]
    terms = [ref[...] for ref in earlier] + pair_terms(bits, sides, coords, first, refs)
    potential = terms[-1]
    product = transfer[len(terms) - 1].astype(F32)
    for level in range(len(terms) - 2, -1, -1):
        matrix = transfer[level].astype(F32)
        potential = dot(potential, matrix, NN, HIGHEST) + terms[level]
        product = dot(product, matrix, NN, HIGHEST)
    potential_ref[...] = potential
    product_ref[...] = product


def turn_kernel(points, tall_ref, norms_ref):
    dimension, rows = points.shape
    tall_ref[...] = jnp.transpose(points[...])
    square = jnp.square(tall_ref[...].astype(F32))
    norms = jnp.sum(square, axis=1, keepdims=True) * (2.0 * LOG2E / dimension)
    norms_ref[...] = jnp.broadcast_to(norms, (rows, 128))


def fill_tile(tall, norms, wide, tile_ref):
    rows, dimension = tall.shape
    scale = 2.0 * LOG2E / dimension
    height = min(256, rows)
    target_norms = row_norms(wide[...]) * scale
    for row in range(0, rows, height):
        band = slice(row, row + height)
        inner = dot(tall[band], wide[...])
        squares = jnp.tile(norms[band], (1, rows // 128)) + target_norms
        tile_ref[band] = jnp.exp2((2.0 * scale) * inner - squares).astype(BF16)


def self_kernel(tall, norms, wide, ordered, near_ref, tile_ref):
    fill_tile(tall, norms, wide, tile_ref)
    near_ref[...] = dot(ordered[...], tile_ref[...], NT)


def near_kernel(mask, tall, norms, wide, ordered, side_tall, side_norms, side_ordered,
                back_wide, back_ordered, message, near, near_ref, back_ref, side_ref, held, tile_ref):
    dimension, sides = wide.shape[0], ordered.shape[0]
    odd = lax.rem(lax.axis_index("leaf"), 2)
    near_ref[...] = near[...]
    held[...] = jnp.zeros_like(held)

    @pl.when(mask[0, 0] > 0)
    def _():
        fill_tile(tall, norms, back_wide, tile_ref)
        near_ref[...] += dot(back_ordered[...], tile_ref[...], NT)
        held[...] = dot(ordered[...], tile_ref[...])

    def pair(other_wide, other_ordered, sum_ref):
        fill_tile(side_tall, side_norms, other_wide, tile_ref)
        sum_ref[...] += dot(side_ordered[...], tile_ref[...])
        side_ref[...] = dot(other_ordered[...], tile_ref[...], NT).astype(BF16)

    first = dimension + 2 * sides
    across = jnp.max(message[first : first + PAD].astype(F32)) > 0.5
    with_next = mask[0, REACH + 1] > 0
    go_odd = jnp.logical_and(odd == 1, across)
    go_even = jnp.logical_and(odd == 0, with_next)

    @pl.when(go_odd)
    def _():
        pair(back_wide, back_ordered, held)

    @pl.when(go_even)
    def _():
        pair(wide, ordered, near_ref)

    @pl.when(jnp.logical_not(jnp.logical_or(go_odd, go_even)))
    def _():
        side_ref[...] = jnp.zeros_like(side_ref)

    back_ref[...] = held[...].astype(BF16)


def final_kernel(others, own_top, potential, product, interp, near, back, side, *refs):
    tops, out_ref = refs[:others], refs[-1]
    sides = out_ref.shape[0]
    dimension = own_top.shape[0] - sides
    total = potential[...]
    above = None
    for top in tops:
        part = dot(
            top[dimension:].astype(F32),
            small_kernel(top[:dimension], own_top[:dimension]),
            NN,
            HIGHEST,
        )
        above = part if above is None else above + part
    if above is not None:
        total = total + dot(above, product[...], NN, HIGHEST)
    high, low = halves(total)
    local_part = near[...] + (back[...].astype(F32) + side[...].astype(F32))
    out_ref[...] = local_part + (dot(high, interp[...]) + dot(low, interp[...]))


def call(kernel, outs, args, scalars=0, scratch=(), anywhere=False, flops=0, exps=0, name=None):
    vmem = pl.BlockSpec(memory_space=pltpu.VMEM)
    smem = pl.BlockSpec(memory_space=pltpu.SMEM)
    rest = pl.BlockSpec(memory_space=pl.ANY) if anywhere else vmem
    specs = [smem] * scalars + [rest] * (len(args) - scalars)
    moved = 0 if anywhere else sum(a.size * a.dtype.itemsize for a in list(args) + list(outs))
    return pl.pallas_call(
        kernel,
        out_shape=outs,
        in_specs=specs,
        out_specs=[vmem] * len(outs),
        scratch_shapes=list(scratch),
        compiler_params=pltpu.CompilerParams(
            vmem_limit_bytes=START_VMEM if anywhere else VMEM_LIMIT
        ),
        cost_estimate=pl.CostEstimate(flops=flops, bytes_accessed=moved, transcendentals=exps),
        name=name,
    )(*args)


def swapped(value, axis, flip):
    count = lax.axis_size(axis)
    return lax.ppermute(value, axis, [(place, place ^ flip) for place in range(count)])


def rotated(value, axis, turn):
    count = lax.axis_size(axis)
    return lax.ppermute(value, axis, [(place, (place + turn) % count) for place in range(count)])


def shape(dims, dtype):
    return jax.ShapeDtypeStruct(dims, dtype)


def local(points, charges, order, near_mask, skeletons, leaf_interp, transfer):
    dimension, rows = points.shape
    sides, count = charges.shape[0], leaf_interp.shape[0]
    leaves, groups = lax.axis_size("leaf"), lax.axis_size("grp")
    levels = leaves.bit_length() - 1
    rounds = []
    level = 0
    while level < levels:
        rounds.append((level, min(2, levels - level)))
        level += rounds[-1][1]
    message = shape((dimension + 2 * sides + PAD, count), BF16)

    def message_shapes(bits):
        return [message] * bits + [shape((sides, count), F32)]

    back_points = rotated(points, "leaf", 2)
    side_points = swapped(points, "leaf", 1)

    bits = rounds[0][1]
    skeletons = jnp.transpose(skeletons, (1, 0, 2))
    transfer = transfer[0]
    inputs = [order.reshape(1, rows), skeletons, near_mask, charges, points, leaf_interp, transfer]
    ordered, coords, *messages, total = call(
        functools.partial(start_kernel, bits),
        [shape((sides, rows), BF16), shape((dimension, count), BF16)] + message_shapes(bits),
        inputs,
        scratch=[pltpu.VMEM(value.shape, value.dtype) for value in inputs]
        + [pltpu.SemaphoreType.DMA((len(inputs),))],
        anywhere=True,
        name="start",
    )

    def exchange(level, bits):
        received = [swapped(messages[0], "leaf", 1 << level)]
        if bits == 2:
            received.append(swapped(messages[1], "leaf", 2 << level))
            received.append(swapped(messages[1], "leaf", 3 << level))
        return received

    received = exchange(0, bits)

    def turned(value):
        return call(
            turn_kernel,
            [shape((rows, dimension), BF16), shape((rows, 128), F32)],
            [value],
            flops=dimension * rows,
            name="turn",
        )

    tile = pltpu.VMEM((rows, rows), BF16)
    tall, norms = turned(points)
    (near,) = call(
        self_kernel,
        [shape((sides, rows), F32)],
        [tall, norms, points, ordered],
        scratch=[tile],
        flops=2 * rows * rows * (dimension + sides),
        exps=rows * rows,
        name="self_tile",
    )
    ordered, near, received = lax.optimization_barrier((ordered, near, received))
    back_ordered = rotated(ordered, "leaf", 2)
    side_ordered = swapped(ordered, "leaf", 1)
    side_tall, side_norms = turned(side_points)
    near, back, side = call(
        near_kernel,
        [shape((sides, rows), F32), shape((sides, rows), BF16), shape((sides, rows), BF16)],
        [near_mask, tall, norms, points, ordered, side_tall, side_norms, side_ordered]
        + [back_points, back_ordered, received[0], near],
        scalars=1,
        scratch=[pltpu.VMEM((sides, rows), F32), tile],
        flops=4 * rows * rows * (dimension + 2 * sides),
        exps=2 * rows * rows,
        name="near_tiles",
    )
    back = rotated(back, "leaf", -2)
    side = swapped(side, "leaf", 1)

    terms = []
    for number, (level, bits) in enumerate(rounds):
        later = rounds[number + 1][1] if number + 1 < len(rounds) else 0
        if number:
            received = exchange(level, bits)
            if len(terms):
                total, terms = lax.optimization_barrier((total, terms))
        outs = []
        if bits == 2:
            outs += [shape((dimension, count), BF16)] * 2 + [shape((sides, count), F32)]
        if later == 0:
            outs += [shape((dimension + sides, count), BF16)]
        else:
            outs += [shape((dimension, count), BF16)] + message_shapes(later)
        results = list(
            call(
                functools.partial(round_kernel, level, bits, later),
                outs,
                [skeletons, transfer, coords, total] + received,
                flops=8 * dimension * count * count,
                name="join_round",
            )
        )
        kept = results[:3] if bits == 2 else []
        if later:
            terms += list(
                call(
                    functools.partial(sibling_kernel, bits, sides),
                    [shape((sides, count), F32)] * bits,
                    [coords, received[0]] + kept,
                    flops=8 * dimension * count * count,
                    exps=2 * count * count,
                    name="sibling_terms",
                )
            )
        else:
            potential, product = call(
                functools.partial(last_sibling_kernel, bits, sides),
                [shape((sides, count), F32), shape((count, count), F32)],
                [coords, received[0], transfer] + kept + terms,
                flops=8 * dimension * count * count,
                exps=2 * count * count,
                name="sibling_sum",
            )
        results = results[len(kept) :]
        if later:
            coords, messages, total = results[0], results[1:-1], results[-1]
    own_top = results[0]
    tops = [rotated(own_top, "grp", turn) for turn in range(1, groups)]
    (out,) = call(
        functools.partial(final_kernel, len(tops)),
        [shape((sides, rows), F32)],
        [own_top, potential, product, leaf_interp, near, back, side] + tops,
        flops=4 * sides * rows * count,
        name="total",
    )
    return out


def solution(mesh):
    in_specs = (
        P(None, ("leaf", "grp")),
        P(None, ("leaf", "grp")),
        P(("leaf", "grp")),
        P(("leaf", "grp"), None),
        P(("leaf", "grp"), None, None),
        P(None, ("leaf", "grp")),
        P(("leaf", "grp"), None, None, None),
    )
    out_specs = P(None, ("leaf", "grp"))
    return jax.shard_map(local, mesh=mesh, in_specs=in_specs, out_specs=out_specs, check_vma=False)
```

```python
import functools

import jax
import jax.numpy as jnp
from jax import lax
from jax.experimental import pallas as pl
from jax.experimental.pallas import tpu as pltpu
from jax.sharding import PartitionSpec as P

REACH = 2
BF16 = jnp.bfloat16
F32 = jnp.float32
LOG2E = 1.4426950408889634
HIGHEST = lax.Precision.HIGHEST
PAD = 16
VMEM_LIMIT = 40 * 1024 * 1024
START_VMEM = 56 * 1024 * 1024

NN = ((1,), (0,))
NT = ((1,), (1,))
TN = ((0,), (0,))


def dot(left, right, contract=NN, precision=None):
    return lax.dot_general(
        left, right, (contract, ((), ())), preferred_element_type=F32, precision=precision
    )


def halves(value):
    high = value.astype(BF16)
    return high, (value - high.astype(F32)).astype(BF16)


def dot_split(left, right, contract=NN):
    rows = left.shape[0]
    both = dot(jnp.concatenate(halves(left), axis=0), right, contract)
    return both[:rows] + both[rows:]


def row_norms(points):
    wide = points.astype(F32)
    return jnp.sum(wide * wide, axis=0, keepdims=True)


def column_norms(points):
    wide = points.astype(F32)
    high, low = halves(wide * wide)
    ones = jnp.ones((points.shape[0], 128), BF16)
    return dot(high, ones, TN) + dot(low, ones, TN)


def one_hot(index, rows, first):
    place = lax.broadcasted_iota(jnp.int32, (rows, index.shape[1]), 0) + first
    return jnp.where(place == index, 1.0, 0.0).astype(BF16)


def small_kernel(source, target):
    scale = 2.0 * LOG2E / source.shape[0]
    inner = dot(source, target, TN)
    squares = column_norms(source)[:, : target.shape[1]] + row_norms(target)
    return jnp.exp2(scale * (2.0 * inner - squares))


def pick(first, second, index, bit):
    count = first.shape[1]
    table = jnp.concatenate(
        [one_hot(index, count, count * bit), one_hot(index, count, count * (1 - bit))], axis=0
    )
    return dot(jnp.concatenate([first, second], axis=1), table).astype(BF16)


def write_messages(weights, coords, transfers, index, near_row, near_ref, far_ref, sum_ref):
    dimension, (sides, count) = coords.shape[0], weights.shape
    once = dot_split(weights, transfers[0], NT)
    summed = once
    if len(transfers) == 2:
        summed = dot_split(once, transfers[1], NT)
    for ref, own, row in ((near_ref, weights, near_row), (far_ref, once, index)):
        if ref is not None:
            ref[:dimension] = coords
            ref[dimension : dimension + sides] = own.astype(BF16)
            ref[dimension + sides : dimension + 2 * sides] = summed.astype(BF16)
            ref[dimension + 2 * sides :] = jnp.broadcast_to(
                row.astype(F32), (PAD, count)
            ).astype(BF16)
    sum_ref[...] = summed


def start_kernel(bits, early, *refs):
    inputs, refs = refs[:7], refs[7:]
    outs, refs = refs[: 4 + bits], refs[4 + bits :]
    held, made, sems, out_sems = refs[:7], refs[7:-2], refs[-2], refs[-1]
    copies = [
        pltpu.make_async_copy(source, target, sems.at[number])
        for number, (source, target) in enumerate(zip(inputs, held))
    ]
    for copy in copies:
        copy.start()
    stores = [
        pltpu.make_async_copy(source, target, out_sems.at[number])
        for number, (source, target) in enumerate(zip(made, outs))
    ]
    order, skeletons, mask, charges, points, interp, transfer = held
    rest_ref, ordered_ref, coords_ref, messages = made[0], made[1], made[2], made[3:]
    dimension, rows = points.shape
    sides, count = charges.shape[0], coords_ref.shape[1]
    for copy in copies[:4]:
        copy.wait()
    width = rows // 4
    for column in range(0, rows, width):
        table = one_hot(order[:, column : column + width], rows, 0)
        part = dot(charges[...], table).astype(BF16)
        ordered_ref[:, column : column + width] = part
        rest_ref[dimension - early :, column : column + width] = part
    copies[4].wait()
    rest_ref[: dimension - early] = points[early:]
    stores[0].start()
    stores[1].start()
    coords = dot(points[...], one_hot(skeletons[0], rows, 0)).astype(BF16)
    coords_ref[...] = coords
    stores[2].start()
    copies[5].wait()
    weights = dot(ordered_ref[...], interp[...], NT)
    copies[6].wait()
    lane = lax.broadcasted_iota(jnp.int32, (1, count), 1)
    pattern = jnp.zeros((1, count), jnp.int32)
    for offset in range(mask.shape[1]):
        pattern = jnp.where(lane == offset, mask[:, offset : offset + 1], pattern)
    write_messages(
        weights,
        coords,
        [transfer[level] for level in range(bits)],
        skeletons[1],
        pattern,
        messages[0],
        messages[1] if bits == 2 else None,
        messages[-1],
    )
    for store in stores[3:]:
        store.start()
    for store in stores:
        store.wait()


def marked(message, dimension, sides, offset):
    first = dimension + 2 * sides
    rows = message[first : first + PAD].astype(F32)
    lane = lax.broadcasted_iota(jnp.int32, rows.shape, 1)
    return jnp.max(jnp.where(lane == REACH + offset, rows, 0.0)) > 0.5


def round_kernel(level, bits, later, skeletons, transfer, coords, total, *refs):
    position = lax.axis_index("leaf")
    dimension, count = coords.shape
    sides = total.shape[0]
    low = (position >> level) & 1
    if bits == 2:
        first, second, third = (ref[...] for ref in refs[:3])
        coords_up_ref, sibling_coords_ref, sibling_weights_ref = refs[3:6]
        outs = refs[6:]
        high = (position >> (level + 1)) & 1
        middle = pick(coords[...], first[:dimension], skeletons[level + 1], low)
        row = dimension + 2 * sides
        index = second[row : row + 1].astype(F32).astype(jnp.int32)
        sibling = pick(second[:dimension], third[:dimension], index, low)
        coords_up_ref[...] = middle
        sibling_coords_ref[...] = sibling
        span = slice(dimension, dimension + sides)
        sibling_weights_ref[...] = second[span].astype(F32) + third[span].astype(F32)
        top = pick(middle, sibling, skeletons[level + 2], high)
        span = slice(dimension + sides, dimension + 2 * sides)
        weights = (
            (total[...] + first[span].astype(F32))
            + (second[span].astype(F32) + third[span].astype(F32))
        )
    else:
        first = refs[0][...]
        outs = refs[1:]
        top = pick(coords[...], first[:dimension], skeletons[level + 1], low)
        weights = total[...] + first[dimension + sides : dimension + 2 * sides].astype(F32)
    level += bits
    if later == 0:
        outs[0][:dimension] = top
        outs[0][dimension:] = weights.astype(BF16)
        return
    outs[0][...] = top
    write_messages(
        weights,
        top,
        [transfer[level + step] for step in range(later)],
        skeletons[level + 1],
        skeletons[level + 1],
        outs[1],
        outs[2] if later == 2 else None,
        outs[-1],
    )


def pair_terms(bits, sides, coords, first, refs):
    dimension = coords.shape[0]
    weights = first[dimension : dimension + sides].astype(F32)
    terms = [dot(weights, small_kernel(first[:dimension], coords[...]), NN, HIGHEST)]
    if bits == 2:
        coords_up, sibling_coords, sibling_weights = refs[:3]
        terms.append(
            dot(sibling_weights[...], small_kernel(sibling_coords[...], coords_up[...]), NN, HIGHEST)
        )
    return terms


def sibling_kernel(bits, sides, coords, first, *refs):
    for ref, term in zip(refs[-bits:], pair_terms(bits, sides, coords, first, refs)):
        ref[...] = term


def last_sibling_kernel(bits, sides, coords, first, transfer, *refs):
    earlier, (potential_ref, product_ref) = refs[3 * (bits - 1) : -2], refs[-2:]
    terms = [ref[...] for ref in earlier] + pair_terms(bits, sides, coords, first, refs)
    potential = terms[-1]
    product = transfer[len(terms) - 1].astype(F32)
    for level in range(len(terms) - 2, -1, -1):
        matrix = transfer[level].astype(F32)
        potential = dot(potential, matrix, NN, HIGHEST) + terms[level]
        product = dot(product, matrix, NN, HIGHEST)
    potential_ref[...] = potential
    product_ref[...] = product


def turn_kernel(points, tall_ref, norms_ref):
    dimension, rows = points.shape
    tall_ref[...] = jnp.transpose(points[...])
    square = jnp.square(tall_ref[...].astype(F32))
    norms = jnp.sum(square, axis=1, keepdims=True) * (2.0 * LOG2E / dimension)
    norms_ref[...] = jnp.broadcast_to(norms, (rows, 128))


def bands(tall, norms, wide):
    rows, dimension = tall.shape
    scale = 2.0 * LOG2E / dimension
    height = min(256, rows)
    target_norms = row_norms(wide[...]) * scale
    for row in range(0, rows, height):
        band = slice(row, row + height)
        inner = dot(tall[band], wide[...])
        squares = jnp.tile(norms[band], (1, rows // 128)) + target_norms
        yield band, jnp.exp2((2.0 * scale) * inner - squares).astype(BF16)


def self_kernel(tall, norms, wide, ordered, near_ref):
    for band, tile in bands(tall, norms, wide):
        near_ref[:, band] = dot(ordered[...], tile, NT)


def near_kernel(tall, norms, wide, ordered, side_tall, side_norms, side_ordered, back_early,
                back_rest, own_message, message, near, near_ref, back_ref, side_ref, back_wide, held):
    dimension, sides = wide.shape[0], ordered.shape[0]
    early = back_early.shape[0]
    back_wide[:early] = back_early[...]
    back_wide[early:] = back_rest[: dimension - early]
    back_ordered = back_rest[dimension - early :]
    odd = lax.rem(lax.axis_index("leaf"), 2)
    with_back = marked(own_message, dimension, sides, -2)
    go_odd = jnp.logical_and(odd == 1, marked(message, dimension, sides, -1))
    go_even = jnp.logical_and(odd == 0, marked(own_message, dimension, sides, 1))
    near_ref[...] = near[...]

    @pl.when(with_back)
    def _():
        for band, tile in bands(tall, norms, back_wide):
            near_ref[:, band] += dot(back_ordered, tile, NT)
            part = dot(ordered[:, band], tile)
            if band.start:
                held[...] += part
            else:
                held[...] = part

    @pl.when(jnp.logical_not(with_back))
    def _():
        held[...] = jnp.zeros_like(held)

    def pair(other_wide, other_ordered, sum_ref):
        for band, tile in bands(side_tall, side_norms, other_wide):
            side_ref[:, band] = dot(other_ordered, tile, NT).astype(BF16)
            sum_ref[...] += dot(side_ordered[:, band], tile)

    @pl.when(go_odd)
    def _():
        pair(back_wide, back_ordered, held)

    @pl.when(go_even)
    def _():
        pair(wide, ordered[...], near_ref)

    @pl.when(jnp.logical_not(jnp.logical_or(go_odd, go_even)))
    def _():
        side_ref[...] = jnp.zeros_like(side_ref)

    back_ref[...] = held[...].astype(BF16)


def far_kernel(others, own_top, potential, product, interp, near, *refs):
    tops, out_ref = refs[:others], refs[-1]
    sides = out_ref.shape[0]
    dimension = own_top.shape[0] - sides
    total = potential[...]
    above = None
    for top in tops:
        part = dot(
            top[dimension:].astype(F32),
            small_kernel(top[:dimension], own_top[:dimension]),
            NN,
            HIGHEST,
        )
        above = part if above is None else above + part
    if above is not None:
        total = total + dot(above, product[...], NN, HIGHEST)
    out_ref[...] = near[...] + dot_split(total, interp[...])


def total_kernel(here, back, side, out_ref):
    out_ref[...] = here[...] + (back[...].astype(F32) + side[...].astype(F32))


def call(kernel, outs, args, scratch=(), anywhere=False, flops=0, exps=0, name=None):
    vmem = pl.BlockSpec(memory_space=pltpu.VMEM)
    rest = pl.BlockSpec(memory_space=pl.ANY) if anywhere else vmem
    moved = 0 if anywhere else sum(a.size * a.dtype.itemsize for a in list(args) + list(outs))
    return pl.pallas_call(
        kernel,
        out_shape=outs,
        in_specs=[rest] * len(args),
        out_specs=[rest if anywhere else vmem] * len(outs),
        scratch_shapes=list(scratch),
        compiler_params=pltpu.CompilerParams(
            vmem_limit_bytes=START_VMEM if anywhere else VMEM_LIMIT
        ),
        cost_estimate=pl.CostEstimate(flops=flops, bytes_accessed=moved, transcendentals=exps),
        name=name,
    )(*args)


def swapped(value, axis, flip):
    count = lax.axis_size(axis)
    return lax.ppermute(value, axis, [(place, place ^ flip) for place in range(count)])


def rotated(value, axis, turn):
    count = lax.axis_size(axis)
    return lax.ppermute(value, axis, [(place, (place + turn) % count) for place in range(count)])


def shape(dims, dtype):
    return jax.ShapeDtypeStruct(dims, dtype)


def local(points, charges, order, near_mask, skeletons, leaf_interp, transfer):
    dimension, rows = points.shape
    sides, count = charges.shape[0], leaf_interp.shape[0]
    leaves, groups = lax.axis_size("leaf"), lax.axis_size("grp")
    levels = leaves.bit_length() - 1
    rounds = []
    level = 0
    while level < levels:
        rounds.append((level, min(2, levels - level)))
        level += rounds[-1][1]
    message = shape((dimension + 2 * sides + PAD, count), BF16)

    def message_shapes(bits):
        return [message] * bits + [shape((sides, count), F32)]

    early = dimension * 3 // 4
    back_early = rotated(points[:early], "leaf", 2)
    side_points = swapped(points, "leaf", 1)

    bits = rounds[0][1]
    skeletons = jnp.transpose(skeletons, (1, 0, 2))
    transfer = transfer[0]
    inputs = [order.reshape(1, rows), skeletons, near_mask, charges, points, leaf_interp, transfer]
    made = [
        shape((dimension - early + sides, rows), BF16),
        shape((sides, rows), BF16),
        shape((dimension, count), BF16),
    ] + message_shapes(bits)
    rest, ordered, coords, *messages, total = call(
        functools.partial(start_kernel, bits, early),
        made,
        inputs,
        scratch=[pltpu.VMEM(value.shape, value.dtype) for value in inputs + made]
        + [pltpu.SemaphoreType.DMA((len(inputs),)), pltpu.SemaphoreType.DMA((len(made),))],
        anywhere=True,
        name="start",
    )
    first_message = messages[0]

    def exchange(level, bits):
        received = [swapped(messages[0], "leaf", 1 << level)]
        if bits == 2:
            received.append(swapped(messages[1], "leaf", 2 << level))
            received.append(swapped(messages[1], "leaf", 3 << level))
        return received

    received = exchange(0, bits)

    def turned(value):
        return call(
            turn_kernel,
            [shape((rows, dimension), BF16), shape((rows, 128), F32)],
            [value],
            flops=dimension * rows,
            name="turn",
        )

    tall, norms = turned(points)
    (near,) = call(
        self_kernel,
        [shape((sides, rows), F32)],
        [tall, norms, points, ordered],
        flops=2 * rows * rows * (dimension + sides),
        exps=rows * rows,
        name="self_tile",
    )
    ordered, rest, near, received = lax.optimization_barrier((ordered, rest, near, received))
    back_rest = rotated(rest, "leaf", 2)
    side_ordered = swapped(ordered, "leaf", 1)
    side_tall, side_norms = turned(side_points)
    near, back, side = call(
        near_kernel,
        [shape((sides, rows), F32), shape((sides, rows), BF16), shape((sides, rows), BF16)],
        [tall, norms, points, ordered, side_tall, side_norms, side_ordered]
        + [back_early, back_rest, first_message, received[0], near],
        scratch=[pltpu.VMEM((dimension, rows), BF16), pltpu.VMEM((sides, rows), F32)],
        flops=4 * rows * rows * (dimension + 2 * sides),
        exps=2 * rows * rows,
        name="near_tiles",
    )
    back = rotated(back, "leaf", -2)
    side = swapped(side, "leaf", 1)

    terms = []
    for number, (level, bits) in enumerate(rounds):
        later = rounds[number + 1][1] if number + 1 < len(rounds) else 0
        if number:
            received = exchange(level, bits)
            if len(terms):
                total, terms = lax.optimization_barrier((total, terms))
        outs = []
        if bits == 2:
            outs += [shape((dimension, count), BF16)] * 2 + [shape((sides, count), F32)]
        if later == 0:
            outs += [shape((dimension + sides, count), BF16)]
        else:
            outs += [shape((dimension, count), BF16)] + message_shapes(later)
        results = list(
            call(
                functools.partial(round_kernel, level, bits, later),
                outs,
                [skeletons, transfer, coords, total] + received,
                flops=8 * dimension * count * count,
                name="join_round",
            )
        )
        kept = results[:3] if bits == 2 else []
        if later:
            terms += list(
                call(
                    functools.partial(sibling_kernel, bits, sides),
                    [shape((sides, count), F32)] * bits,
                    [coords, received[0]] + kept,
                    flops=8 * dimension * count * count,
                    exps=2 * count * count,
                    name="sibling_terms",
                )
            )
        else:
            potential, product = call(
                functools.partial(last_sibling_kernel, bits, sides),
                [shape((sides, count), F32), shape((count, count), F32)],
                [coords, received[0], transfer] + kept + terms,
                flops=8 * dimension * count * count,
                exps=2 * count * count,
                name="sibling_sum",
            )
        results = results[len(kept) :]
        if later:
            coords, messages, total = results[0], results[1:-1], results[-1]
    own_top = results[0]
    tops = [rotated(own_top, "grp", turn) for turn in range(1, groups)]
    (here,) = call(
        functools.partial(far_kernel, len(tops)),
        [shape((sides, rows), F32)],
        [own_top, potential, product, leaf_interp, near] + tops,
        flops=4 * sides * rows * count,
        name="far_field",
    )
    (out,) = call(
        total_kernel, [shape((sides, rows), F32)], [here, back, side], flops=2 * sides * rows, name="total"
    )
    return out


def solution(mesh):
    in_specs = (
        P(None, ("leaf", "grp")),
        P(None, ("leaf", "grp")),
        P(("leaf", "grp")),
        P(("leaf", "grp"), None),
        P(("leaf", "grp"), None, None),
        P(None, ("leaf", "grp")),
        P(("leaf", "grp"), None, None, None),
    )
    out_specs = P(None, ("leaf", "grp"))
    return jax.shard_map(local, mesh=mesh, in_specs=in_specs, out_specs=out_specs, check_vma=False)
```

```python
import functools

import jax
import jax.numpy as jnp
from jax import lax
from jax.experimental import pallas as pl
from jax.experimental.pallas import tpu as pltpu
from jax.sharding import PartitionSpec as P

REACH = 2
BF16 = jnp.bfloat16
F32 = jnp.float32
LOG2E = 1.4426950408889634
HIGHEST = lax.Precision.HIGHEST
PAD = 16
VMEM_LIMIT = 40 * 1024 * 1024
START_VMEM = 56 * 1024 * 1024

NN = ((1,), (0,))
NT = ((1,), (1,))
TN = ((0,), (0,))


def dot(left, right, contract=NN, precision=None):
    return lax.dot_general(
        left, right, (contract, ((), ())), preferred_element_type=F32, precision=precision
    )


def halves(value):
    high = value.astype(BF16)
    return high, (value - high.astype(F32)).astype(BF16)


def dot_split(left, right, contract=NN):
    rows = left.shape[0]
    both = dot(jnp.concatenate(halves(left), axis=0), right, contract)
    return both[:rows] + both[rows:]


def row_norms(points):
    wide = points.astype(F32)
    return jnp.sum(wide * wide, axis=0, keepdims=True)


def column_norms(points):
    wide = points.astype(F32)
    high, low = halves(wide * wide)
    ones = jnp.ones((points.shape[0], 128), BF16)
    return dot(high, ones, TN) + dot(low, ones, TN)


def one_hot(index, rows, first):
    place = lax.broadcasted_iota(jnp.int32, (rows, index.shape[1]), 0) + first
    return jnp.where(place == index, 1.0, 0.0).astype(BF16)


def small_kernel(source, target):
    scale = 2.0 * LOG2E / source.shape[0]
    inner = dot(source, target, TN)
    squares = column_norms(source)[:, : target.shape[1]] + row_norms(target)
    return jnp.exp2(scale * (2.0 * inner - squares))


def pick(first, second, index, bit):
    count = first.shape[1]
    table = jnp.concatenate(
        [one_hot(index, count, count * bit), one_hot(index, count, count * (1 - bit))], axis=0
    )
    return dot(jnp.concatenate([first, second], axis=1), table).astype(BF16)


def write_message(weights, coords, matrix, message_ref, passed_ref):
    dimension, sides = coords.shape[0], weights.shape[0]
    passed = dot_split(weights, matrix, NT)
    message_ref[:dimension] = coords
    message_ref[dimension : dimension + sides] = weights.astype(BF16)
    message_ref[dimension + sides : dimension + 2 * sides] = passed.astype(BF16)
    passed_ref[...] = passed


def start_kernel(*refs):
    inputs, outs, held = refs[:7], refs[7:12], refs[12:19]
    made, sems, out_sems = refs[19:24], refs[24], refs[25]
    copies = [
        pltpu.make_async_copy(source, target, sems.at[number])
        for number, (source, target) in enumerate(zip(inputs, held))
    ]
    for copy in copies:
        copy.start()
    stores = [
        pltpu.make_async_copy(source, target, out_sems.at[number])
        for number, (source, target) in enumerate(zip(made, outs))
    ]
    order, skeletons, mask, charges, points, interp, transfer = held
    ordered_ref, coords_ref, marks_ref, message_ref, passed_ref = made
    dimension, rows = points.shape
    sides, count = passed_ref.shape
    for copy in copies[:4]:
        copy.wait()
    width = rows // 4
    for column in range(0, rows, width):
        table = one_hot(order[:, column : column + width], rows, 0)
        ordered_ref[:, column : column + width] = dot(charges[...], table).astype(BF16)
    stores[0].start()
    copies[4].wait()
    coords = dot(points[...], one_hot(skeletons[0], rows, 0)).astype(BF16)
    coords_ref[...] = coords
    stores[1].start()
    lane = lax.broadcasted_iota(jnp.int32, (1, count), 1)
    pattern = jnp.zeros((1, count), jnp.int32)
    for offset in range(mask.shape[1]):
        pattern = jnp.where(lane == offset, mask[:, offset : offset + 1], pattern)
    marks = jnp.broadcast_to(pattern.astype(F32), (PAD, count)).astype(BF16)
    marks_ref[...] = marks
    message_ref[dimension + 2 * sides :] = marks
    stores[2].start()
    copies[5].wait()
    weights = dot(ordered_ref[...], interp[...], NT)
    copies[6].wait()
    write_message(weights, coords, transfer[0], message_ref, passed_ref)
    stores[3].start()
    stores[4].start()
    for store in stores:
        store.wait()


def marked(marks, offset):
    rows = marks.astype(F32)
    lane = lax.broadcasted_iota(jnp.int32, rows.shape, 1)
    return jnp.max(jnp.where(lane == REACH + offset, rows, 0.0)) > 0.5


def round_kernel(level, last, skeletons, transfer, coords, passed, message, *outs):
    dimension = coords.shape[0]
    sides = passed.shape[0]
    bit = (lax.axis_index("leaf") >> level) & 1
    joined = pick(coords[...], message[:dimension], skeletons[level + 1], bit)
    span = slice(dimension + sides, dimension + 2 * sides)
    weights = passed[...] + message[span].astype(F32)
    if last:
        outs[0][:dimension] = joined
        outs[0][dimension:] = weights.astype(BF16)
        return
    outs[0][...] = joined
    write_message(weights, joined, transfer[level + 1], outs[1], outs[2])


def sibling_term(coords, message, sides):
    dimension = coords.shape[0]
    weights = message[dimension : dimension + sides].astype(F32)
    return dot(weights, small_kernel(message[:dimension], coords[...]), NN, HIGHEST)


def early_terms_kernel(levels, sides, transfer, *refs):
    outs = refs[2 * (levels - 1) :]
    for level in range(levels - 1):
        outs[level][...] = sibling_term(refs[2 * level], refs[2 * level + 1], sides)
    product = transfer[levels - 1].astype(F32)
    for level in range(levels - 2, -1, -1):
        product = dot(product, transfer[level].astype(F32), NN, HIGHEST)
    outs[-1][...] = product


def last_term_kernel(sides, transfer, coords, message, *refs):
    terms, potential_ref = refs[:-1], refs[-1]
    potential = sibling_term(coords, message, sides)
    for level in range(len(terms) - 1, -1, -1):
        potential = dot_split(potential, transfer[level]) + terms[level][...]
    potential_ref[...] = potential


def turn_kernel(points, tall_ref, norms_ref):
    dimension, rows = points.shape
    tall_ref[...] = jnp.transpose(points[...])
    square = jnp.square(tall_ref[...].astype(F32))
    norms = jnp.sum(square, axis=1, keepdims=True) * (2.0 * LOG2E / dimension)
    norms_ref[...] = jnp.broadcast_to(norms, (rows, 128))


def bands(tall, norms, wide):
    rows, dimension = tall.shape
    scale = 2.0 * LOG2E / dimension
    height = min(256, rows)
    target_norms = row_norms(wide[...]) * scale
    for row in range(0, rows, height):
        band = slice(row, row + height)
        inner = dot(tall[band], wide[...])
        squares = jnp.tile(norms[band], (1, rows // 128)) + target_norms
        yield band, jnp.exp2((2.0 * scale) * inner - squares).astype(BF16)


def self_kernel(tall, norms, wide, ordered, near_ref):
    for band, tile in bands(tall, norms, wide):
        near_ref[:, band] = dot(ordered[...], tile, NT)


def back_kernel(tall, norms, ordered, back_wide, back_ordered, marks, near, near_ref, held_ref):
    near_ref[...] = near[...]
    used = marked(marks[...], -2)

    @pl.when(used)
    def _():
        for band, tile in bands(tall, norms, back_wide):
            near_ref[:, band] += dot(back_ordered[...], tile, NT)
            part = dot(ordered[:, band], tile)
            if band.start:
                held_ref[...] += part
            else:
                held_ref[...] = part

    @pl.when(jnp.logical_not(used))
    def _():
        held_ref[...] = jnp.zeros_like(held_ref)


def pair_kernel(wide, ordered, side_tall, side_norms, side_ordered, back_wide, back_ordered,
                marks, message, near, held, near_ref, back_ref, side_ref, sum_ref):
    odd = lax.rem(lax.axis_index("leaf"), 2)
    go_odd = jnp.logical_and(odd == 1, marked(message[message.shape[0] - PAD :], -1))
    go_even = jnp.logical_and(odd == 0, marked(marks[...], 1))

    def pair(other_wide, other_ordered, base, out_ref):
        for band, tile in bands(side_tall, side_norms, other_wide):
            side_ref[:, band] = dot(other_ordered[...], tile, NT).astype(BF16)
            part = dot(side_ordered[:, band], tile)
            if band.start == 0:
                part = part + base[...]
            if band.stop < wide.shape[1]:
                sum_ref[...] = part if band.start == 0 else sum_ref[...] + part
            else:
                if band.start:
                    part = part + sum_ref[...]
                out_ref[...] = part.astype(out_ref.dtype)

    @pl.when(go_odd)
    def _():
        pair(back_wide, back_ordered, held, back_ref)
        near_ref[...] = near[...]

    @pl.when(go_even)
    def _():
        pair(wide, ordered, near, near_ref)
        back_ref[...] = held[...].astype(BF16)

    @pl.when(jnp.logical_not(jnp.logical_or(go_odd, go_even)))
    def _():
        near_ref[...] = near[...]
        back_ref[...] = held[...].astype(BF16)
        side_ref[...] = jnp.zeros_like(side_ref)


def far_kernel(others, own_top, potential, product, interp, near, *refs):
    tops, out_ref = refs[:others], refs[-1]
    sides = out_ref.shape[0]
    dimension = own_top.shape[0] - sides
    total = potential[...]
    above = None
    for top in tops:
        part = dot(
            top[dimension:].astype(F32),
            small_kernel(top[:dimension], own_top[:dimension]),
            NN,
            HIGHEST,
        )
        above = part if above is None else above + part
    if above is not None:
        total = total + dot(above, product[...], NN, HIGHEST)
    out_ref[...] = near[...] + dot_split(total, interp[...])


def total_kernel(here, back, side, out_ref):
    out_ref[...] = here[...] + (back[...].astype(F32) + side[...].astype(F32))


def call(kernel, outs, args, scratch=(), anywhere=False, flops=0, exps=0, name=None):
    vmem = pl.BlockSpec(memory_space=pltpu.VMEM)
    rest = pl.BlockSpec(memory_space=pl.ANY) if anywhere else vmem
    moved = 0 if anywhere else sum(a.size * a.dtype.itemsize for a in list(args) + list(outs))
    return pl.pallas_call(
        kernel,
        out_shape=outs,
        in_specs=[rest] * len(args),
        out_specs=[rest if anywhere else vmem] * len(outs),
        scratch_shapes=list(scratch),
        compiler_params=pltpu.CompilerParams(
            vmem_limit_bytes=START_VMEM if anywhere else VMEM_LIMIT
        ),
        cost_estimate=pl.CostEstimate(flops=flops, bytes_accessed=moved, transcendentals=exps),
        name=name,
    )(*args)


def swapped(value, axis, flip):
    count = lax.axis_size(axis)
    return lax.ppermute(value, axis, [(place, place ^ flip) for place in range(count)])


def rotated(value, axis, turn):
    count = lax.axis_size(axis)
    return lax.ppermute(value, axis, [(place, (place + turn) % count) for place in range(count)])


def shape(dims, dtype):
    return jax.ShapeDtypeStruct(dims, dtype)


def local(points, charges, order, near_mask, skeletons, leaf_interp, transfer):
    dimension, rows = points.shape
    sides, count = charges.shape[0], leaf_interp.shape[0]
    leaves, groups = lax.axis_size("leaf"), lax.axis_size("grp")
    levels = leaves.bit_length() - 1
    skeletons = jnp.transpose(skeletons, (1, 0, 2))
    transfer = transfer[0]
    block_sums = shape((sides, rows), F32)
    block_values = shape((sides, rows), BF16)
    node_points = shape((dimension, count), BF16)
    node_sums = shape((sides, count), F32)
    tile_flops = 2 * rows * rows * (dimension + 2 * sides)

    back_points = rotated(points, "leaf", 2)

    inputs = [order.reshape(1, rows), skeletons, near_mask, charges, points, leaf_interp, transfer]
    made = [
        block_values,
        node_points,
        shape((PAD, count), BF16),
        shape((dimension + 2 * sides + PAD, count), BF16),
        node_sums,
    ]
    ordered, coords, marks, message, passed = call(
        start_kernel,
        made,
        inputs,
        scratch=[pltpu.VMEM(value.shape, value.dtype) for value in inputs + made]
        + [pltpu.SemaphoreType.DMA((len(inputs),)), pltpu.SemaphoreType.DMA((len(made),))],
        anywhere=True,
        name="start",
    )
    def turned(value):
        return call(
            turn_kernel,
            [shape((rows, dimension), BF16), shape((rows, 128), F32)],
            [value],
            flops=dimension * rows,
            name="turn",
        )

    tall, norms = turned(lax.optimization_barrier((points, passed))[0])
    (near,) = call(
        self_kernel,
        [block_sums],
        [tall, norms, points, ordered],
        flops=tile_flops,
        exps=rows * rows,
        name="self_tile",
    )

    history = []
    for level in range(levels):
        received = swapped(message, "leaf", 1 << level)
        if level == 0:
            received, near, early_points = lax.optimization_barrier((received, near, points))
            first_received = received
            side_points = swapped(early_points, "leaf", 1)
        history += [coords, received]
        if level == min(2, levels - 1):
            near, held = call(
                back_kernel,
                [block_sums, block_sums],
                [tall, norms, ordered, back_points, back_ordered, marks]
                + [lax.optimization_barrier((near, passed))[0]],
                flops=tile_flops,
                exps=rows * rows,
                name="back_tile",
            )
            passed, held = lax.optimization_barrier((passed, held))
        last = level == levels - 1
        if last:
            side_tall, side_norms = turned(side_points)
            near, back, side = call(
                pair_kernel,
                [block_sums, block_values, block_values],
                [points, ordered, side_tall, side_norms, side_ordered, back_points, back_ordered]
                + [marks, first_received, lax.optimization_barrier((near, passed))[0], held],
                scratch=[pltpu.VMEM((sides, rows), F32)],
                flops=tile_flops,
                exps=rows * rows,
                name="pair_tile",
            )
            passed, near = lax.optimization_barrier((passed, near))
            back = rotated(back, "leaf", -2)
            side = swapped(side, "leaf", 1)
            *terms, product = call(
                functools.partial(early_terms_kernel, levels, sides),
                [node_sums] * (levels - 1) + [shape((count, count), F32)],
                [transfer] + history[:-2],
                flops=8 * levels * dimension * count * count,
                exps=levels * count * count,
                name="early_terms",
            )
            passed, terms, product = lax.optimization_barrier((passed, terms, product))
        if last:
            outs = [shape((dimension + sides, count), BF16)]
        else:
            outs = [node_points, shape((dimension + 2 * sides, count), BF16), node_sums]
        results = call(
            functools.partial(round_kernel, level, last),
            outs,
            [skeletons, transfer, coords, passed, received],
            flops=8 * dimension * count * count,
            name="join_level",
        )
        if not last:
            coords, message, passed = results
        if level == 0:
            sent = lax.optimization_barrier((ordered, results[-1]))[0]
            back_ordered = rotated(sent, "leaf", 2)
            side_ordered = swapped(sent, "leaf", 1)
    own_top = results[0]
    tops = [rotated(own_top, "grp", turn) for turn in range(1, groups)]
    (potential,) = call(
        functools.partial(last_term_kernel, sides),
        [node_sums],
        [transfer] + history[-2:] + list(terms),
        flops=8 * dimension * count * count,
        exps=count * count,
        name="last_term",
    )
    (here,) = call(
        functools.partial(far_kernel, len(tops)),
        [block_sums],
        [own_top, potential, product, leaf_interp, near] + tops,
        flops=4 * sides * rows * count,
        name="far_field",
    )
    (out,) = call(total_kernel, [block_sums], [here, back, side], flops=2 * sides * rows, name="total")
    return out


def solution(mesh):
    in_specs = (
        P(None, ("leaf", "grp")),
        P(None, ("leaf", "grp")),
        P(("leaf", "grp")),
        P(("leaf", "grp"), None),
        P(("leaf", "grp"), None, None),
        P(None, ("leaf", "grp")),
        P(("leaf", "grp"), None, None, None),
    )
    out_specs = P(None, ("leaf", "grp"))
    return jax.shard_map(local, mesh=mesh, in_specs=in_specs, out_specs=out_specs, check_vma=False)
```

```python
import functools

import jax
import jax.numpy as jnp
from jax import lax
from jax.experimental import pallas as pl
from jax.experimental.pallas import tpu as pltpu
from jax.sharding import PartitionSpec as P

REACH = 2
BF16 = jnp.bfloat16
F32 = jnp.float32
LOG2E = 1.4426950408889634
HIGHEST = lax.Precision.HIGHEST
PAD = 16
VMEM_LIMIT = 40 * 1024 * 1024
START_VMEM = 56 * 1024 * 1024

NN = ((1,), (0,))
NT = ((1,), (1,))
TN = ((0,), (0,))


def dot(left, right, contract=NN, precision=None):
    return lax.dot_general(
        left, right, (contract, ((), ())), preferred_element_type=F32, precision=precision
    )


def halves(value):
    high = value.astype(BF16)
    return high, (value - high.astype(F32)).astype(BF16)


def dot_split(left, right, contract=NN):
    rows = left.shape[0]
    both = dot(jnp.concatenate(halves(left), axis=0), right, contract)
    return both[:rows] + both[rows:]


def row_norms(points):
    wide = points.astype(F32)
    return jnp.sum(wide * wide, axis=0, keepdims=True)


def column_norms(points):
    wide = points.astype(F32)
    high, low = halves(wide * wide)
    ones = jnp.ones((points.shape[0], 128), BF16)
    return dot(high, ones, TN) + dot(low, ones, TN)


def one_hot(index, rows, first):
    place = lax.broadcasted_iota(jnp.int32, (rows, index.shape[1]), 0) + first
    return jnp.where(place == index, 1.0, 0.0).astype(BF16)


def small_kernel(source, target):
    scale = 2.0 * LOG2E / source.shape[0]
    inner = dot(source, target, TN)
    squares = column_norms(source)[:, : target.shape[1]] + row_norms(target)
    return jnp.exp2(scale * (2.0 * inner - squares))


def pick(first, second, index, bit):
    count = first.shape[1]
    table = jnp.concatenate(
        [one_hot(index, count, count * bit), one_hot(index, count, count * (1 - bit))], axis=0
    )
    return dot(jnp.concatenate([first, second], axis=1), table).astype(BF16)


def write_message(weights, coords, matrix, message_ref, passed_ref):
    dimension, sides = coords.shape[0], weights.shape[0]
    passed = dot_split(weights, matrix, NT)
    message_ref[:dimension] = coords
    message_ref[dimension : dimension + sides] = weights.astype(BF16)
    message_ref[dimension + sides : dimension + 2 * sides] = passed.astype(BF16)
    passed_ref[...] = passed


def start_kernel(*refs):
    inputs, outs, held = refs[:7], refs[7:12], refs[12:19]
    made, sems, out_sems = refs[19:24], refs[24], refs[25]
    copies = [
        pltpu.make_async_copy(source, target, sems.at[number])
        for number, (source, target) in enumerate(zip(inputs, held))
    ]
    for copy in copies:
        copy.start()
    stores = [
        pltpu.make_async_copy(source, target, out_sems.at[number])
        for number, (source, target) in enumerate(zip(made, outs))
    ]
    order, skeletons, mask, charges, points, interp, transfer = held
    ordered_ref, coords_ref, marks_ref, message_ref, passed_ref = made
    dimension, rows = points.shape
    sides, count = passed_ref.shape
    for copy in copies[:4]:
        copy.wait()
    width = rows // 4
    for column in range(0, rows, width):
        table = one_hot(order[:, column : column + width], rows, 0)
        ordered_ref[:, column : column + width] = dot(charges[...], table).astype(BF16)
    stores[0].start()
    copies[4].wait()
    coords = dot(points[...], one_hot(skeletons[0], rows, 0)).astype(BF16)
    coords_ref[...] = coords
    stores[1].start()
    lane = lax.broadcasted_iota(jnp.int32, (1, count), 1)
    pattern = jnp.zeros((1, count), jnp.int32)
    for offset in range(mask.shape[1]):
        pattern = jnp.where(lane == offset, mask[:, offset : offset + 1], pattern)
    marks = jnp.broadcast_to(pattern.astype(F32), (PAD, count)).astype(BF16)
    marks_ref[...] = marks
    message_ref[dimension + 2 * sides :] = marks
    stores[2].start()
    copies[5].wait()
    weights = dot(ordered_ref[...], interp[...], NT)
    copies[6].wait()
    write_message(weights, coords, transfer[0], message_ref, passed_ref)
    stores[3].start()
    stores[4].start()
    for store in stores:
        store.wait()


def marked(marks, offset):
    rows = marks.astype(F32)
    lane = lax.broadcasted_iota(jnp.int32, rows.shape, 1)
    return jnp.max(jnp.where(lane == REACH + offset, rows, 0.0)) > 0.5


def round_kernel(level, last, skeletons, transfer, coords, passed, message, *outs):
    dimension = coords.shape[0]
    sides = passed.shape[0]
    bit = (lax.axis_index("leaf") >> level) & 1
    joined = pick(coords[...], message[:dimension], skeletons[level + 1], bit)
    span = slice(dimension + sides, dimension + 2 * sides)
    weights = passed[...] + message[span].astype(F32)
    if last:
        outs[0][:dimension] = joined
        outs[0][dimension:] = weights.astype(BF16)
        return
    outs[0][...] = joined
    write_message(weights, joined, transfer[level + 1], outs[1], outs[2])


def sibling_term(coords, message, sides):
    dimension = coords.shape[0]
    weights = message[dimension : dimension + sides].astype(F32)
    return dot(weights, small_kernel(message[:dimension], coords[...]), NN, HIGHEST)


def early_terms_kernel(levels, sides, transfer, *refs):
    outs = refs[2 * (levels - 1) :]
    for level in range(levels - 1):
        outs[level][...] = sibling_term(refs[2 * level], refs[2 * level + 1], sides)
    product = transfer[levels - 1].astype(F32)
    for level in range(levels - 2, -1, -1):
        product = dot(product, transfer[level].astype(F32), NN, HIGHEST)
    outs[-1][...] = product


def last_term_kernel(sides, transfer, coords, message, *refs):
    terms, potential_ref = refs[:-1], refs[-1]
    potential = sibling_term(coords, message, sides)
    for level in range(len(terms) - 1, -1, -1):
        potential = dot_split(potential, transfer[level]) + terms[level][...]
    potential_ref[...] = potential


def turn_kernel(points, tall_ref, norms_ref):
    dimension, rows = points.shape
    tall_ref[...] = jnp.transpose(points[...])
    square = jnp.square(tall_ref[...].astype(F32))
    norms = jnp.sum(square, axis=1, keepdims=True) * (2.0 * LOG2E / dimension)
    norms_ref[...] = jnp.broadcast_to(norms, (rows, 128))


def bands(tall, norms, wide):
    rows, dimension = tall.shape
    scale = 2.0 * LOG2E / dimension
    height = min(256, rows)
    target_norms = row_norms(wide[...]) * scale
    for row in range(0, rows, height):
        band = slice(row, row + height)
        inner = dot(tall[band], wide[...])
        squares = jnp.tile(norms[band], (1, rows // 128)) + target_norms
        yield band, jnp.exp2((2.0 * scale) * inner - squares).astype(BF16)


def self_kernel(tall, norms, wide, ordered, near_ref):
    for band, tile in bands(tall, norms, wide):
        near_ref[:, band] = dot(ordered[...], tile, NT)


def back_kernel(tall, norms, ordered, back_wide, back_ordered, marks, near, near_ref, held_ref):
    near_ref[...] = near[...]
    used = marked(marks[...], -2)

    @pl.when(used)
    def _():
        for band, tile in bands(tall, norms, back_wide):
            near_ref[:, band] += dot(back_ordered[...], tile, NT)
            part = dot(ordered[:, band], tile)
            if band.start:
                held_ref[...] += part
            else:
                held_ref[...] = part

    @pl.when(jnp.logical_not(used))
    def _():
        held_ref[...] = jnp.zeros_like(held_ref)


def pair_kernel(wide, ordered, side_tall, side_norms, side_ordered, back_wide, back_ordered,
                marks, message, near, held, near_ref, back_ref, side_ref, sum_ref):
    odd = lax.rem(lax.axis_index("leaf"), 2)
    go_odd = jnp.logical_and(odd == 1, marked(message[message.shape[0] - PAD :], -1))
    go_even = jnp.logical_and(odd == 0, marked(marks[...], 1))

    def pair(other_wide, other_ordered, base, out_ref):
        for band, tile in bands(side_tall, side_norms, other_wide):
            side_ref[:, band] = dot(other_ordered[...], tile, NT).astype(BF16)
            part = dot(side_ordered[:, band], tile)
            if band.start == 0:
                part = part + base[...]
            if band.stop < wide.shape[1]:
                sum_ref[...] = part if band.start == 0 else sum_ref[...] + part
            else:
                if band.start:
                    part = part + sum_ref[...]
                out_ref[...] = part.astype(out_ref.dtype)

    @pl.when(go_odd)
    def _():
        pair(back_wide, back_ordered, held, back_ref)
        near_ref[...] = near[...]

    @pl.when(go_even)
    def _():
        pair(wide, ordered, near, near_ref)
        back_ref[...] = held[...].astype(BF16)

    @pl.when(jnp.logical_not(jnp.logical_or(go_odd, go_even)))
    def _():
        near_ref[...] = near[...]
        back_ref[...] = held[...].astype(BF16)
        side_ref[...] = jnp.zeros_like(side_ref)


def far_kernel(others, own_top, potential, product, interp, near, *refs):
    tops, out_ref = refs[:others], refs[-1]
    sides = out_ref.shape[0]
    dimension = own_top.shape[0] - sides
    total = potential[...]
    above = None
    for top in tops:
        part = dot(
            top[dimension:].astype(F32),
            small_kernel(top[:dimension], own_top[:dimension]),
            NN,
            HIGHEST,
        )
        above = part if above is None else above + part
    if above is not None:
        total = total + dot(above, product[...], NN, HIGHEST)
    out_ref[...] = near[...] + dot_split(total, interp[...])


def total_kernel(here, back, side, out_ref):
    out_ref[...] = here[...] + (back[...].astype(F32) + side[...].astype(F32))


def call(kernel, outs, args, scratch=(), anywhere=False, flops=0, exps=0, name=None):
    vmem = pl.BlockSpec(memory_space=pltpu.VMEM)
    rest = pl.BlockSpec(memory_space=pl.ANY) if anywhere else vmem
    moved = 0 if anywhere else sum(a.size * a.dtype.itemsize for a in list(args) + list(outs))
    return pl.pallas_call(
        kernel,
        out_shape=outs,
        in_specs=[rest] * len(args),
        out_specs=[rest if anywhere else vmem] * len(outs),
        scratch_shapes=list(scratch),
        compiler_params=pltpu.CompilerParams(
            vmem_limit_bytes=START_VMEM if anywhere else VMEM_LIMIT
        ),
        cost_estimate=pl.CostEstimate(flops=flops, bytes_accessed=moved, transcendentals=exps),
        name=name,
    )(*args)


def swapped(value, axis, flip):
    count = lax.axis_size(axis)
    return lax.ppermute(value, axis, [(place, place ^ flip) for place in range(count)])


def rotated(value, axis, turn):
    count = lax.axis_size(axis)
    return lax.ppermute(value, axis, [(place, (place + turn) % count) for place in range(count)])


def shape(dims, dtype):
    return jax.ShapeDtypeStruct(dims, dtype)


def local(points, charges, order, near_mask, skeletons, leaf_interp, transfer):
    dimension, rows = points.shape
    sides, count = charges.shape[0], leaf_interp.shape[0]
    leaves, groups = lax.axis_size("leaf"), lax.axis_size("grp")
    levels = leaves.bit_length() - 1
    skeletons = jnp.transpose(skeletons, (1, 0, 2))
    transfer = transfer[0]
    block_sums = shape((sides, rows), F32)
    block_values = shape((sides, rows), BF16)
    node_points = shape((dimension, count), BF16)
    node_sums = shape((sides, count), F32)
    tile_flops = 2 * rows * rows * (dimension + 2 * sides)

    back_points = rotated(points, "leaf", 2)

    inputs = [order.reshape(1, rows), skeletons, near_mask, charges, points, leaf_interp, transfer]
    made = [
        block_values,
        node_points,
        shape((PAD, count), BF16),
        shape((dimension + 2 * sides + PAD, count), BF16),
        node_sums,
    ]
    ordered, coords, marks, message, passed = call(
        start_kernel,
        made,
        inputs,
        scratch=[pltpu.VMEM(value.shape, value.dtype) for value in inputs + made]
        + [pltpu.SemaphoreType.DMA((len(inputs),)), pltpu.SemaphoreType.DMA((len(made),))],
        anywhere=True,
        name="start",
    )
    def turned(value):
        return call(
            turn_kernel,
            [shape((rows, dimension), BF16), shape((rows, 128), F32)],
            [value],
            flops=dimension * rows,
            name="turn",
        )

    tall, norms = turned(lax.optimization_barrier((points, passed))[0])
    (near,) = call(
        self_kernel,
        [block_sums],
        [tall, norms, points, ordered],
        flops=tile_flops,
        exps=rows * rows,
        name="self_tile",
    )

    history = []
    for level in range(levels):
        received = swapped(message, "leaf", 1 << level)
        if level == 0:
            received, near, early_points = lax.optimization_barrier((received, near, points))
            first_received = received
            side_points = swapped(early_points, "leaf", 1)
        if level == 1:
            received, back_points = lax.optimization_barrier((received, back_points))
        history += [coords, received]
        if level == levels - 1:
            near, held = call(
                back_kernel,
                [block_sums, block_sums],
                [tall, norms, ordered, back_points, back_ordered, marks]
                + [lax.optimization_barrier((near, passed))[0]],
                flops=tile_flops,
                exps=rows * rows,
                name="back_tile",
            )
            passed, held = lax.optimization_barrier((passed, held))
        last = level == levels - 1
        if last:
            side_tall, side_norms = turned(side_points)
            near, back, side = call(
                pair_kernel,
                [block_sums, block_values, block_values],
                [points, ordered, side_tall, side_norms, side_ordered, back_points, back_ordered]
                + [marks, first_received, lax.optimization_barrier((near, passed))[0], held],
                scratch=[pltpu.VMEM((sides, rows), F32)],
                flops=tile_flops,
                exps=rows * rows,
                name="pair_tile",
            )
            passed, near = lax.optimization_barrier((passed, near))
            back = rotated(back, "leaf", -2)
            side = swapped(side, "leaf", 1)
            *terms, product = call(
                functools.partial(early_terms_kernel, levels, sides),
                [node_sums] * (levels - 1) + [shape((count, count), F32)],
                [transfer] + history[:-2],
                flops=8 * levels * dimension * count * count,
                exps=levels * count * count,
                name="early_terms",
            )
            passed, terms, product = lax.optimization_barrier((passed, terms, product))
        if last:
            outs = [shape((dimension + sides, count), BF16)]
        else:
            outs = [node_points, shape((dimension + 2 * sides, count), BF16), node_sums]
        results = call(
            functools.partial(round_kernel, level, last),
            outs,
            [skeletons, transfer, coords, passed, received],
            flops=8 * dimension * count * count,
            name="join_level",
        )
        if not last:
            coords, message, passed = results
        if level == min(1, levels - 1):
            sent = lax.optimization_barrier((ordered, results[-1]))[0]
            back_ordered = rotated(sent, "leaf", 2)
            side_ordered = swapped(sent, "leaf", 1)
    own_top = results[0]
    tops = [rotated(own_top, "grp", turn) for turn in range(1, groups)]
    (potential,) = call(
        functools.partial(last_term_kernel, sides),
        [node_sums],
        [transfer] + history[-2:] + list(terms),
        flops=8 * dimension * count * count,
        exps=count * count,
        name="last_term",
    )
    (here,) = call(
        functools.partial(far_kernel, len(tops)),
        [block_sums],
        [own_top, potential, product, leaf_interp, near] + tops,
        flops=4 * sides * rows * count,
        name="far_field",
    )
    (out,) = call(total_kernel, [block_sums], [here, back, side], flops=2 * sides * rows, name="total")
    return out


def solution(mesh):
    in_specs = (
        P(None, ("leaf", "grp")),
        P(None, ("leaf", "grp")),
        P(("leaf", "grp")),
        P(("leaf", "grp"), None),
        P(("leaf", "grp"), None, None),
        P(None, ("leaf", "grp")),
        P(("leaf", "grp"), None, None, None),
    )
    out_specs = P(None, ("leaf", "grp"))
    return jax.shard_map(local, mesh=mesh, in_specs=in_specs, out_specs=out_specs, check_vma=False)
```

```python
import functools

import jax
import jax.numpy as jnp
from jax import lax
from jax.experimental import pallas as pl
from jax.experimental.pallas import tpu as pltpu
from jax.sharding import PartitionSpec as P

REACH = 2
BF16 = jnp.bfloat16
F32 = jnp.float32
LOG2E = 1.4426950408889634
HIGHEST = lax.Precision.HIGHEST
PAD = 16
JOIN_FLOPS = 500
VMEM_LIMIT = 40 * 1024 * 1024
START_VMEM = 56 * 1024 * 1024

NN = ((1,), (0,))
NT = ((1,), (1,))
TN = ((0,), (0,))


def dot(left, right, contract=NN, precision=None):
    return lax.dot_general(
        left, right, (contract, ((), ())), preferred_element_type=F32, precision=precision
    )


def halves(value):
    high = value.astype(BF16)
    return high, (value - high.astype(F32)).astype(BF16)


def dot_split(left, right, contract=NN):
    rows = left.shape[0]
    both = dot(jnp.concatenate(halves(left), axis=0), right, contract)
    return both[:rows] + both[rows:]


def row_norms(points):
    wide = points.astype(F32)
    return jnp.sum(wide * wide, axis=0, keepdims=True)


def column_norms(points):
    wide = points.astype(F32)
    high, low = halves(wide * wide)
    ones = jnp.ones((points.shape[0], 128), BF16)
    return dot(high, ones, TN) + dot(low, ones, TN)


def one_hot(index, rows, first):
    place = lax.broadcasted_iota(jnp.int32, (rows, index.shape[1]), 0) + first
    return jnp.where(place == index, 1.0, 0.0).astype(BF16)


def small_kernel(source, target):
    scale = 2.0 * LOG2E / source.shape[0]
    inner = dot(source, target, TN)
    squares = column_norms(source)[:, : target.shape[1]] + row_norms(target)
    return jnp.exp2(scale * (2.0 * inner - squares))


def pick(first, second, index, bit):
    count = first.shape[1]
    table = jnp.concatenate(
        [one_hot(index, count, count * bit), one_hot(index, count, count * (1 - bit))], axis=0
    )
    return dot(jnp.concatenate([first, second], axis=1), table).astype(BF16)


def write_message(weights, coords, matrix, message_ref, passed_ref):
    dimension, sides = coords.shape[0], weights.shape[0]
    passed = dot_split(weights, matrix, NT)
    message_ref[:dimension] = coords
    message_ref[dimension : dimension + sides] = weights.astype(BF16)
    message_ref[dimension + sides : dimension + 2 * sides] = passed.astype(BF16)
    passed_ref[...] = passed


def start_kernel(*refs):
    inputs, outs, held = refs[:7], refs[7:12], refs[12:19]
    made, sems, out_sems = refs[19:24], refs[24], refs[25]
    copies = [
        pltpu.make_async_copy(source, target, sems.at[number])
        for number, (source, target) in enumerate(zip(inputs, held))
    ]
    for copy in copies:
        copy.start()
    stores = [
        pltpu.make_async_copy(source, target, out_sems.at[number])
        for number, (source, target) in enumerate(zip(made, outs))
    ]
    order, skeletons, mask, charges, points, interp, transfer = held
    ordered_ref, coords_ref, marks_ref, message_ref, passed_ref = made
    dimension, rows = points.shape
    sides, count = passed_ref.shape
    for copy in copies[:4]:
        copy.wait()
    width = rows // 4
    for column in range(0, rows, width):
        table = one_hot(order[:, column : column + width], rows, 0)
        ordered_ref[:, column : column + width] = dot(charges[...], table).astype(BF16)
    stores[0].start()
    copies[4].wait()
    coords = dot(points[...], one_hot(skeletons[0], rows, 0)).astype(BF16)
    coords_ref[...] = coords
    stores[1].start()
    lane = lax.broadcasted_iota(jnp.int32, (1, count), 1)
    pattern = jnp.zeros((1, count), jnp.int32)
    for offset in range(mask.shape[1]):
        pattern = jnp.where(lane == offset, mask[:, offset : offset + 1], pattern)
    marks = jnp.broadcast_to(pattern.astype(F32), (PAD, count)).astype(BF16)
    marks_ref[...] = marks
    message_ref[dimension + 2 * sides :] = marks
    stores[2].start()
    copies[5].wait()
    weights = dot(ordered_ref[...], interp[...], NT)
    copies[6].wait()
    write_message(weights, coords, transfer[0], message_ref, passed_ref)
    stores[3].start()
    stores[4].start()
    for store in stores:
        store.wait()


def marked(marks, offset):
    rows = marks.astype(F32)
    lane = lax.broadcasted_iota(jnp.int32, rows.shape, 1)
    return jnp.max(jnp.where(lane == REACH + offset, rows, 0.0)) > 0.5


def round_kernel(level, last, skeletons, transfer, coords, passed, message, *outs):
    dimension = coords.shape[0]
    sides = passed.shape[0]
    bit = (lax.axis_index("leaf") >> level) & 1
    joined = pick(coords[...], message[:dimension], skeletons[level + 1], bit)
    span = slice(dimension + sides, dimension + 2 * sides)
    weights = passed[...] + message[span].astype(F32)
    if last:
        outs[0][:dimension] = joined
        outs[0][dimension:] = weights.astype(BF16)
        return
    outs[0][...] = joined
    write_message(weights, joined, transfer[level + 1], outs[1], outs[2])


def sibling_term(coords, message, sides):
    dimension = coords.shape[0]
    weights = message[dimension : dimension + sides].astype(F32)
    return dot(weights, small_kernel(message[:dimension], coords[...]), NN, HIGHEST)


def early_terms_kernel(levels, sides, transfer, *refs):
    outs = refs[2 * (levels - 1) :]
    for level in range(levels - 1):
        outs[level][...] = sibling_term(refs[2 * level], refs[2 * level + 1], sides)
    product = transfer[levels - 1].astype(F32)
    for level in range(levels - 2, -1, -1):
        product = dot(product, transfer[level].astype(F32), NN, HIGHEST)
    outs[-1][...] = product


def last_term_kernel(sides, transfer, coords, message, *refs):
    terms, potential_ref = refs[:-1], refs[-1]
    potential = sibling_term(coords, message, sides)
    for level in range(len(terms) - 1, -1, -1):
        potential = dot_split(potential, transfer[level]) + terms[level][...]
    potential_ref[...] = potential


def lane_norms(tall):
    square = jnp.square(tall.astype(F32))
    norms = jnp.sum(square, axis=1, keepdims=True) * (2.0 * LOG2E / tall.shape[1])
    return jnp.broadcast_to(norms, (tall.shape[0], 128))


def turn_kernel(points, ordered, tall_ref, norms_ref):
    dimension, rows = points.shape
    sides = ordered.shape[0]
    tall_ref[:rows] = jnp.transpose(points[...])
    norms_ref[...] = lane_norms(tall_ref[:rows])
    for number in range(rows // dimension):
        first = rows + number * sides
        tall_ref[first : first + sides] = ordered[:, number * dimension : (number + 1) * dimension]


def bands(tall, norms, wide):
    dimension, rows = wide.shape
    scale = 2.0 * LOG2E / dimension
    target_norms = row_norms(wide[...]) * scale
    for row in range(0, rows, dimension):
        band = slice(row, row + dimension)
        source = tall[band]
        inner = dot(source, wide[...])
        own = lane_norms(source) if norms is None else norms[band]
        squares = jnp.tile(own, (1, rows // 128)) + target_norms
        yield band, jnp.exp2((2.0 * scale) * inner - squares).astype(BF16)


def self_kernel(tall, norms, wide, ordered, near_ref):
    for band, tile in bands(tall, norms, wide):
        near_ref[:, band] = dot(ordered[...], tile, NT)


def near_kernel(tall, norms, wide, ordered, side_tall, back_wide, back_ordered, marks, message,
                near, near_ref, back_ref, side_ref, held):
    dimension, rows = wide.shape
    sides = ordered.shape[0]
    odd = lax.rem(lax.axis_index("leaf"), 2)
    with_back = marked(marks[...], -2)
    go_odd = jnp.logical_and(odd == 1, marked(message[message.shape[0] - PAD :], -1))
    go_even = jnp.logical_and(odd == 0, marked(marks[...], 1))
    near_ref[...] = near[...]

    @pl.when(with_back)
    def _():
        for band, tile in bands(tall, norms, back_wide):
            near_ref[:, band] += dot(back_ordered[...], tile, NT)
            part = dot(ordered[:, band], tile)
            if band.start:
                held[...] += part
            else:
                held[...] = part

    @pl.when(jnp.logical_not(with_back))
    def _():
        held[...] = jnp.zeros_like(held)

    def pair(other_wide, other_ordered, sum_ref):
        for band, tile in bands(side_tall, None, other_wide):
            side_ref[:, band] = dot(other_ordered[...], tile, NT).astype(BF16)
            first = rows + band.start // dimension * sides
            sum_ref[...] += dot(side_tall[first : first + sides], tile)

    @pl.when(go_odd)
    def _():
        pair(back_wide, back_ordered, held)

    @pl.when(go_even)
    def _():
        pair(wide, ordered, near_ref)

    @pl.when(jnp.logical_not(jnp.logical_or(go_odd, go_even)))
    def _():
        side_ref[...] = jnp.zeros_like(side_ref)

    back_ref[...] = held[...].astype(BF16)


def far_kernel(others, own_top, potential, product, interp, near, *refs):
    tops, out_ref = refs[:others], refs[-1]
    sides = out_ref.shape[0]
    dimension = own_top.shape[0] - sides
    total = potential[...]
    above = None
    for top in tops:
        part = dot(
            top[dimension:].astype(F32),
            small_kernel(top[:dimension], own_top[:dimension]),
            NN,
            HIGHEST,
        )
        above = part if above is None else above + part
    if above is not None:
        total = total + dot(above, product[...], NN, HIGHEST)
    out_ref[...] = near[...] + dot_split(total, interp[...])


def total_kernel(here, back, side, out_ref):
    out_ref[...] = here[...] + (back[...].astype(F32) + side[...].astype(F32))


def call(kernel, outs, args, scratch=(), anywhere=False, flops=0, exps=0, name=None):
    vmem = pl.BlockSpec(memory_space=pltpu.VMEM)
    rest = pl.BlockSpec(memory_space=pl.ANY) if anywhere else vmem
    moved = 0 if anywhere or flops == 0 else sum(a.size * a.dtype.itemsize for a in list(args) + list(outs))
    return pl.pallas_call(
        kernel,
        out_shape=outs,
        in_specs=[rest] * len(args),
        out_specs=[rest if anywhere else vmem] * len(outs),
        scratch_shapes=list(scratch),
        compiler_params=pltpu.CompilerParams(
            vmem_limit_bytes=START_VMEM if anywhere else VMEM_LIMIT
        ),
        cost_estimate=pl.CostEstimate(flops=flops, bytes_accessed=moved, transcendentals=exps),
        name=name,
    )(*args)


def swapped(value, axis, flip):
    count = lax.axis_size(axis)
    return lax.ppermute(value, axis, [(place, place ^ flip) for place in range(count)])


def rotated(value, axis, turn):
    count = lax.axis_size(axis)
    return lax.ppermute(value, axis, [(place, (place + turn) % count) for place in range(count)])


def shape(dims, dtype):
    return jax.ShapeDtypeStruct(dims, dtype)


def local(points, charges, order, near_mask, skeletons, leaf_interp, transfer):
    dimension, rows = points.shape
    sides, count = charges.shape[0], leaf_interp.shape[0]
    leaves, groups = lax.axis_size("leaf"), lax.axis_size("grp")
    levels = leaves.bit_length() - 1
    skeletons = jnp.transpose(skeletons, (1, 0, 2))
    transfer = transfer[0]
    block_sums = shape((sides, rows), F32)
    block_values = shape((sides, rows), BF16)
    node_points = shape((dimension, count), BF16)
    node_sums = shape((sides, count), F32)
    tile_flops = 2 * rows * rows * (dimension + 2 * sides)

    back_points = rotated(points, "leaf", 2)

    inputs = [order.reshape(1, rows), skeletons, near_mask, charges, points, leaf_interp, transfer]
    made = [
        block_values,
        node_points,
        shape((PAD, count), BF16),
        shape((dimension + 2 * sides + PAD, count), BF16),
        node_sums,
    ]
    ordered, coords, marks, message, passed = call(
        start_kernel,
        made,
        inputs,
        scratch=[pltpu.VMEM(value.shape, value.dtype) for value in inputs + made]
        + [pltpu.SemaphoreType.DMA((len(inputs),)), pltpu.SemaphoreType.DMA((len(made),))],
        anywhere=True,
        name="start",
    )
    tall, norms = call(
        turn_kernel,
        [shape((rows + sides * rows // dimension, dimension), BF16), shape((rows, 128), F32)],
        [points, ordered],
        name="turn",
    )
    (near,) = call(
        self_kernel,
        [block_sums],
        [tall, norms, points, ordered],
        name="self_tile",
    )

    history = []
    for level in range(levels):
        received = swapped(message, "leaf", 1 << level)
        if level == 0:
            received, near = lax.optimization_barrier((received, near))
            first_received = received
            side_tall = swapped(tall, "leaf", 1)
        if level == 1:
            received, back_points = lax.optimization_barrier((received, back_points))
        history += [coords, received]
        last = level == levels - 1
        if last:
            near, back, side = call(
                near_kernel,
                [block_sums, block_values, block_values],
                [tall, norms, points, ordered, side_tall, back_points, back_ordered]
                + [marks, first_received, lax.optimization_barrier((near, passed))[0]],
                scratch=[pltpu.VMEM((sides, rows), F32)],
                flops=2 * tile_flops,
                exps=2 * rows * rows,
                name="near_tiles",
            )
            passed, near = lax.optimization_barrier((passed, near))
            back = rotated(back, "leaf", -2)
            side = swapped(side, "leaf", 1)
            *terms, product = call(
                functools.partial(early_terms_kernel, levels, sides),
                [node_sums] * (levels - 1) + [shape((count, count), F32)],
                [transfer] + history[:-2],
                flops=8 * levels * dimension * count * count,
                exps=levels * count * count,
                name="early_terms",
            )
            passed, terms, product = lax.optimization_barrier((passed, terms, product))
        if last:
            outs = [shape((dimension + sides, count), BF16)]
        else:
            outs = [node_points, shape((dimension + 2 * sides, count), BF16), node_sums]
        results = call(
            functools.partial(round_kernel, level, last),
            outs,
            [skeletons, transfer, coords, passed, received],
            flops=JOIN_FLOPS * dimension * count * count,
            name="join_level",
        )
        if not last:
            coords, message, passed = results
        if level == min(1, levels - 1):
            sent = lax.optimization_barrier((ordered, results[-1]))[0]
            back_ordered = rotated(sent, "leaf", 2)
    own_top = results[0]
    tops = [rotated(own_top, "grp", turn) for turn in range(1, groups)]
    (potential,) = call(
        functools.partial(last_term_kernel, sides),
        [node_sums],
        [transfer] + history[-2:] + list(terms),
        flops=8 * dimension * count * count,
        exps=count * count,
        name="last_term",
    )
    (here,) = call(
        functools.partial(far_kernel, len(tops)),
        [block_sums],
        [own_top, potential, product, leaf_interp, near] + tops,
        flops=4 * sides * rows * count,
        name="far_field",
    )
    (out,) = call(total_kernel, [block_sums], [here, back, side], flops=2 * sides * rows, name="total")
    return out


def solution(mesh):
    in_specs = (
        P(None, ("leaf", "grp")),
        P(None, ("leaf", "grp")),
        P(("leaf", "grp")),
        P(("leaf", "grp"), None),
        P(("leaf", "grp"), None, None),
        P(None, ("leaf", "grp")),
        P(("leaf", "grp"), None, None, None),
    )
    out_specs = P(None, ("leaf", "grp"))
    return jax.shard_map(local, mesh=mesh, in_specs=in_specs, out_specs=out_specs, check_vma=False)
```

```python
import functools

import jax
import jax.numpy as jnp
from jax import lax
from jax.experimental import pallas as pl
from jax.experimental.pallas import tpu as pltpu
from jax.sharding import PartitionSpec as P

REACH = 2
BF16 = jnp.bfloat16
F32 = jnp.float32
LOG2E = 1.4426950408889634
HIGHEST = lax.Precision.HIGHEST
PAD = 16
JOIN_FLOPS = 500
VMEM_LIMIT = 40 * 1024 * 1024
START_VMEM = 56 * 1024 * 1024

NN = ((1,), (0,))
NT = ((1,), (1,))
TN = ((0,), (0,))


def dot(left, right, contract=NN, precision=None):
    return lax.dot_general(
        left, right, (contract, ((), ())), preferred_element_type=F32, precision=precision
    )


def halves(value):
    high = value.astype(BF16)
    return high, (value - high.astype(F32)).astype(BF16)


def dot_split(left, right, contract=NN):
    rows = left.shape[0]
    both = dot(jnp.concatenate(halves(left), axis=0), right, contract)
    return both[:rows] + both[rows:]


def row_norms(points):
    wide = points.astype(F32)
    return jnp.sum(wide * wide, axis=0, keepdims=True)


def column_norms(points):
    wide = points.astype(F32)
    high, low = halves(wide * wide)
    ones = jnp.ones((points.shape[0], 128), BF16)
    return dot(high, ones, TN) + dot(low, ones, TN)


def one_hot(index, rows, first):
    place = lax.broadcasted_iota(jnp.int32, (rows, index.shape[1]), 0) + first
    return jnp.where(place == index, 1.0, 0.0).astype(BF16)


def small_kernel(source, target):
    scale = 2.0 * LOG2E / source.shape[0]
    inner = dot(source, target, TN)
    squares = column_norms(source)[:, : target.shape[1]] + row_norms(target)
    return jnp.exp2(scale * (2.0 * inner - squares))


def pick(first, second, index, bit):
    count = first.shape[1]
    table = jnp.concatenate(
        [one_hot(index, count, count * bit), one_hot(index, count, count * (1 - bit))], axis=0
    )
    return dot(jnp.concatenate([first, second], axis=1), table).astype(BF16)


def write_message(weights, coords, matrix, message_ref, passed_ref):
    dimension, sides = coords.shape[0], weights.shape[0]
    passed = dot_split(weights, matrix, NT)
    message_ref[:dimension] = coords
    message_ref[dimension : dimension + sides] = weights.astype(BF16)
    message_ref[dimension + sides : dimension + 2 * sides] = passed.astype(BF16)
    passed_ref[...] = passed


def start_kernel(*refs):
    inputs, outs, held = refs[:7], refs[7:12], refs[12:19]
    made, sems, out_sems = refs[19:24], refs[24], refs[25]
    copies = [
        pltpu.make_async_copy(source, target, sems.at[number])
        for number, (source, target) in enumerate(zip(inputs, held))
    ]
    for copy in copies:
        copy.start()
    stores = [
        pltpu.make_async_copy(source, target, out_sems.at[number])
        for number, (source, target) in enumerate(zip(made, outs))
    ]
    order, skeletons, mask, charges, points, interp, transfer = held
    ordered_ref, coords_ref, marks_ref, message_ref, passed_ref = made
    dimension, rows = points.shape
    sides, count = passed_ref.shape
    for copy in copies[:4]:
        copy.wait()
    width = rows // 4
    for column in range(0, rows, width):
        table = one_hot(order[:, column : column + width], rows, 0)
        ordered_ref[:, column : column + width] = dot(charges[...], table).astype(BF16)
    stores[0].start()
    copies[4].wait()
    coords = dot(points[...], one_hot(skeletons[0], rows, 0)).astype(BF16)
    coords_ref[...] = coords
    stores[1].start()
    lane = lax.broadcasted_iota(jnp.int32, (1, count), 1)
    pattern = jnp.zeros((1, count), jnp.int32)
    for offset in range(mask.shape[1]):
        pattern = jnp.where(lane == offset, mask[:, offset : offset + 1], pattern)
    marks = jnp.broadcast_to(pattern.astype(F32), (PAD, count)).astype(BF16)
    marks_ref[...] = marks
    message_ref[dimension + 2 * sides :] = marks
    stores[2].start()
    copies[5].wait()
    weights = dot(ordered_ref[...], interp[...], NT)
    copies[6].wait()
    write_message(weights, coords, transfer[0], message_ref, passed_ref)
    stores[3].start()
    stores[4].start()
    for store in stores:
        store.wait()


def marked(marks, offset):
    rows = marks.astype(F32)
    lane = lax.broadcasted_iota(jnp.int32, rows.shape, 1)
    return jnp.max(jnp.where(lane == REACH + offset, rows, 0.0)) > 0.5


def round_kernel(level, last, skeletons, transfer, coords, passed, message, *outs):
    dimension = coords.shape[0]
    sides = passed.shape[0]
    bit = (lax.axis_index("leaf") >> level) & 1
    joined = pick(coords[...], message[:dimension], skeletons[level + 1], bit)
    span = slice(dimension + sides, dimension + 2 * sides)
    weights = passed[...] + message[span].astype(F32)
    if last:
        outs[0][:dimension] = joined
        outs[0][dimension:] = weights.astype(BF16)
        return
    outs[0][...] = joined
    write_message(weights, joined, transfer[level + 1], outs[1], outs[2])


def sibling_term(coords, message, sides):
    dimension = coords.shape[0]
    weights = message[dimension : dimension + sides].astype(F32)
    return dot(weights, small_kernel(message[:dimension], coords[...]), NN, HIGHEST)


def early_terms_kernel(levels, sides, transfer, *refs):
    outs = refs[2 * (levels - 1) :]
    for level in range(levels - 1):
        outs[level][...] = sibling_term(refs[2 * level], refs[2 * level + 1], sides)
    product = transfer[levels - 1].astype(F32)
    for level in range(levels - 2, -1, -1):
        product = dot(product, transfer[level].astype(F32), NN, HIGHEST)
    outs[-1][...] = product


def last_term_kernel(sides, transfer, coords, message, *refs):
    terms, potential_ref = refs[:-1], refs[-1]
    potential = sibling_term(coords, message, sides)
    for level in range(len(terms) - 1, -1, -1):
        potential = dot_split(potential, transfer[level]) + terms[level][...]
    potential_ref[...] = potential


def lane_norms(tall):
    square = jnp.square(tall.astype(F32))
    norms = jnp.sum(square, axis=1, keepdims=True) * (2.0 * LOG2E / tall.shape[1])
    return jnp.broadcast_to(norms, (tall.shape[0], 128))


def turn_kernel(points, ordered, tall_ref, norms_ref):
    dimension, rows = points.shape
    sides = ordered.shape[0]
    tall_ref[:rows] = jnp.transpose(points[...])
    norms_ref[...] = lane_norms(tall_ref[:rows])
    for number in range(rows // dimension):
        first = rows + number * sides
        tall_ref[first : first + sides] = ordered[:, number * dimension : (number + 1) * dimension]


def bands(tall, norms, wide):
    dimension, rows = wide.shape
    scale = 2.0 * LOG2E / dimension
    target_norms = row_norms(wide[...]) * scale
    for row in range(0, rows, dimension):
        band = slice(row, row + dimension)
        source = tall[band]
        inner = dot(source, wide[...])
        own = lane_norms(source) if norms is None else norms[band]
        squares = jnp.tile(own, (1, rows // 128)) + target_norms
        yield band, jnp.exp2((2.0 * scale) * inner - squares).astype(BF16)


def self_kernel(tall, norms, wide, ordered, near_ref):
    for band, tile in bands(tall, norms, wide):
        near_ref[:, band] = dot(ordered[...], tile, NT)


def near_kernel(tall, norms, wide, ordered, side_tall, back_wide, back_ordered, marks, message,
                near, near_ref, back_ref, side_ref, held):
    dimension, rows = wide.shape
    sides = ordered.shape[0]
    odd = lax.rem(lax.axis_index("leaf"), 2)
    with_back = marked(marks[...], -2)
    go_odd = jnp.logical_and(odd == 1, marked(message[message.shape[0] - PAD :], -1))
    go_even = jnp.logical_and(odd == 0, marked(marks[...], 1))
    near_ref[...] = near[...]

    @pl.when(with_back)
    def _():
        for band, tile in bands(tall, norms, back_wide):
            near_ref[:, band] += dot(back_ordered[...], tile, NT)
            part = dot(ordered[:, band], tile)
            if band.start:
                held[...] += part
            else:
                held[...] = part

    @pl.when(jnp.logical_not(with_back))
    def _():
        held[...] = jnp.zeros_like(held)

    def pair(other_wide, other_ordered, sum_ref):
        for band, tile in bands(side_tall, None, other_wide):
            side_ref[:, band] = dot(other_ordered[...], tile, NT).astype(BF16)
            first = rows + band.start // dimension * sides
            sum_ref[...] += dot(side_tall[first : first + sides], tile)

    @pl.when(go_odd)
    def _():
        pair(back_wide, back_ordered, held)

    @pl.when(go_even)
    def _():
        pair(wide, ordered, near_ref)

    @pl.when(jnp.logical_not(jnp.logical_or(go_odd, go_even)))
    def _():
        side_ref[...] = jnp.zeros_like(side_ref)

    back_ref[...] = held[...].astype(BF16)


def far_kernel(others, own_top, potential, product, interp, near, *refs):
    tops, out_ref = refs[:others], refs[-1]
    sides = out_ref.shape[0]
    dimension = own_top.shape[0] - sides
    total = potential[...]
    above = None
    for top in tops:
        part = dot(
            top[dimension:].astype(F32),
            small_kernel(top[:dimension], own_top[:dimension]),
            NN,
            HIGHEST,
        )
        above = part if above is None else above + part
    if above is not None:
        total = total + dot(above, product[...], NN, HIGHEST)
    out_ref[...] = near[...] + dot_split(total, interp[...])


def total_kernel(here, back, side, out_ref):
    out_ref[...] = here[...] + (back[...].astype(F32) + side[...].astype(F32))


def call(kernel, outs, args, scratch=(), anywhere=False, flops=0, exps=0, name=None):
    vmem = pl.BlockSpec(memory_space=pltpu.VMEM)
    rest = pl.BlockSpec(memory_space=pl.ANY) if anywhere else vmem
    moved = 0 if anywhere or flops == 0 else sum(a.size * a.dtype.itemsize for a in list(args) + list(outs))
    return pl.pallas_call(
        kernel,
        out_shape=outs,
        in_specs=[rest] * len(args),
        out_specs=[rest if anywhere else vmem] * len(outs),
        scratch_shapes=list(scratch),
        compiler_params=pltpu.CompilerParams(
            vmem_limit_bytes=START_VMEM if anywhere else VMEM_LIMIT
        ),
        cost_estimate=pl.CostEstimate(flops=flops, bytes_accessed=moved, transcendentals=exps),
        name=name,
    )(*args)


def swapped(value, axis, flip):
    count = lax.axis_size(axis)
    return lax.ppermute(value, axis, [(place, place ^ flip) for place in range(count)])


def rotated(value, axis, turn):
    count = lax.axis_size(axis)
    return lax.ppermute(value, axis, [(place, (place + turn) % count) for place in range(count)])


def shifted(value, axis, step):
    places = range(lax.axis_size(axis))
    return lax.ppermute(
        value, axis, [(place, place + step) for place in places if place + step in places]
    )


def shape(dims, dtype):
    return jax.ShapeDtypeStruct(dims, dtype)


def local(points, charges, order, near_mask, skeletons, leaf_interp, transfer):
    dimension, rows = points.shape
    sides, count = charges.shape[0], leaf_interp.shape[0]
    leaves, groups = lax.axis_size("leaf"), lax.axis_size("grp")
    levels = leaves.bit_length() - 1
    skeletons = jnp.transpose(skeletons, (1, 0, 2))
    transfer = transfer[0]
    block_sums = shape((sides, rows), F32)
    block_values = shape((sides, rows), BF16)
    node_points = shape((dimension, count), BF16)
    node_sums = shape((sides, count), F32)
    tile_flops = 2 * rows * rows * (dimension + 2 * sides)

    back_points = rotated(points, "leaf", 2)

    inputs = [order.reshape(1, rows), skeletons, near_mask, charges, points, leaf_interp, transfer]
    made = [
        block_values,
        node_points,
        shape((PAD, count), BF16),
        shape((dimension + 2 * sides + PAD, count), BF16),
        node_sums,
    ]
    ordered, coords, marks, message, passed = call(
        start_kernel,
        made,
        inputs,
        scratch=[pltpu.VMEM(value.shape, value.dtype) for value in inputs + made]
        + [pltpu.SemaphoreType.DMA((len(inputs),)), pltpu.SemaphoreType.DMA((len(made),))],
        anywhere=True,
        name="start",
    )
    tall, norms = call(
        turn_kernel,
        [shape((rows + sides * rows // dimension, dimension), BF16), shape((rows, 128), F32)],
        [points, ordered],
        name="turn",
    )
    (near,) = call(
        self_kernel,
        [block_sums],
        [tall, norms, points, ordered],
        name="self_tile",
    )

    history = []
    for level in range(levels):
        received = swapped(message, "leaf", 1 << level)
        if level == 0:
            received, near = lax.optimization_barrier((received, near))
            first_received = received
            side_tall = swapped(tall, "leaf", 1)
        if level == 1:
            received, back_points = lax.optimization_barrier((received, back_points))
        history += [coords, received]
        last = level == levels - 1
        if last:
            near, back, side = call(
                near_kernel,
                [block_sums, block_values, block_values],
                [tall, norms, points, ordered, side_tall, back_points, back_ordered]
                + [marks, first_received, lax.optimization_barrier((near, passed))[0]],
                scratch=[pltpu.VMEM((sides, rows), F32)],
                flops=2 * tile_flops,
                exps=2 * rows * rows,
                name="near_tiles",
            )
            passed, near = lax.optimization_barrier((passed, near))
            back = shifted(back, "leaf", -2)
            side = swapped(side, "leaf", 1)
            *terms, product = call(
                functools.partial(early_terms_kernel, levels, sides),
                [node_sums] * (levels - 1) + [shape((count, count), F32)],
                [transfer] + history[:-2],
                flops=8 * levels * dimension * count * count,
                exps=levels * count * count,
                name="early_terms",
            )
            passed, terms, product = lax.optimization_barrier((passed, terms, product))
        if last:
            outs = [shape((dimension + sides, count), BF16)]
        else:
            outs = [node_points, shape((dimension + 2 * sides, count), BF16), node_sums]
        results = call(
            functools.partial(round_kernel, level, last),
            outs,
            [skeletons, transfer, coords, passed, received],
            flops=(JOIN_FLOPS if level < 2 else 8) * dimension * count * count,
            name="join_level",
        )
        if not last:
            coords, message, passed = results
        if level == 0:
            sent = lax.optimization_barrier((ordered, results[-1]))[0]
            back_ordered = shifted(sent, "leaf", 2)
    own_top = results[0]
    tops = [rotated(own_top, "grp", turn) for turn in range(1, groups)]
    (potential,) = call(
        functools.partial(last_term_kernel, sides),
        [node_sums],
        [transfer] + history[-2:] + list(terms),
        flops=8 * dimension * count * count,
        exps=count * count,
        name="last_term",
    )
    (here,) = call(
        functools.partial(far_kernel, len(tops)),
        [block_sums],
        [own_top, potential, product, leaf_interp, near] + tops,
        flops=4 * sides * rows * count,
        name="far_field",
    )
    (out,) = call(total_kernel, [block_sums], [here, back, side], flops=2 * sides * rows, name="total")
    return out


def solution(mesh):
    in_specs = (
        P(None, ("leaf", "grp")),
        P(None, ("leaf", "grp")),
        P(("leaf", "grp")),
        P(("leaf", "grp"), None),
        P(("leaf", "grp"), None, None),
        P(None, ("leaf", "grp")),
        P(("leaf", "grp"), None, None, None),
    )
    out_specs = P(None, ("leaf", "grp"))
    return jax.shard_map(local, mesh=mesh, in_specs=in_specs, out_specs=out_specs, check_vma=False)
```

```python
import functools

import jax
import jax.numpy as jnp
from jax import lax
from jax.experimental import pallas as pl
from jax.experimental.pallas import tpu as pltpu
from jax.sharding import PartitionSpec as P

REACH = 2
BF16 = jnp.bfloat16
F32 = jnp.float32
LOG2E = 1.4426950408889634
HIGHEST = lax.Precision.HIGHEST
PAD = 16
JOIN_FLOPS = 500
VMEM_LIMIT = 40 * 1024 * 1024
START_VMEM = 56 * 1024 * 1024

NN = ((1,), (0,))
NT = ((1,), (1,))
TN = ((0,), (0,))


def dot(left, right, contract=NN, precision=None):
    return lax.dot_general(
        left, right, (contract, ((), ())), preferred_element_type=F32, precision=precision
    )


def halves(value):
    high = value.astype(BF16)
    return high, (value - high.astype(F32)).astype(BF16)


def dot_split(left, right, contract=NN):
    rows = left.shape[0]
    both = dot(jnp.concatenate(halves(left), axis=0), right, contract)
    return both[:rows] + both[rows:]


def row_norms(points):
    wide = points.astype(F32)
    return jnp.sum(wide * wide, axis=0, keepdims=True)


def column_norms(points):
    wide = points.astype(F32)
    high, low = halves(wide * wide)
    ones = jnp.ones((points.shape[0], 128), BF16)
    return dot(high, ones, TN) + dot(low, ones, TN)


def one_hot(index, rows, first):
    place = lax.broadcasted_iota(jnp.int32, (rows, index.shape[1]), 0) + first
    return jnp.where(place == index, 1.0, 0.0).astype(BF16)


def small_kernel(source, target):
    scale = 2.0 * LOG2E / source.shape[0]
    inner = dot(source, target, TN)
    squares = column_norms(source)[:, : target.shape[1]] + row_norms(target)
    return jnp.exp2(scale * (2.0 * inner - squares))


def pick(first, second, index, bit):
    count = first.shape[1]
    table = jnp.concatenate(
        [one_hot(index, count, count * bit), one_hot(index, count, count * (1 - bit))], axis=0
    )
    return dot(jnp.concatenate([first, second], axis=1), table).astype(BF16)


def write_message(weights, coords, matrix, message_ref, passed_ref):
    dimension, sides = coords.shape[0], weights.shape[0]
    passed = dot_split(weights, matrix, NT)
    message_ref[:dimension] = coords
    message_ref[dimension : dimension + sides] = weights.astype(BF16)
    message_ref[dimension + sides : dimension + 2 * sides] = passed.astype(BF16)
    passed_ref[...] = passed


def start_kernel(*refs):
    inputs, outs, held = refs[:7], refs[7:12], refs[12:19]
    made, sems, out_sems = refs[19:24], refs[24], refs[25]
    copies = [
        pltpu.make_async_copy(source, target, sems.at[number])
        for number, (source, target) in enumerate(zip(inputs, held))
    ]
    for copy in copies:
        copy.start()
    stores = [
        pltpu.make_async_copy(source, target, out_sems.at[number])
        for number, (source, target) in enumerate(zip(made, outs))
    ]
    order, skeletons, mask, charges, points, interp, transfer = held
    ordered_ref, coords_ref, marks_ref, message_ref, passed_ref = made
    dimension, rows = points.shape
    sides, count = passed_ref.shape
    for copy in copies[:4]:
        copy.wait()
    width = rows // 4
    for column in range(0, rows, width):
        table = one_hot(order[:, column : column + width], rows, 0)
        ordered_ref[:, column : column + width] = dot(charges[...], table).astype(BF16)
    stores[0].start()
    copies[4].wait()
    coords = dot(points[...], one_hot(skeletons[0], rows, 0)).astype(BF16)
    coords_ref[...] = coords
    stores[1].start()
    lane = lax.broadcasted_iota(jnp.int32, (1, count), 1)
    pattern = jnp.zeros((1, count), jnp.int32)
    for offset in range(mask.shape[1]):
        pattern = jnp.where(lane == offset, mask[:, offset : offset + 1], pattern)
    marks = jnp.broadcast_to(pattern.astype(F32), (PAD, count)).astype(BF16)
    marks_ref[...] = marks
    message_ref[dimension + 2 * sides :] = marks
    stores[2].start()
    copies[5].wait()
    weights = dot(ordered_ref[...], interp[...], NT)
    copies[6].wait()
    write_message(weights, coords, transfer[0], message_ref, passed_ref)
    stores[3].start()
    stores[4].start()
    for store in stores:
        store.wait()


def marked(marks, offset):
    rows = marks.astype(F32)
    lane = lax.broadcasted_iota(jnp.int32, rows.shape, 1)
    return jnp.max(jnp.where(lane == REACH + offset, rows, 0.0)) > 0.5


def round_kernel(level, last, skeletons, transfer, coords, passed, message, *outs):
    dimension = coords.shape[0]
    sides = passed.shape[0]
    bit = (lax.axis_index("leaf") >> level) & 1
    joined = pick(coords[...], message[:dimension], skeletons[level + 1], bit)
    span = slice(dimension + sides, dimension + 2 * sides)
    weights = passed[...] + message[span].astype(F32)
    if last:
        outs[0][:dimension] = joined
        outs[0][dimension:] = weights.astype(BF16)
        return
    outs[0][...] = joined
    write_message(weights, joined, transfer[level + 1], outs[1], outs[2])


def sibling_term(coords, message, sides):
    dimension = coords.shape[0]
    weights = message[dimension : dimension + sides].astype(F32)
    return dot(weights, small_kernel(message[:dimension], coords[...]), NN, HIGHEST)


def term_kernel(sides, levels, transfer, coords, message, term_ref, *product_ref):
    term_ref[...] = sibling_term(coords, message, sides)
    if product_ref:
        product = transfer[levels - 1].astype(F32)
        for level in range(levels - 2, -1, -1):
            product = dot(product, transfer[level].astype(F32), NN, HIGHEST)
        product_ref[0][...] = product


def last_terms_kernel(sides, levels, transfer, *refs):
    pairs, terms, potential_ref = refs[:4], refs[4:-1], refs[-1]
    late = [sibling_term(pairs[0], pairs[1], sides), sibling_term(pairs[2], pairs[3], sides)]
    terms = [ref[...] for ref in terms] + late
    potential = terms[-1]
    for level in range(levels - 2, -1, -1):
        potential = dot_split(potential, transfer[level]) + terms[level]
    potential_ref[...] = potential


def lane_norms(tall):
    square = jnp.square(tall.astype(F32))
    norms = jnp.sum(square, axis=1, keepdims=True) * (2.0 * LOG2E / tall.shape[1])
    return jnp.broadcast_to(norms, (tall.shape[0], 128))


def turn_kernel(points, ordered, tall_ref, norms_ref):
    dimension, rows = points.shape
    sides = ordered.shape[0]
    tall_ref[:rows] = jnp.transpose(points[...])
    norms_ref[...] = lane_norms(tall_ref[:rows])
    for number in range(rows // dimension):
        first = rows + number * sides
        tall_ref[first : first + sides] = ordered[:, number * dimension : (number + 1) * dimension]


def bands(tall, norms, wide):
    dimension, rows = wide.shape
    scale = 2.0 * LOG2E / dimension
    target_norms = row_norms(wide[...]) * scale
    for row in range(0, rows, dimension):
        band = slice(row, row + dimension)
        source = tall[band]
        inner = dot(source, wide[...])
        own = lane_norms(source) if norms is None else norms[band]
        squares = jnp.tile(own, (1, rows // 128)) + target_norms
        yield band, jnp.exp2((2.0 * scale) * inner - squares).astype(BF16)


def self_kernel(tall, norms, wide, ordered, near_ref):
    for band, tile in bands(tall, norms, wide):
        near_ref[:, band] = dot(ordered[...], tile, NT)


def back_kernel(tall, norms, ordered, back_wide, back_ordered, marks, near, near_ref, held_ref):
    near_ref[...] = near[...]
    used = marked(marks[...], -2)

    @pl.when(used)
    def _():
        for band, tile in bands(tall, norms, back_wide):
            near_ref[:, band] += dot(back_ordered[...], tile, NT)
            part = dot(ordered[:, band], tile)
            if band.start:
                held_ref[...] += part
            else:
                held_ref[...] = part

    @pl.when(jnp.logical_not(used))
    def _():
        held_ref[...] = jnp.zeros_like(held_ref)


def pair_kernel(wide, ordered, side_tall, back_wide, back_ordered, marks, message, near, held,
                near_ref, back_ref, side_ref, sum_ref):
    dimension, rows = wide.shape
    sides = ordered.shape[0]
    odd = lax.rem(lax.axis_index("leaf"), 2)
    go_odd = jnp.logical_and(odd == 1, marked(message[message.shape[0] - PAD :], -1))
    go_even = jnp.logical_and(odd == 0, marked(marks[...], 1))

    def pair(other_wide, other_ordered):
        for band, tile in bands(side_tall, None, other_wide):
            side_ref[:, band] = dot(other_ordered[...], tile, NT).astype(BF16)
            first = rows + band.start // dimension * sides
            part = dot(side_tall[first : first + sides], tile)
            if band.start:
                sum_ref[...] += part
            else:
                sum_ref[...] = part

    @pl.when(go_odd)
    def _():
        pair(back_wide, back_ordered)
        back_ref[...] = (held[...] + sum_ref[...]).astype(BF16)
        near_ref[...] = near[...]

    @pl.when(go_even)
    def _():
        pair(wide, ordered)
        back_ref[...] = held[...].astype(BF16)
        near_ref[...] = near[...] + sum_ref[...]

    @pl.when(jnp.logical_not(jnp.logical_or(go_odd, go_even)))
    def _():
        back_ref[...] = held[...].astype(BF16)
        near_ref[...] = near[...]
        side_ref[...] = jnp.zeros_like(side_ref)


def far_kernel(others, own_top, potential, product, interp, near, *refs):
    tops, out_ref = refs[:others], refs[-1]
    sides = out_ref.shape[0]
    dimension = own_top.shape[0] - sides
    total = potential[...]
    above = None
    for top in tops:
        part = dot(
            top[dimension:].astype(F32),
            small_kernel(top[:dimension], own_top[:dimension]),
            NN,
            HIGHEST,
        )
        above = part if above is None else above + part
    if above is not None:
        total = total + dot(above, product[...], NN, HIGHEST)
    out_ref[...] = near[...] + dot_split(total, interp[...])


def total_kernel(here, back, side, out_ref):
    out_ref[...] = here[...] + (back[...].astype(F32) + side[...].astype(F32))


def call(kernel, outs, args, scratch=(), anywhere=False, flops=0, exps=0, name=None):
    vmem = pl.BlockSpec(memory_space=pltpu.VMEM)
    rest = pl.BlockSpec(memory_space=pl.ANY) if anywhere else vmem
    moved = 0 if anywhere or flops == 0 else sum(a.size * a.dtype.itemsize for a in list(args) + list(outs))
    return pl.pallas_call(
        kernel,
        out_shape=outs,
        in_specs=[rest] * len(args),
        out_specs=[rest if anywhere else vmem] * len(outs),
        scratch_shapes=list(scratch),
        compiler_params=pltpu.CompilerParams(
            vmem_limit_bytes=START_VMEM if anywhere else VMEM_LIMIT
        ),
        cost_estimate=pl.CostEstimate(flops=flops, bytes_accessed=moved, transcendentals=exps),
        name=name,
    )(*args)


def swapped(value, axis, flip):
    count = lax.axis_size(axis)
    return lax.ppermute(value, axis, [(place, place ^ flip) for place in range(count)])


def rotated(value, axis, turn):
    count = lax.axis_size(axis)
    return lax.ppermute(value, axis, [(place, (place + turn) % count) for place in range(count)])


def shifted(value, axis, step):
    places = range(lax.axis_size(axis))
    return lax.ppermute(
        value, axis, [(place, place + step) for place in places if place + step in places]
    )


def shape(dims, dtype):
    return jax.ShapeDtypeStruct(dims, dtype)


def local(points, charges, order, near_mask, skeletons, leaf_interp, transfer):
    dimension, rows = points.shape
    sides, count = charges.shape[0], leaf_interp.shape[0]
    leaves, groups = lax.axis_size("leaf"), lax.axis_size("grp")
    levels = leaves.bit_length() - 1
    skeletons = jnp.transpose(skeletons, (1, 0, 2))
    transfer = transfer[0]
    block_sums = shape((sides, rows), F32)
    block_values = shape((sides, rows), BF16)
    node_points = shape((dimension, count), BF16)
    node_sums = shape((sides, count), F32)
    tile_flops = 2 * rows * rows * (dimension + 2 * sides)

    back_points = rotated(points, "leaf", 2)

    inputs = [order.reshape(1, rows), skeletons, near_mask, charges, points, leaf_interp, transfer]
    made = [
        block_values,
        node_points,
        shape((PAD, count), BF16),
        shape((dimension + 2 * sides + PAD, count), BF16),
        node_sums,
    ]
    ordered, coords, marks, message, passed = call(
        start_kernel,
        made,
        inputs,
        scratch=[pltpu.VMEM(value.shape, value.dtype) for value in inputs + made]
        + [pltpu.SemaphoreType.DMA((len(inputs),)), pltpu.SemaphoreType.DMA((len(made),))],
        anywhere=True,
        name="start",
    )
    tall, norms = call(
        turn_kernel,
        [shape((rows + sides * rows // dimension, dimension), BF16), shape((rows, 128), F32)],
        [points, ordered],
        name="turn",
    )
    (near,) = call(
        self_kernel,
        [block_sums],
        [tall, norms, points, ordered],
        name="self_tile",
    )

    history, terms = [], []
    for level in range(levels):
        received = swapped(message, "leaf", 1 << level)
        if level == 0:
            received, near = lax.optimization_barrier((received, near))
            first_received = received
            side_tall = swapped(tall, "leaf", 1)
        if level == 1:
            received, back_points = lax.optimization_barrier((received, back_points))
        last = level == levels - 1
        if level and not last:
            made = call(
                functools.partial(term_kernel, sides, levels),
                [node_sums] + [shape((count, count), F32)] * (level == 1),
                [transfer] + history[-2:],
                flops=8 * dimension * count * count,
                name="sibling_term",
            )
            terms.append(made[0])
            if level == 1:
                product = made[1]
            passed = lax.optimization_barrier((passed, made[0]))[0]
        history += [coords, received]
        if level == levels - 2:
            near, held = call(
                back_kernel,
                [block_sums, block_sums],
                [tall, norms, ordered, back_points, back_ordered, marks]
                + [lax.optimization_barrier((near, passed))[0]],
                flops=tile_flops,
                exps=rows * rows,
                name="back_tile",
            )
            passed, held = lax.optimization_barrier((passed, held))
        if last:
            near, back, side = call(
                pair_kernel,
                [block_sums, block_values, block_values],
                [points, ordered, side_tall, back_points, back_ordered, marks, first_received]
                + [lax.optimization_barrier((near, passed))[0], held],
                scratch=[pltpu.VMEM((sides, rows), F32)],
                flops=tile_flops,
                exps=rows * rows,
                name="pair_tile",
            )
            passed, near = lax.optimization_barrier((passed, near))
            back = shifted(back, "leaf", -2)
            side = swapped(side, "leaf", 1)
        if last:
            outs = [shape((dimension + sides, count), BF16)]
        else:
            outs = [node_points, shape((dimension + 2 * sides, count), BF16), node_sums]
        results = call(
            functools.partial(round_kernel, level, last),
            outs,
            [skeletons, transfer, coords, passed, received],
            flops=(JOIN_FLOPS if level < 2 else 8) * dimension * count * count,
            name="join_level",
        )
        if not last:
            coords, message, passed = results
        if level == 0:
            sent = lax.optimization_barrier((ordered, results[-1]))[0]
            back_ordered = shifted(sent, "leaf", 2)
    own_top = results[0]
    tops = [rotated(own_top, "grp", turn) for turn in range(1, groups)]
    (potential,) = call(
        functools.partial(last_terms_kernel, sides, levels),
        [node_sums],
        [transfer] + history[-4:] + terms,
        flops=8 * dimension * count * count,
        exps=count * count,
        name="last_terms",
    )
    (here,) = call(
        functools.partial(far_kernel, len(tops)),
        [block_sums],
        [own_top, potential, product, leaf_interp, near] + tops,
        flops=4 * sides * rows * count,
        name="far_field",
    )
    (out,) = call(total_kernel, [block_sums], [here, back, side], flops=2 * sides * rows, name="total")
    return out


def solution(mesh):
    in_specs = (
        P(None, ("leaf", "grp")),
        P(None, ("leaf", "grp")),
        P(("leaf", "grp")),
        P(("leaf", "grp"), None),
        P(("leaf", "grp"), None, None),
        P(None, ("leaf", "grp")),
        P(("leaf", "grp"), None, None, None),
    )
    out_specs = P(None, ("leaf", "grp"))
    return jax.shard_map(local, mesh=mesh, in_specs=in_specs, out_specs=out_specs, check_vma=False)
```

```python
import functools

import jax
import jax.numpy as jnp
from jax import lax
from jax.experimental import pallas as pl
from jax.experimental.pallas import tpu as pltpu
from jax.sharding import PartitionSpec as P

REACH = 2
BF16 = jnp.bfloat16
F32 = jnp.float32
LOG2E = 1.4426950408889634
HIGHEST = lax.Precision.HIGHEST
PAD = 16
JOIN_FLOPS = 500
VMEM_LIMIT = 40 * 1024 * 1024
START_VMEM = 56 * 1024 * 1024

NN = ((1,), (0,))
NT = ((1,), (1,))
TN = ((0,), (0,))


def dot(left, right, contract=NN, precision=None):
    return lax.dot_general(
        left, right, (contract, ((), ())), preferred_element_type=F32, precision=precision
    )


def halves(value):
    high = value.astype(BF16)
    return high, (value - high.astype(F32)).astype(BF16)


def dot_split(left, right, contract=NN):
    rows = left.shape[0]
    both = dot(jnp.concatenate(halves(left), axis=0), right, contract)
    return both[:rows] + both[rows:]


def row_norms(points):
    wide = points.astype(F32)
    return jnp.sum(wide * wide, axis=0, keepdims=True)


def column_norms(points):
    wide = points.astype(F32)
    high, low = halves(wide * wide)
    ones = jnp.ones((points.shape[0], 128), BF16)
    return dot(high, ones, TN) + dot(low, ones, TN)


def one_hot(index, rows, first):
    place = lax.broadcasted_iota(jnp.int32, (rows, index.shape[1]), 0) + first
    return jnp.where(place == index, 1.0, 0.0).astype(BF16)


def small_kernel(source, target):
    scale = 2.0 * LOG2E / source.shape[0]
    inner = dot(source, target, TN)
    squares = column_norms(source)[:, : target.shape[1]] + row_norms(target)
    return jnp.exp2(scale * (2.0 * inner - squares))


def pick(first, second, index, bit):
    count = first.shape[1]
    table = jnp.concatenate(
        [one_hot(index, count, count * bit), one_hot(index, count, count * (1 - bit))], axis=0
    )
    return dot(jnp.concatenate([first, second], axis=1), table).astype(BF16)


def write_message(weights, coords, matrix, message_ref, passed_ref):
    dimension, sides = coords.shape[0], weights.shape[0]
    passed = dot_split(weights, matrix, NT)
    message_ref[:dimension] = coords
    message_ref[dimension : dimension + sides] = weights.astype(BF16)
    message_ref[dimension + sides : dimension + 2 * sides] = passed.astype(BF16)
    passed_ref[...] = passed


def start_kernel(*refs):
    inputs, outs, held = refs[:7], refs[7:12], refs[12:19]
    made, sems, out_sems = refs[19:24], refs[24], refs[25]
    copies = [
        pltpu.make_async_copy(source, target, sems.at[number])
        for number, (source, target) in enumerate(zip(inputs, held))
    ]
    for copy in copies:
        copy.start()
    stores = [
        pltpu.make_async_copy(source, target, out_sems.at[number])
        for number, (source, target) in enumerate(zip(made, outs))
    ]
    order, skeletons, mask, charges, points, interp, transfer = held
    ordered_ref, coords_ref, marks_ref, message_ref, passed_ref = made
    dimension, rows = points.shape
    sides, count = passed_ref.shape
    for copy in copies[:4]:
        copy.wait()
    width = rows // 4
    for column in range(0, rows, width):
        table = one_hot(order[:, column : column + width], rows, 0)
        ordered_ref[:, column : column + width] = dot(charges[...], table).astype(BF16)
    stores[0].start()
    copies[4].wait()
    coords = dot(points[...], one_hot(skeletons[0], rows, 0)).astype(BF16)
    coords_ref[...] = coords
    stores[1].start()
    lane = lax.broadcasted_iota(jnp.int32, (1, count), 1)
    pattern = jnp.zeros((1, count), jnp.int32)
    for offset in range(mask.shape[1]):
        pattern = jnp.where(lane == offset, mask[:, offset : offset + 1], pattern)
    marks = jnp.broadcast_to(pattern.astype(F32), (PAD, count)).astype(BF16)
    marks_ref[...] = marks
    message_ref[dimension + 2 * sides :] = marks
    stores[2].start()
    copies[5].wait()
    weights = dot(ordered_ref[...], interp[...], NT)
    copies[6].wait()
    write_message(weights, coords, transfer[0], message_ref, passed_ref)
    stores[3].start()
    stores[4].start()
    for store in stores:
        store.wait()


def marked(marks, offset):
    rows = marks.astype(F32)
    lane = lax.broadcasted_iota(jnp.int32, rows.shape, 1)
    return jnp.max(jnp.where(lane == REACH + offset, rows, 0.0)) > 0.5


def round_kernel(level, last, skeletons, transfer, coords, passed, message, *outs):
    dimension = coords.shape[0]
    sides = passed.shape[0]
    bit = (lax.axis_index("leaf") >> level) & 1
    joined = pick(coords[...], message[:dimension], skeletons[level + 1], bit)
    span = slice(dimension + sides, dimension + 2 * sides)
    weights = passed[...] + message[span].astype(F32)
    if last:
        outs[0][:dimension] = joined
        outs[0][dimension:] = weights.astype(BF16)
        return
    outs[0][...] = joined
    write_message(weights, joined, transfer[level + 1], outs[1], outs[2])


def sibling_term(coords, message, sides):
    dimension = coords.shape[0]
    weights = message[dimension : dimension + sides].astype(F32)
    return dot(weights, small_kernel(message[:dimension], coords[...]), NN, HIGHEST)


def term_kernel(sides, levels, transfer, coords, message, term_ref, *product_ref):
    term_ref[...] = sibling_term(coords, message, sides)
    if product_ref:
        product = transfer[levels - 1].astype(F32)
        for level in range(levels - 2, -1, -1):
            product = dot(product, transfer[level].astype(F32), NN, HIGHEST)
        product_ref[0][...] = product


def last_terms_kernel(sides, levels, transfer, *refs):
    pairs, terms, potential_ref = refs[:4], refs[4:-1], refs[-1]
    late = [sibling_term(pairs[0], pairs[1], sides), sibling_term(pairs[2], pairs[3], sides)]
    terms = [ref[...] for ref in terms] + late
    potential = terms[-1]
    for level in range(levels - 2, -1, -1):
        potential = dot_split(potential, transfer[level]) + terms[level]
    potential_ref[...] = potential


def lane_norms(tall):
    square = jnp.square(tall.astype(F32))
    norms = jnp.sum(square, axis=1, keepdims=True) * (2.0 * LOG2E / tall.shape[1])
    return jnp.broadcast_to(norms, (tall.shape[0], 128))


def turn_kernel(points, ordered, tall_ref, norms_ref):
    dimension, rows = points.shape
    sides = ordered.shape[0]
    tall_ref[:rows] = jnp.transpose(points[...])
    norms_ref[...] = lane_norms(tall_ref[:rows])
    for number in range(rows // dimension):
        first = rows + number * sides
        tall_ref[first : first + sides] = ordered[:, number * dimension : (number + 1) * dimension]


def bands(tall, norms, wide):
    dimension, rows = wide.shape
    scale = 2.0 * LOG2E / dimension
    target_norms = row_norms(wide[...]) * scale
    for row in range(0, rows, dimension):
        band = slice(row, row + dimension)
        source = tall[band]
        inner = dot(source, wide[...])
        own = lane_norms(source) if norms is None else norms[band]
        squares = jnp.tile(own, (1, rows // 128)) + target_norms
        yield band, jnp.exp2((2.0 * scale) * inner - squares).astype(BF16)


def self_kernel(tall, norms, wide, ordered, near_ref):
    for band, tile in bands(tall, norms, wide):
        near_ref[:, band] = dot(ordered[...], tile, NT)


def back_kernel(tall, norms, ordered, back_wide, back_ordered, marks, near, near_ref, held_ref):
    near_ref[...] = near[...]
    used = marked(marks[...], -2)

    @pl.when(used)
    def _():
        for band, tile in bands(tall, norms, back_wide):
            near_ref[:, band] += dot(back_ordered[...], tile, NT)
            part = dot(ordered[:, band], tile)
            if band.start:
                held_ref[...] += part
            else:
                held_ref[...] = part

    @pl.when(jnp.logical_not(used))
    def _():
        held_ref[...] = jnp.zeros_like(held_ref)


def pair_kernel(wide, ordered, side_tall, back_wide, back_ordered, marks, message, near, held,
                near_ref, back_ref, side_ref, sum_ref):
    dimension, rows = wide.shape
    sides = ordered.shape[0]
    odd = lax.rem(lax.axis_index("leaf"), 2)
    go_odd = jnp.logical_and(odd == 1, marked(message[message.shape[0] - PAD :], -1))
    go_even = jnp.logical_and(odd == 0, marked(marks[...], 1))

    def pair(other_wide, other_ordered):
        for band, tile in bands(side_tall, None, other_wide):
            side_ref[:, band] = dot(other_ordered[...], tile, NT).astype(BF16)
            first = rows + band.start // dimension * sides
            part = dot(side_tall[first : first + sides], tile)
            if band.start:
                sum_ref[...] += part
            else:
                sum_ref[...] = part

    @pl.when(go_odd)
    def _():
        pair(back_wide, back_ordered)
        back_ref[...] = (held[...] + sum_ref[...]).astype(BF16)
        near_ref[...] = near[...]

    @pl.when(go_even)
    def _():
        pair(wide, ordered)
        back_ref[...] = held[...].astype(BF16)
        near_ref[...] = near[...] + sum_ref[...]

    @pl.when(jnp.logical_not(jnp.logical_or(go_odd, go_even)))
    def _():
        back_ref[...] = held[...].astype(BF16)
        near_ref[...] = near[...]
        side_ref[...] = jnp.zeros_like(side_ref)


def far_kernel(others, own_top, potential, product, interp, near, *refs):
    tops, out_ref = refs[:others], refs[-1]
    sides = out_ref.shape[0]
    dimension = own_top.shape[0] - sides
    total = potential[...]
    above = None
    for top in tops:
        part = dot(
            top[dimension:].astype(F32),
            small_kernel(top[:dimension], own_top[:dimension]),
            NN,
            HIGHEST,
        )
        above = part if above is None else above + part
    if above is not None:
        total = total + dot(above, product[...], NN, HIGHEST)
    out_ref[...] = near[...] + dot_split(total, interp[...])


def total_kernel(here, back, side, out_ref):
    out_ref[...] = here[...] + (back[...].astype(F32) + side[...].astype(F32))


def call(kernel, outs, args, scratch=(), anywhere=False, flops=0, exps=0, name=None):
    vmem = pl.BlockSpec(memory_space=pltpu.VMEM)
    rest = pl.BlockSpec(memory_space=pl.ANY) if anywhere else vmem
    moved = 0 if anywhere or flops == 0 else sum(a.size * a.dtype.itemsize for a in list(args) + list(outs))
    return pl.pallas_call(
        kernel,
        out_shape=outs,
        in_specs=[rest] * len(args),
        out_specs=[rest if anywhere else vmem] * len(outs),
        scratch_shapes=list(scratch),
        compiler_params=pltpu.CompilerParams(
            vmem_limit_bytes=START_VMEM if anywhere else VMEM_LIMIT
        ),
        cost_estimate=pl.CostEstimate(flops=flops, bytes_accessed=moved, transcendentals=exps),
        name=name,
    )(*args)


def swapped(value, axis, flip):
    count = lax.axis_size(axis)
    return lax.ppermute(value, axis, [(place, place ^ flip) for place in range(count)])


def rotated(value, axis, turn):
    count = lax.axis_size(axis)
    return lax.ppermute(value, axis, [(place, (place + turn) % count) for place in range(count)])


def shifted(value, axis, step):
    places = range(lax.axis_size(axis))
    return lax.ppermute(
        value, axis, [(place, place + step) for place in places if place + step in places]
    )


def shape(dims, dtype):
    return jax.ShapeDtypeStruct(dims, dtype)


def local(points, charges, order, near_mask, skeletons, leaf_interp, transfer):
    dimension, rows = points.shape
    sides, count = charges.shape[0], leaf_interp.shape[0]
    leaves, groups = lax.axis_size("leaf"), lax.axis_size("grp")
    levels = leaves.bit_length() - 1
    skeletons = jnp.transpose(skeletons, (1, 0, 2))
    transfer = transfer[0]
    block_sums = shape((sides, rows), F32)
    block_values = shape((sides, rows), BF16)
    node_points = shape((dimension, count), BF16)
    node_sums = shape((sides, count), F32)
    tile_flops = 2 * rows * rows * (dimension + 2 * sides)

    back_points = rotated(points, "leaf", 2)

    inputs = [order.reshape(1, rows), skeletons, near_mask, charges, points, leaf_interp, transfer]
    made = [
        block_values,
        node_points,
        shape((PAD, count), BF16),
        shape((dimension + 2 * sides + PAD, count), BF16),
        node_sums,
    ]
    ordered, coords, marks, message, passed = call(
        start_kernel,
        made,
        inputs,
        scratch=[pltpu.VMEM(value.shape, value.dtype) for value in inputs + made]
        + [pltpu.SemaphoreType.DMA((len(inputs),)), pltpu.SemaphoreType.DMA((len(made),))],
        anywhere=True,
        name="start",
    )
    tall, norms = call(
        turn_kernel,
        [shape((rows + sides * rows // dimension, dimension), BF16), shape((rows, 128), F32)],
        [points, ordered],
        name="turn",
    )
    (near,) = call(
        self_kernel,
        [block_sums],
        [tall, norms, points, ordered],
        name="self_tile",
    )

    history, terms = [], []
    for level in range(levels):
        received = swapped(message, "leaf", 1 << level)
        if level == 0:
            received, near = lax.optimization_barrier((received, near))
            first_received = received
            side_tall = swapped(tall, "leaf", 1)
        if level == 1:
            received, back_points = lax.optimization_barrier((received, back_points))
        last = level == levels - 1
        if level and not last:
            made = call(
                functools.partial(term_kernel, sides, levels),
                [node_sums] + [shape((count, count), F32)] * (level == 1),
                [transfer] + history[-2:],
                flops=8 * dimension * count * count,
                name="sibling_term",
            )
            terms.append(made[0])
            if level == 1:
                product = made[1]
            passed = lax.optimization_barrier((passed, made[0]))[0]
        history += [coords, received]
        if level == levels - 2:
            near, held = call(
                back_kernel,
                [block_sums, block_sums],
                [tall, norms, ordered, back_points, back_ordered, marks]
                + [lax.optimization_barrier((near, passed))[0]],
                flops=tile_flops,
                exps=rows * rows,
                name="back_tile",
            )
            passed, held = lax.optimization_barrier((passed, held))
        if last:
            near, back, side = call(
                pair_kernel,
                [block_sums, block_values, block_values],
                [points, ordered, side_tall, back_points, back_ordered, marks, first_received]
                + [lax.optimization_barrier((near, passed))[0], held],
                scratch=[pltpu.VMEM((sides, rows), F32)],
                flops=tile_flops,
                exps=rows * rows,
                name="pair_tile",
            )
            passed, near = lax.optimization_barrier((passed, near))
            back = rotated(back, "leaf", -2)
            side = swapped(side, "leaf", 1)
        if last:
            outs = [shape((dimension + sides, count), BF16)]
        else:
            outs = [node_points, shape((dimension + 2 * sides, count), BF16), node_sums]
        results = call(
            functools.partial(round_kernel, level, last),
            outs,
            [skeletons, transfer, coords, passed, received],
            flops=(JOIN_FLOPS if level < 2 else 8) * dimension * count * count,
            name="join_level",
        )
        if not last:
            coords, message, passed = results
        if level == 0:
            sent = lax.optimization_barrier((ordered, results[-1]))[0]
            back_ordered = shifted(sent, "leaf", 2)
    own_top = results[0]
    tops = [rotated(own_top, "grp", turn) for turn in range(1, groups)]
    (potential,) = call(
        functools.partial(last_terms_kernel, sides, levels),
        [node_sums],
        [transfer] + history[-4:] + terms,
        flops=8 * dimension * count * count,
        exps=count * count,
        name="last_terms",
    )
    (here,) = call(
        functools.partial(far_kernel, len(tops)),
        [block_sums],
        [own_top, potential, product, leaf_interp, near] + tops,
        flops=4 * sides * rows * count,
        name="far_field",
    )
    (out,) = call(total_kernel, [block_sums], [here, back, side], flops=2 * sides * rows, name="total")
    return out


def solution(mesh):
    in_specs = (
        P(None, ("leaf", "grp")),
        P(None, ("leaf", "grp")),
        P(("leaf", "grp")),
        P(("leaf", "grp"), None),
        P(("leaf", "grp"), None, None),
        P(None, ("leaf", "grp")),
        P(("leaf", "grp"), None, None, None),
    )
    out_specs = P(None, ("leaf", "grp"))
    return jax.shard_map(local, mesh=mesh, in_specs=in_specs, out_specs=out_specs, check_vma=False)
```

```python
import functools

import jax
import jax.numpy as jnp
from jax import lax
from jax.experimental import pallas as pl
from jax.experimental.pallas import tpu as pltpu
from jax.sharding import PartitionSpec as P

REACH = 2
BF16 = jnp.bfloat16
F32 = jnp.float32
LOG2E = 1.4426950408889634
HIGHEST = lax.Precision.HIGHEST
PAD = 16
JOIN_FLOPS = 500
VMEM_LIMIT = 40 * 1024 * 1024
START_VMEM = 56 * 1024 * 1024

NN = ((1,), (0,))
NT = ((1,), (1,))
TN = ((0,), (0,))


def dot(left, right, contract=NN, precision=None):
    return lax.dot_general(
        left, right, (contract, ((), ())), preferred_element_type=F32, precision=precision
    )


def halves(value):
    high = value.astype(BF16)
    return high, (value - high.astype(F32)).astype(BF16)


def dot_split(left, right, contract=NN):
    rows = left.shape[0]
    both = dot(jnp.concatenate(halves(left), axis=0), right, contract)
    return both[:rows] + both[rows:]


def row_norms(points):
    wide = points.astype(F32)
    return jnp.sum(wide * wide, axis=0, keepdims=True)


def column_norms(points):
    wide = points.astype(F32)
    high, low = halves(wide * wide)
    ones = jnp.ones((points.shape[0], 128), BF16)
    return dot(high, ones, TN) + dot(low, ones, TN)


def one_hot(index, rows, first):
    place = lax.broadcasted_iota(jnp.int32, (rows, index.shape[1]), 0) + first
    return jnp.where(place == index, 1.0, 0.0).astype(BF16)


def small_kernel(source, target):
    scale = 2.0 * LOG2E / source.shape[0]
    inner = dot(source, target, TN)
    squares = column_norms(source)[:, : target.shape[1]] + row_norms(target)
    return jnp.exp2(scale * (2.0 * inner - squares))


def pick(first, second, index, bit):
    count = first.shape[1]
    table = jnp.concatenate(
        [one_hot(index, count, count * bit), one_hot(index, count, count * (1 - bit))], axis=0
    )
    return dot(jnp.concatenate([first, second], axis=1), table).astype(BF16)


def write_message(weights, coords, matrix, message_ref, passed_ref):
    dimension, sides = coords.shape[0], weights.shape[0]
    passed = dot_split(weights, matrix, NT)
    message_ref[:dimension] = coords
    message_ref[dimension : dimension + sides] = weights.astype(BF16)
    message_ref[dimension + sides : dimension + 2 * sides] = passed.astype(BF16)
    passed_ref[...] = passed


def start_kernel(*refs):
    inputs, outs, held = refs[:7], refs[7:12], refs[12:19]
    made, sems, out_sems = refs[19:24], refs[24], refs[25]
    copies = [
        pltpu.make_async_copy(source, target, sems.at[number])
        for number, (source, target) in enumerate(zip(inputs, held))
    ]
    for copy in copies:
        copy.start()
    stores = [
        pltpu.make_async_copy(source, target, out_sems.at[number])
        for number, (source, target) in enumerate(zip(made, outs))
    ]
    order, skeletons, mask, charges, points, interp, transfer = held
    ordered_ref, coords_ref, marks_ref, message_ref, passed_ref = made
    dimension, rows = points.shape
    sides, count = passed_ref.shape
    for copy in copies[:4]:
        copy.wait()
    width = rows // 4
    for column in range(0, rows, width):
        table = one_hot(order[:, column : column + width], rows, 0)
        ordered_ref[:, column : column + width] = dot(charges[...], table).astype(BF16)
    stores[0].start()
    copies[4].wait()
    coords = dot(points[...], one_hot(skeletons[0], rows, 0)).astype(BF16)
    coords_ref[...] = coords
    stores[1].start()
    lane = lax.broadcasted_iota(jnp.int32, (1, count), 1)
    pattern = jnp.zeros((1, count), jnp.int32)
    for offset in range(mask.shape[1]):
        pattern = jnp.where(lane == offset, mask[:, offset : offset + 1], pattern)
    marks = jnp.broadcast_to(pattern.astype(F32), (PAD, count)).astype(BF16)
    marks_ref[...] = marks
    message_ref[dimension + 2 * sides :] = marks
    stores[2].start()
    copies[5].wait()
    weights = dot(ordered_ref[...], interp[...], NT)
    copies[6].wait()
    write_message(weights, coords, transfer[0], message_ref, passed_ref)
    stores[3].start()
    stores[4].start()
    for store in stores:
        store.wait()


def marked(marks, offset):
    rows = marks.astype(F32)
    lane = lax.broadcasted_iota(jnp.int32, rows.shape, 1)
    return jnp.max(jnp.where(lane == REACH + offset, rows, 0.0)) > 0.5


def round_kernel(level, last, skeletons, transfer, coords, passed, message, *outs):
    dimension = coords.shape[0]
    sides = passed.shape[0]
    bit = (lax.axis_index("leaf") >> level) & 1
    joined = pick(coords[...], message[:dimension], skeletons[level + 1], bit)
    span = slice(dimension + sides, dimension + 2 * sides)
    weights = passed[...] + message[span].astype(F32)
    if last:
        outs[0][:dimension] = joined
        outs[0][dimension:] = weights.astype(BF16)
        return
    outs[0][...] = joined
    write_message(weights, joined, transfer[level + 1], outs[1], outs[2])


def sibling_term(coords, message, sides):
    dimension = coords.shape[0]
    weights = message[dimension : dimension + sides].astype(F32)
    return dot(weights, small_kernel(message[:dimension], coords[...]), NN, HIGHEST)


def term_kernel(sides, levels, transfer, coords, message, term_ref, *product_ref):
    term_ref[...] = sibling_term(coords, message, sides)
    if product_ref:
        product = transfer[levels - 1].astype(F32)
        for level in range(levels - 2, -1, -1):
            product = dot(product, transfer[level].astype(F32), NN, HIGHEST)
        product_ref[0][...] = product


def last_terms_kernel(sides, levels, transfer, *refs):
    pairs, terms, potential_ref = refs[:4], refs[4:-1], refs[-1]
    late = [sibling_term(pairs[0], pairs[1], sides), sibling_term(pairs[2], pairs[3], sides)]
    terms = [ref[...] for ref in terms] + late
    potential = terms[-1]
    for level in range(levels - 2, -1, -1):
        potential = dot_split(potential, transfer[level]) + terms[level]
    potential_ref[...] = potential


def lane_norms(tall):
    square = jnp.square(tall.astype(F32))
    norms = jnp.sum(square, axis=1, keepdims=True) * (2.0 * LOG2E / tall.shape[1])
    return jnp.broadcast_to(norms, (tall.shape[0], 128))


def turn_kernel(points, ordered, tall_ref, norms_ref):
    dimension, rows = points.shape
    sides = ordered.shape[0]
    tall_ref[:rows] = jnp.transpose(points[...])
    norms_ref[...] = lane_norms(tall_ref[:rows])
    for number in range(rows // dimension):
        first = rows + number * sides
        tall_ref[first : first + sides] = ordered[:, number * dimension : (number + 1) * dimension]


def bands(tall, norms, wide):
    dimension, rows = wide.shape
    scale = 2.0 * LOG2E / dimension
    target_norms = row_norms(wide[...]) * scale
    for row in range(0, rows, dimension):
        band = slice(row, row + dimension)
        source = tall[band]
        inner = dot(source, wide[...])
        own = lane_norms(source) if norms is None else norms[band]
        squares = jnp.tile(own, (1, rows // 128)) + target_norms
        yield band, jnp.exp2((2.0 * scale) * inner - squares).astype(BF16)


def self_kernel(tall, norms, wide, ordered, near_ref):
    for band, tile in bands(tall, norms, wide):
        near_ref[:, band] = dot(ordered[...], tile, NT)


def near_kernel(tall, norms, wide, ordered, side_tall, back_wide, back_ordered, marks, message,
                near, near_ref, back_ref, side_ref, held):
    dimension, rows = wide.shape
    sides = ordered.shape[0]
    odd = lax.rem(lax.axis_index("leaf"), 2)
    with_back = marked(marks[...], -2)
    go_odd = jnp.logical_and(odd == 1, marked(message[message.shape[0] - PAD :], -1))
    go_even = jnp.logical_and(odd == 0, marked(marks[...], 1))
    near_ref[...] = near[...]

    @pl.when(with_back)
    def _():
        for band, tile in bands(tall, norms, back_wide):
            near_ref[:, band] += dot(back_ordered[...], tile, NT)
            part = dot(ordered[:, band], tile)
            if band.start:
                held[...] += part
            else:
                held[...] = part

    @pl.when(jnp.logical_not(with_back))
    def _():
        held[...] = jnp.zeros_like(held)

    def pair(other_wide, other_ordered, sum_ref):
        for band, tile in bands(side_tall, None, other_wide):
            side_ref[:, band] = dot(other_ordered[...], tile, NT).astype(BF16)
            first = rows + band.start // dimension * sides
            sum_ref[...] += dot(side_tall[first : first + sides], tile)

    @pl.when(go_odd)
    def _():
        pair(back_wide, back_ordered, held)

    @pl.when(go_even)
    def _():
        pair(wide, ordered, near_ref)

    @pl.when(jnp.logical_not(jnp.logical_or(go_odd, go_even)))
    def _():
        side_ref[...] = jnp.zeros_like(side_ref)

    back_ref[...] = held[...].astype(BF16)


def far_kernel(others, own_top, potential, product, interp, near, *refs):
    tops, out_ref = refs[:others], refs[-1]
    sides = out_ref.shape[0]
    dimension = own_top.shape[0] - sides
    total = potential[...]
    above = None
    for top in tops:
        part = dot(
            top[dimension:].astype(F32),
            small_kernel(top[:dimension], own_top[:dimension]),
            NN,
            HIGHEST,
        )
        above = part if above is None else above + part
    if above is not None:
        total = total + dot(above, product[...], NN, HIGHEST)
    out_ref[...] = near[...] + dot_split(total, interp[...])


def total_kernel(here, back, side, out_ref):
    out_ref[...] = here[...] + (back[...].astype(F32) + side[...].astype(F32))


def call(kernel, outs, args, scratch=(), anywhere=False, flops=0, exps=0, name=None):
    vmem = pl.BlockSpec(memory_space=pltpu.VMEM)
    rest = pl.BlockSpec(memory_space=pl.ANY) if anywhere else vmem
    moved = 0 if anywhere or flops == 0 else sum(a.size * a.dtype.itemsize for a in list(args) + list(outs))
    return pl.pallas_call(
        kernel,
        out_shape=outs,
        in_specs=[rest] * len(args),
        out_specs=[rest if anywhere else vmem] * len(outs),
        scratch_shapes=list(scratch),
        compiler_params=pltpu.CompilerParams(
            vmem_limit_bytes=START_VMEM if anywhere else VMEM_LIMIT
        ),
        cost_estimate=pl.CostEstimate(flops=flops, bytes_accessed=moved, transcendentals=exps),
        name=name,
    )(*args)


def swapped(value, axis, flip):
    count = lax.axis_size(axis)
    return lax.ppermute(value, axis, [(place, place ^ flip) for place in range(count)])


def rotated(value, axis, turn):
    count = lax.axis_size(axis)
    return lax.ppermute(value, axis, [(place, (place + turn) % count) for place in range(count)])


def shifted(value, axis, step):
    places = range(lax.axis_size(axis))
    return lax.ppermute(
        value, axis, [(place, place + step) for place in places if place + step in places]
    )


def shape(dims, dtype):
    return jax.ShapeDtypeStruct(dims, dtype)


def local(points, charges, order, near_mask, skeletons, leaf_interp, transfer):
    dimension, rows = points.shape
    sides, count = charges.shape[0], leaf_interp.shape[0]
    leaves, groups = lax.axis_size("leaf"), lax.axis_size("grp")
    levels = leaves.bit_length() - 1
    skeletons = jnp.transpose(skeletons, (1, 0, 2))
    transfer = transfer[0]
    block_sums = shape((sides, rows), F32)
    block_values = shape((sides, rows), BF16)
    node_points = shape((dimension, count), BF16)
    node_sums = shape((sides, count), F32)
    tile_flops = 2 * rows * rows * (dimension + 2 * sides)

    back_points = rotated(points, "leaf", 2)

    inputs = [order.reshape(1, rows), skeletons, near_mask, charges, points, leaf_interp, transfer]
    made = [
        block_values,
        node_points,
        shape((PAD, count), BF16),
        shape((dimension + 2 * sides + PAD, count), BF16),
        node_sums,
    ]
    ordered, coords, marks, message, passed = call(
        start_kernel,
        made,
        inputs,
        scratch=[pltpu.VMEM(value.shape, value.dtype) for value in inputs + made]
        + [pltpu.SemaphoreType.DMA((len(inputs),)), pltpu.SemaphoreType.DMA((len(made),))],
        anywhere=True,
        name="start",
    )
    tall, norms = call(
        turn_kernel,
        [shape((rows + sides * rows // dimension, dimension), BF16), shape((rows, 128), F32)],
        [points, ordered],
        name="turn",
    )
    (near,) = call(
        self_kernel,
        [block_sums],
        [tall, norms, points, ordered],
        name="self_tile",
    )

    history, terms = [], []
    for level in range(levels):
        received = swapped(message, "leaf", 1 << level)
        if level == 0:
            received, near = lax.optimization_barrier((received, near))
            first_received = received
            side_tall = swapped(tall, "leaf", 1)
        if level == 1:
            received, back_points = lax.optimization_barrier((received, back_points))
        last = level == levels - 1
        if level and not last:
            made = call(
                functools.partial(term_kernel, sides, levels),
                [node_sums] + [shape((count, count), F32)] * (level == 1),
                [transfer] + history[-2:],
                flops=8 * dimension * count * count,
                name="sibling_term",
            )
            terms.append(made[0])
            if level == 1:
                product = made[1]
                passed = lax.optimization_barrier((passed, made[0]))[0]
        history += [coords, received]
        if last:
            near, back, side = call(
                near_kernel,
                [block_sums, block_values, block_values],
                [tall, norms, points, ordered, side_tall, back_points, back_ordered]
                + [marks, first_received, lax.optimization_barrier((near, passed))[0]],
                scratch=[pltpu.VMEM((sides, rows), F32)],
                flops=2 * tile_flops,
                exps=2 * rows * rows,
                name="near_tiles",
            )
            passed, near, terms = lax.optimization_barrier((passed, near, terms))
            back = rotated(back, "leaf", -2)
            side = swapped(side, "leaf", 1)
        if last:
            outs = [shape((dimension + sides, count), BF16)]
        else:
            outs = [node_points, shape((dimension + 2 * sides, count), BF16), node_sums]
        results = call(
            functools.partial(round_kernel, level, last),
            outs,
            [skeletons, transfer, coords, passed, received],
            flops=JOIN_FLOPS * dimension * count * count,
            name="join_level",
        )
        if not last:
            coords, message, passed = results
        if level == min(1, levels - 1):
            sent = lax.optimization_barrier((ordered, results[-1]))[0]
            back_ordered = shifted(sent, "leaf", 2)
    own_top = results[0]
    tops = [rotated(own_top, "grp", turn) for turn in range(1, groups)]
    (potential,) = call(
        functools.partial(last_terms_kernel, sides, levels),
        [node_sums],
        [transfer] + history[-4:] + terms,
        flops=8 * dimension * count * count,
        exps=count * count,
        name="last_terms",
    )
    (here,) = call(
        functools.partial(far_kernel, len(tops)),
        [block_sums],
        [own_top, potential, product, leaf_interp, near] + tops,
        flops=4 * sides * rows * count,
        name="far_field",
    )
    (out,) = call(total_kernel, [block_sums], [here, back, side], flops=2 * sides * rows, name="total")
    return out


def solution(mesh):
    in_specs = (
        P(None, ("leaf", "grp")),
        P(None, ("leaf", "grp")),
        P(("leaf", "grp")),
        P(("leaf", "grp"), None),
        P(("leaf", "grp"), None, None),
        P(None, ("leaf", "grp")),
        P(("leaf", "grp"), None, None, None),
    )
    out_specs = P(None, ("leaf", "grp"))
    return jax.shard_map(local, mesh=mesh, in_specs=in_specs, out_specs=out_specs, check_vma=False)
```

```python
import functools

import jax
import jax.numpy as jnp
from jax import lax
from jax.experimental import pallas as pl
from jax.experimental.pallas import tpu as pltpu
from jax.sharding import PartitionSpec as P

REACH = 2
BF16 = jnp.bfloat16
F32 = jnp.float32
LOG2E = 1.4426950408889634
HIGHEST = lax.Precision.HIGHEST
PAD = 16
JOIN_FLOPS = 500
VMEM_LIMIT = 40 * 1024 * 1024
START_VMEM = 56 * 1024 * 1024

NN = ((1,), (0,))
NT = ((1,), (1,))
TN = ((0,), (0,))


def dot(left, right, contract=NN, precision=None):
    return lax.dot_general(
        left, right, (contract, ((), ())), preferred_element_type=F32, precision=precision
    )


def halves(value):
    high = value.astype(BF16)
    return high, (value - high.astype(F32)).astype(BF16)


def dot_split(left, right, contract=NN):
    rows = left.shape[0]
    both = dot(jnp.concatenate(halves(left), axis=0), right, contract)
    return both[:rows] + both[rows:]


def row_norms(points):
    wide = points.astype(F32)
    return jnp.sum(wide * wide, axis=0, keepdims=True)


def column_norms(points):
    wide = points.astype(F32)
    high, low = halves(wide * wide)
    ones = jnp.ones((points.shape[0], 128), BF16)
    return dot(high, ones, TN) + dot(low, ones, TN)


def one_hot(index, rows, first):
    place = lax.broadcasted_iota(jnp.int32, (rows, index.shape[1]), 0) + first
    return jnp.where(place == index, 1.0, 0.0).astype(BF16)


def small_kernel(source, target):
    scale = 2.0 * LOG2E / source.shape[0]
    inner = dot(source, target, TN)
    squares = column_norms(source)[:, : target.shape[1]] + row_norms(target)
    return jnp.exp2(scale * (2.0 * inner - squares))


def pick(first, second, index, bit):
    count = first.shape[1]
    table = jnp.concatenate(
        [one_hot(index, count, count * bit), one_hot(index, count, count * (1 - bit))], axis=0
    )
    return dot(jnp.concatenate([first, second], axis=1), table).astype(BF16)


def write_message(weights, coords, matrix, message_ref, passed_ref):
    dimension, sides = coords.shape[0], weights.shape[0]
    passed = dot_split(weights, matrix, NT)
    message_ref[:dimension] = coords
    message_ref[dimension : dimension + sides] = weights.astype(BF16)
    message_ref[dimension + sides : dimension + 2 * sides] = passed.astype(BF16)
    passed_ref[...] = passed


def start_kernel(*refs):
    inputs, outs, held = refs[:7], refs[7:12], refs[12:19]
    made, sems, out_sems = refs[19:24], refs[24], refs[25]
    copies = [
        pltpu.make_async_copy(source, target, sems.at[number])
        for number, (source, target) in enumerate(zip(inputs, held))
    ]
    for copy in copies:
        copy.start()
    stores = [
        pltpu.make_async_copy(source, target, out_sems.at[number])
        for number, (source, target) in enumerate(zip(made, outs))
    ]
    order, skeletons, mask, charges, points, interp, transfer = held
    ordered_ref, coords_ref, marks_ref, message_ref, passed_ref = made
    dimension, rows = points.shape
    sides, count = passed_ref.shape
    for copy in copies[:4]:
        copy.wait()
    width = rows // 4
    for column in range(0, rows, width):
        table = one_hot(order[:, column : column + width], rows, 0)
        ordered_ref[:, column : column + width] = dot(charges[...], table).astype(BF16)
    stores[0].start()
    copies[4].wait()
    coords = dot(points[...], one_hot(skeletons[0], rows, 0)).astype(BF16)
    coords_ref[...] = coords
    stores[1].start()
    lane = lax.broadcasted_iota(jnp.int32, (1, count), 1)
    pattern = jnp.zeros((1, count), jnp.int32)
    for offset in range(mask.shape[1]):
        pattern = jnp.where(lane == offset, mask[:, offset : offset + 1], pattern)
    marks = jnp.broadcast_to(pattern.astype(F32), (PAD, count)).astype(BF16)
    marks_ref[...] = marks
    message_ref[dimension + 2 * sides :] = marks
    stores[2].start()
    copies[5].wait()
    weights = dot(ordered_ref[...], interp[...], NT)
    copies[6].wait()
    write_message(weights, coords, transfer[0], message_ref, passed_ref)
    stores[3].start()
    stores[4].start()
    for store in stores:
        store.wait()


def marked(marks, offset):
    rows = marks.astype(F32)
    lane = lax.broadcasted_iota(jnp.int32, rows.shape, 1)
    return jnp.max(jnp.where(lane == REACH + offset, rows, 0.0)) > 0.5


def round_kernel(level, last, skeletons, transfer, coords, passed, message, *outs):
    dimension = coords.shape[0]
    sides = passed.shape[0]
    bit = (lax.axis_index("leaf") >> level) & 1
    joined = pick(coords[...], message[:dimension], skeletons[level + 1], bit)
    span = slice(dimension + sides, dimension + 2 * sides)
    weights = passed[...] + message[span].astype(F32)
    if last:
        outs[0][:dimension] = joined
        outs[0][dimension:] = weights.astype(BF16)
        return
    outs[0][...] = joined
    write_message(weights, joined, transfer[level + 1], outs[1], outs[2])


def sibling_term(coords, message, sides):
    dimension = coords.shape[0]
    weights = message[dimension : dimension + sides].astype(F32)
    return dot(weights, small_kernel(message[:dimension], coords[...]), NN, HIGHEST)


def term_kernel(sides, levels, transfer, coords, message, term_ref, *product_ref):
    term_ref[...] = sibling_term(coords, message, sides)
    if product_ref:
        product = transfer[levels - 1].astype(F32)
        for level in range(levels - 2, -1, -1):
            product = dot(product, transfer[level].astype(F32), NN, HIGHEST)
        product_ref[0][...] = product


def last_terms_kernel(sides, levels, transfer, *refs):
    pairs, terms, potential_ref = refs[:4], refs[4:-1], refs[-1]
    late = [sibling_term(pairs[0], pairs[1], sides), sibling_term(pairs[2], pairs[3], sides)]
    terms = [ref[...] for ref in terms] + late
    potential = terms[-1]
    for level in range(levels - 2, -1, -1):
        potential = dot_split(potential, transfer[level]) + terms[level]
    potential_ref[...] = potential


def lane_norms(tall):
    square = jnp.square(tall.astype(F32))
    norms = jnp.sum(square, axis=1, keepdims=True) * (2.0 * LOG2E / tall.shape[1])
    return jnp.broadcast_to(norms, (tall.shape[0], 128))


def turn_kernel(points, ordered, tall_ref, norms_ref):
    dimension, rows = points.shape
    sides = ordered.shape[0]
    tall_ref[:rows] = jnp.transpose(points[...])
    norms_ref[...] = lane_norms(tall_ref[:rows])
    for number in range(rows // dimension):
        first = rows + number * sides
        tall_ref[first : first + sides] = ordered[:, number * dimension : (number + 1) * dimension]


def bands(tall, norms, wide):
    dimension, rows = wide.shape
    scale = 2.0 * LOG2E / dimension
    target_norms = row_norms(wide[...]) * scale
    for row in range(0, rows, dimension):
        band = slice(row, row + dimension)
        source = tall[band]
        inner = dot(source, wide[...])
        own = lane_norms(source) if norms is None else norms[band]
        squares = jnp.tile(own, (1, rows // 128)) + target_norms
        yield band, jnp.exp2((2.0 * scale) * inner - squares).astype(BF16)


def self_kernel(tall, norms, wide, ordered, near_ref):
    for band, tile in bands(tall, norms, wide):
        near_ref[:, band] = dot(ordered[...], tile, NT)


def back_kernel(tall, norms, ordered, back_wide, back_ordered, marks, near, near_ref, held_ref):
    near_ref[...] = near[...]
    used = marked(marks[...], -2)

    @pl.when(used)
    def _():
        for band, tile in bands(tall, norms, back_wide):
            near_ref[:, band] += dot(back_ordered[...], tile, NT)
            part = dot(ordered[:, band], tile)
            if band.start:
                held_ref[...] += part
            else:
                held_ref[...] = part

    @pl.when(jnp.logical_not(used))
    def _():
        held_ref[...] = jnp.zeros_like(held_ref)


def pair_kernel(wide, ordered, side_tall, back_wide, back_ordered, marks, message, near, held,
                near_ref, back_ref, side_ref, sum_ref):
    dimension, rows = wide.shape
    sides = ordered.shape[0]
    odd = lax.rem(lax.axis_index("leaf"), 2)
    go_odd = jnp.logical_and(odd == 1, marked(message[message.shape[0] - PAD :], -1))
    go_even = jnp.logical_and(odd == 0, marked(marks[...], 1))

    def pair(other_wide, other_ordered):
        for band, tile in bands(side_tall, None, other_wide):
            side_ref[:, band] = dot(other_ordered[...], tile, NT).astype(BF16)
            first = rows + band.start // dimension * sides
            part = dot(side_tall[first : first + sides], tile)
            if band.start:
                sum_ref[...] += part
            else:
                sum_ref[...] = part

    @pl.when(go_odd)
    def _():
        pair(back_wide, back_ordered)
        back_ref[...] = (held[...] + sum_ref[...]).astype(BF16)
        near_ref[...] = near[...]

    @pl.when(go_even)
    def _():
        pair(wide, ordered)
        back_ref[...] = held[...].astype(BF16)
        near_ref[...] = near[...] + sum_ref[...]

    @pl.when(jnp.logical_not(jnp.logical_or(go_odd, go_even)))
    def _():
        back_ref[...] = held[...].astype(BF16)
        near_ref[...] = near[...]
        side_ref[...] = jnp.zeros_like(side_ref)


def far_kernel(others, own_top, potential, product, interp, near, *refs):
    tops, out_ref = refs[:others], refs[-1]
    sides = out_ref.shape[0]
    dimension = own_top.shape[0] - sides
    total = potential[...]
    above = None
    for top in tops:
        part = dot(
            top[dimension:].astype(F32),
            small_kernel(top[:dimension], own_top[:dimension]),
            NN,
            HIGHEST,
        )
        above = part if above is None else above + part
    if above is not None:
        total = total + dot(above, product[...], NN, HIGHEST)
    out_ref[...] = near[...] + dot_split(total, interp[...])


def total_kernel(here, back, side, out_ref):
    out_ref[...] = here[...] + (back[...].astype(F32) + side[...].astype(F32))


def call(kernel, outs, args, scratch=(), anywhere=False, flops=0, exps=0, name=None):
    vmem = pl.BlockSpec(memory_space=pltpu.VMEM)
    rest = pl.BlockSpec(memory_space=pl.ANY) if anywhere else vmem
    moved = 0 if anywhere or flops == 0 else sum(a.size * a.dtype.itemsize for a in list(args) + list(outs))
    return pl.pallas_call(
        kernel,
        out_shape=outs,
        in_specs=[rest] * len(args),
        out_specs=[rest if anywhere else vmem] * len(outs),
        scratch_shapes=list(scratch),
        compiler_params=pltpu.CompilerParams(
            vmem_limit_bytes=START_VMEM if anywhere else VMEM_LIMIT
        ),
        cost_estimate=pl.CostEstimate(flops=flops, bytes_accessed=moved, transcendentals=exps),
        name=name,
    )(*args)


def swapped(value, axis, flip):
    count = lax.axis_size(axis)
    return lax.ppermute(value, axis, [(place, place ^ flip) for place in range(count)])


def rotated(value, axis, turn):
    count = lax.axis_size(axis)
    return lax.ppermute(value, axis, [(place, (place + turn) % count) for place in range(count)])


def shifted(value, axis, step):
    places = range(lax.axis_size(axis))
    return lax.ppermute(
        value, axis, [(place, place + step) for place in places if place + step in places]
    )


def shape(dims, dtype):
    return jax.ShapeDtypeStruct(dims, dtype)


def local(points, charges, order, near_mask, skeletons, leaf_interp, transfer):
    dimension, rows = points.shape
    sides, count = charges.shape[0], leaf_interp.shape[0]
    leaves, groups = lax.axis_size("leaf"), lax.axis_size("grp")
    levels = leaves.bit_length() - 1
    skeletons = jnp.transpose(skeletons, (1, 0, 2))
    transfer = transfer[0]
    block_sums = shape((sides, rows), F32)
    block_values = shape((sides, rows), BF16)
    node_points = shape((dimension, count), BF16)
    node_sums = shape((sides, count), F32)
    tile_flops = 2 * rows * rows * (dimension + 2 * sides)

    back_points = rotated(points, "leaf", 2)

    inputs = [order.reshape(1, rows), skeletons, near_mask, charges, points, leaf_interp, transfer]
    made = [
        block_values,
        node_points,
        shape((PAD, count), BF16),
        shape((dimension + 2 * sides + PAD, count), BF16),
        node_sums,
    ]
    ordered, coords, marks, message, passed = call(
        start_kernel,
        made,
        inputs,
        scratch=[pltpu.VMEM(value.shape, value.dtype) for value in inputs + made]
        + [pltpu.SemaphoreType.DMA((len(inputs),)), pltpu.SemaphoreType.DMA((len(made),))],
        anywhere=True,
        name="start",
    )
    tall, norms = call(
        turn_kernel,
        [shape((rows + sides * rows // dimension, dimension), BF16), shape((rows, 128), F32)],
        [points, ordered],
        name="turn",
    )
    history, terms = [], []
    for level in range(levels):
        received = swapped(message, "leaf", 1 << level)
        if level == 0:
            first_received = received
            side_tall = swapped(tall, "leaf", 1)
        if level == 1:
            received, back_points = lax.optimization_barrier((received, back_points))
        last = level == levels - 1
        if level and not last:
            made = call(
                functools.partial(term_kernel, sides, levels),
                [node_sums] + [shape((count, count), F32)] * (level == 1),
                [transfer] + history[-2:],
                flops=8 * dimension * count * count,
                name="sibling_term",
            )
            terms.append(made[0])
            if level == 1:
                product = made[1]
            passed = lax.optimization_barrier((passed, made[0]))[0]
        history += [coords, received]
        if level == levels - 2:
            near, held = call(
                back_kernel,
                [block_sums, block_sums],
                [tall, norms, ordered, back_points, back_ordered, marks]
                + [lax.optimization_barrier((near, passed))[0]],
                flops=tile_flops,
                exps=rows * rows,
                name="back_tile",
            )
            passed, held = lax.optimization_barrier((passed, held))
        if last:
            near, back, side = call(
                pair_kernel,
                [block_sums, block_values, block_values],
                [points, ordered, side_tall, back_points, back_ordered, marks, first_received]
                + [lax.optimization_barrier((near, passed))[0], held],
                scratch=[pltpu.VMEM((sides, rows), F32)],
                flops=tile_flops,
                exps=rows * rows,
                name="pair_tile",
            )
            passed, near = lax.optimization_barrier((passed, near))
            back = rotated(back, "leaf", -2)
            side = swapped(side, "leaf", 1)
        if last:
            outs = [shape((dimension + sides, count), BF16)]
        else:
            outs = [node_points, shape((dimension + 2 * sides, count), BF16), node_sums]
        results = call(
            functools.partial(round_kernel, level, last),
            outs,
            [skeletons, transfer, coords, passed, received],
            flops=(JOIN_FLOPS if level < 2 else 8) * dimension * count * count,
            name="join_level",
        )
        if not last:
            coords, message, passed = results
        if level == 0:
            (near,) = call(
                self_kernel,
                [block_sums],
                [tall, norms, points, lax.optimization_barrier((ordered, results[-1]))[0]],
                name="self_tile",
            )
            sent = lax.optimization_barrier((ordered, near))[0]
            back_ordered = shifted(sent, "leaf", 2)
    own_top = results[0]
    tops = [rotated(own_top, "grp", turn) for turn in range(1, groups)]
    (potential,) = call(
        functools.partial(last_terms_kernel, sides, levels),
        [node_sums],
        [transfer] + history[-4:] + terms,
        flops=8 * dimension * count * count,
        exps=count * count,
        name="last_terms",
    )
    (here,) = call(
        functools.partial(far_kernel, len(tops)),
        [block_sums],
        [own_top, potential, product, leaf_interp, near] + tops,
        flops=4 * sides * rows * count,
        name="far_field",
    )
    (out,) = call(total_kernel, [block_sums], [here, back, side], flops=2 * sides * rows, name="total")
    return out


def solution(mesh):
    in_specs = (
        P(None, ("leaf", "grp")),
        P(None, ("leaf", "grp")),
        P(("leaf", "grp")),
        P(("leaf", "grp"), None),
        P(("leaf", "grp"), None, None),
        P(None, ("leaf", "grp")),
        P(("leaf", "grp"), None, None, None),
    )
    out_specs = P(None, ("leaf", "grp"))
    return jax.shard_map(local, mesh=mesh, in_specs=in_specs, out_specs=out_specs, check_vma=False)
```

```python
import functools

import jax
import jax.numpy as jnp
from jax import lax
from jax.experimental import pallas as pl
from jax.experimental.pallas import tpu as pltpu
from jax.sharding import PartitionSpec as P

REACH = 2
BF16 = jnp.bfloat16
F32 = jnp.float32
LOG2E = 1.4426950408889634
PAD = 16
JOIN_FLOPS = 500
VMEM_LIMIT = 40 * 1024 * 1024
START_VMEM = 56 * 1024 * 1024

NN = ((1,), (0,))
NT = ((1,), (1,))
TN = ((0,), (0,))


def dot(left, right, contract=NN, precision=None):
    return lax.dot_general(
        left, right, (contract, ((), ())), preferred_element_type=F32, precision=precision
    )


def halves(value):
    high = value.astype(BF16)
    return high, (value - high.astype(F32)).astype(BF16)


def dot_split(left, right, contract=NN):
    rows = left.shape[0]
    both = dot(jnp.concatenate(halves(left), axis=0), right, contract)
    return both[:rows] + both[rows:]


def dot_parts(left, right):
    rows, columns = left.shape[0], right.shape[1]
    if left.dtype != BF16:
        left = jnp.concatenate(halves(left), axis=0)
    both = dot(left, jnp.concatenate(halves(right), axis=1))
    total = both[:rows, :columns] + both[:rows, columns:]
    if left.shape[0] > rows:
        total = total + (both[rows:, :columns] + both[rows:, columns:])
    return total


def row_norms(points):
    wide = points.astype(F32)
    return jnp.sum(wide * wide, axis=0, keepdims=True)


def column_norms(points):
    wide = points.astype(F32)
    high, low = halves(wide * wide)
    ones = jnp.ones((points.shape[0], 128), BF16)
    return dot(high, ones, TN) + dot(low, ones, TN)


def one_hot(index, rows, first):
    place = lax.broadcasted_iota(jnp.int32, (rows, index.shape[1]), 0) + first
    return jnp.where(place == index, 1.0, 0.0).astype(BF16)


def small_kernel(source, target):
    scale = 2.0 * LOG2E / source.shape[0]
    inner = dot(source, target, TN)
    squares = column_norms(source)[:, : target.shape[1]] + row_norms(target)
    return jnp.exp2(scale * (2.0 * inner - squares))


def pick(first, second, index, bit):
    count = first.shape[1]
    table = jnp.concatenate(
        [one_hot(index, count, count * bit), one_hot(index, count, count * (1 - bit))], axis=0
    )
    return dot(jnp.concatenate([first, second], axis=1), table).astype(BF16)


def write_message(weights, coords, matrix, message_ref, passed_ref):
    dimension, sides = coords.shape[0], weights.shape[0]
    passed = dot_split(weights, matrix, NT)
    message_ref[:dimension] = coords
    message_ref[dimension : dimension + sides] = weights.astype(BF16)
    message_ref[dimension + sides : dimension + 2 * sides] = passed.astype(BF16)
    passed_ref[...] = passed


def start_kernel(*refs):
    inputs, outs, held = refs[:7], refs[7:12], refs[12:19]
    made, sems, out_sems = refs[19:24], refs[24], refs[25]
    copies = [
        pltpu.make_async_copy(source, target, sems.at[number])
        for number, (source, target) in enumerate(zip(inputs, held))
    ]
    for copy in copies:
        copy.start()
    stores = [
        pltpu.make_async_copy(source, target, out_sems.at[number])
        for number, (source, target) in enumerate(zip(made, outs))
    ]
    order, skeletons, mask, charges, points, interp, transfer = held
    ordered_ref, coords_ref, marks_ref, message_ref, passed_ref = made
    dimension, rows = points.shape
    sides, count = passed_ref.shape
    for copy in copies[:4]:
        copy.wait()
    width = rows // 4
    for column in range(0, rows, width):
        table = one_hot(order[:, column : column + width], rows, 0)
        ordered_ref[:, column : column + width] = dot(charges[...], table).astype(BF16)
    stores[0].start()
    copies[4].wait()
    coords = dot(points[...], one_hot(skeletons[0], rows, 0)).astype(BF16)
    coords_ref[...] = coords
    stores[1].start()
    lane = lax.broadcasted_iota(jnp.int32, (1, count), 1)
    pattern = jnp.zeros((1, count), jnp.int32)
    for offset in range(mask.shape[1]):
        pattern = jnp.where(lane == offset, mask[:, offset : offset + 1], pattern)
    marks = jnp.broadcast_to(pattern.astype(F32), (PAD, count)).astype(BF16)
    marks_ref[...] = marks
    message_ref[dimension + 2 * sides :] = marks
    stores[2].start()
    copies[5].wait()
    weights = dot(ordered_ref[...], interp[...], NT)
    copies[6].wait()
    write_message(weights, coords, transfer[0], message_ref, passed_ref)
    stores[3].start()
    stores[4].start()
    for store in stores:
        store.wait()


def marked(marks, offset):
    rows = marks.astype(F32)
    lane = lax.broadcasted_iota(jnp.int32, rows.shape, 1)
    return jnp.max(jnp.where(lane == REACH + offset, rows, 0.0)) > 0.5


def round_kernel(level, last, skeletons, transfer, coords, passed, message, *outs):
    dimension = coords.shape[0]
    sides = passed.shape[0]
    bit = (lax.axis_index("leaf") >> level) & 1
    joined = pick(coords[...], message[:dimension], skeletons[level + 1], bit)
    span = slice(dimension + sides, dimension + 2 * sides)
    weights = passed[...] + message[span].astype(F32)
    if last:
        outs[0][:dimension] = joined
        outs[0][dimension:] = weights.astype(BF16)
        return
    outs[0][...] = joined
    write_message(weights, joined, transfer[level + 1], outs[1], outs[2])


def sibling_term(coords, message, sides):
    dimension = coords.shape[0]
    weights = message[dimension : dimension + sides]
    return dot_parts(weights, small_kernel(message[:dimension], coords[...]))


def term_kernel(sides, levels, transfer, coords, message, term_ref, *product_ref):
    term_ref[...] = sibling_term(coords, message, sides)
    if product_ref:
        product = transfer[levels - 1].astype(F32)
        for level in range(levels - 2, -1, -1):
            product = dot_split(product, transfer[level])
        product_ref[0][...] = product


def last_terms_kernel(sides, levels, transfer, *refs):
    pairs, terms, potential_ref = refs[:4], refs[4:-1], refs[-1]
    late = [sibling_term(pairs[0], pairs[1], sides), sibling_term(pairs[2], pairs[3], sides)]
    terms = [ref[...] for ref in terms] + late
    potential = terms[-1]
    for level in range(levels - 2, -1, -1):
        potential = dot_split(potential, transfer[level]) + terms[level]
    potential_ref[...] = potential


def lane_norms(tall):
    square = jnp.square(tall.astype(F32))
    norms = jnp.sum(square, axis=1, keepdims=True) * (2.0 * LOG2E / tall.shape[1])
    return jnp.broadcast_to(norms, (tall.shape[0], 128))


def turn_kernel(points, ordered, tall_ref, norms_ref):
    dimension, rows = points.shape
    sides = ordered.shape[0]
    tall_ref[:rows] = jnp.transpose(points[...])
    norms_ref[...] = lane_norms(tall_ref[:rows])
    for number in range(rows // dimension):
        first = rows + number * sides
        tall_ref[first : first + sides] = ordered[:, number * dimension : (number + 1) * dimension]


def bands(tall, norms, wide):
    dimension, rows = wide.shape
    scale = 2.0 * LOG2E / dimension
    target_norms = row_norms(wide[...]) * scale
    for row in range(0, rows, dimension):
        band = slice(row, row + dimension)
        source = tall[band]
        inner = dot(source, wide[...])
        own = lane_norms(source) if norms is None else norms[band]
        squares = jnp.tile(own, (1, rows // 128)) + target_norms
        yield band, jnp.exp2((2.0 * scale) * inner - squares).astype(BF16)


def self_kernel(tall, norms, wide, ordered, near_ref):
    for band, tile in bands(tall, norms, wide):
        near_ref[:, band] = dot(ordered[...], tile, NT)


def back_kernel(tall, norms, ordered, back_wide, back_ordered, marks, near, near_ref, held_ref):
    near_ref[...] = near[...]
    used = marked(marks[...], -2)

    @pl.when(used)
    def _():
        for band, tile in bands(tall, norms, back_wide):
            near_ref[:, band] += dot(back_ordered[...], tile, NT)
            part = dot(ordered[:, band], tile)
            if band.start:
                held_ref[...] += part
            else:
                held_ref[...] = part

    @pl.when(jnp.logical_not(used))
    def _():
        held_ref[...] = jnp.zeros_like(held_ref)


def pair_kernel(wide, ordered, side_tall, back_wide, back_ordered, marks, message, near, held,
                near_ref, back_ref, side_ref, sum_ref):
    dimension, rows = wide.shape
    sides = ordered.shape[0]
    odd = lax.rem(lax.axis_index("leaf"), 2)
    go_odd = jnp.logical_and(odd == 1, marked(message[message.shape[0] - PAD :], -1))
    go_even = jnp.logical_and(odd == 0, marked(marks[...], 1))

    def pair(other_wide, other_ordered):
        for band, tile in bands(side_tall, None, other_wide):
            side_ref[:, band] = dot(other_ordered[...], tile, NT).astype(BF16)
            first = rows + band.start // dimension * sides
            part = dot(side_tall[first : first + sides], tile)
            if band.start:
                sum_ref[...] += part
            else:
                sum_ref[...] = part

    @pl.when(go_odd)
    def _():
        pair(back_wide, back_ordered)
        back_ref[...] = (held[...] + sum_ref[...]).astype(BF16)
        near_ref[...] = near[...]

    @pl.when(go_even)
    def _():
        pair(wide, ordered)
        back_ref[...] = held[...].astype(BF16)
        near_ref[...] = near[...] + sum_ref[...]

    @pl.when(jnp.logical_not(jnp.logical_or(go_odd, go_even)))
    def _():
        back_ref[...] = held[...].astype(BF16)
        near_ref[...] = near[...]
        side_ref[...] = jnp.zeros_like(side_ref)


def far_kernel(others, own_top, potential, product, interp, near, side, *refs):
    tops, out_ref = refs[:others], refs[-1]
    sides = out_ref.shape[0]
    dimension = own_top.shape[0] - sides
    total = potential[...]
    above = None
    for top in tops:
        part = dot_parts(top[dimension:], small_kernel(top[:dimension], own_top[:dimension]))
        above = part if above is None else above + part
    if above is not None:
        total = total + dot_parts(above, product[...])
    out_ref[...] = (near[...] + side[...].astype(F32)) + dot_split(total, interp[...])


def total_kernel(here, back, out_ref):
    out_ref[...] = here[...] + back[...].astype(F32)


def call(kernel, outs, args, scratch=(), anywhere=False, flops=0, exps=0, name=None):
    vmem = pl.BlockSpec(memory_space=pltpu.VMEM)
    rest = pl.BlockSpec(memory_space=pl.ANY) if anywhere else vmem
    moved = 0 if anywhere or flops == 0 else sum(a.size * a.dtype.itemsize for a in list(args) + list(outs))
    return pl.pallas_call(
        kernel,
        out_shape=outs,
        in_specs=[rest] * len(args),
        out_specs=[rest if anywhere else vmem] * len(outs),
        scratch_shapes=list(scratch),
        compiler_params=pltpu.CompilerParams(
            vmem_limit_bytes=START_VMEM if anywhere else VMEM_LIMIT
        ),
        cost_estimate=pl.CostEstimate(flops=flops, bytes_accessed=moved, transcendentals=exps),
        name=name,
    )(*args)


def swapped(value, axis, flip):
    count = lax.axis_size(axis)
    return lax.ppermute(value, axis, [(place, place ^ flip) for place in range(count)])


def rotated(value, axis, turn):
    count = lax.axis_size(axis)
    return lax.ppermute(value, axis, [(place, (place + turn) % count) for place in range(count)])


def shifted(value, axis, step):
    places = range(lax.axis_size(axis))
    return lax.ppermute(
        value, axis, [(place, place + step) for place in places if place + step in places]
    )


def shape(dims, dtype):
    return jax.ShapeDtypeStruct(dims, dtype)


def local(points, charges, order, near_mask, skeletons, leaf_interp, transfer):
    dimension, rows = points.shape
    sides, count = charges.shape[0], leaf_interp.shape[0]
    leaves, groups = lax.axis_size("leaf"), lax.axis_size("grp")
    levels = leaves.bit_length() - 1
    skeletons = jnp.transpose(skeletons, (1, 0, 2))
    transfer = transfer[0]
    block_sums = shape((sides, rows), F32)
    block_values = shape((sides, rows), BF16)
    node_points = shape((dimension, count), BF16)
    node_sums = shape((sides, count), F32)
    tile_flops = 2 * rows * rows * (dimension + 2 * sides)

    back_points = rotated(points, "leaf", 2)

    inputs = [order.reshape(1, rows), skeletons, near_mask, charges, points, leaf_interp, transfer]
    made = [
        block_values,
        node_points,
        shape((PAD, count), BF16),
        shape((dimension + 2 * sides + PAD, count), BF16),
        node_sums,
    ]
    ordered, coords, marks, message, passed = call(
        start_kernel,
        made,
        inputs,
        scratch=[pltpu.VMEM(value.shape, value.dtype) for value in inputs + made]
        + [pltpu.SemaphoreType.DMA((len(inputs),)), pltpu.SemaphoreType.DMA((len(made),))],
        anywhere=True,
        name="start",
    )
    tall, norms = call(
        turn_kernel,
        [shape((rows + sides * rows // dimension, dimension), BF16), shape((rows, 128), F32)],
        [points, ordered],
        name="turn",
    )
    history, terms = [], []
    for level in range(levels):
        received = swapped(message, "leaf", 1 << level)
        if level == 0:
            first_received = received
            side_tall = swapped(tall, "leaf", 1)
        if level == 1:
            received, back_points = lax.optimization_barrier((received, back_points))
        last = level == levels - 1
        if level and not last:
            made = call(
                functools.partial(term_kernel, sides, levels),
                [node_sums] + [shape((count, count), F32)] * (level == 1),
                [transfer] + history[-2:],
                flops=8 * dimension * count * count,
                name="sibling_term",
            )
            terms.append(made[0])
            if level == 1:
                product = made[1]
            passed = lax.optimization_barrier((passed, made[0]))[0]
        history += [coords, received]
        if level == levels - 2:
            near, held = call(
                back_kernel,
                [block_sums, block_sums],
                [tall, norms, ordered, back_points, back_ordered, marks]
                + [lax.optimization_barrier((near, passed))[0]],
                flops=tile_flops,
                exps=rows * rows,
                name="back_tile",
            )
            passed, held = lax.optimization_barrier((passed, held))
        if last:
            near, back, side = call(
                pair_kernel,
                [block_sums, block_values, block_values],
                [points, ordered, side_tall, back_points, back_ordered, marks, first_received]
                + [lax.optimization_barrier((near, passed))[0], held],
                scratch=[pltpu.VMEM((sides, rows), F32)],
                flops=tile_flops,
                exps=rows * rows,
                name="pair_tile",
            )
            passed, near = lax.optimization_barrier((passed, near))
            back = rotated(back, "leaf", -2)
            side = swapped(side, "leaf", 1)
        if last:
            outs = [shape((dimension + sides, count), BF16)]
        else:
            outs = [node_points, shape((dimension + 2 * sides, count), BF16), node_sums]
        results = call(
            functools.partial(round_kernel, level, last),
            outs,
            [skeletons, transfer, coords, passed, received],
            flops=(JOIN_FLOPS if level < 2 else 8) * dimension * count * count,
            name="join_level",
        )
        if not last:
            coords, message, passed = results
        if level == 0:
            (near,) = call(
                self_kernel,
                [block_sums],
                [tall, norms, points, lax.optimization_barrier((ordered, results[-1]))[0]],
                name="self_tile",
            )
            sent = lax.optimization_barrier((ordered, near))[0]
            back_ordered = shifted(sent, "leaf", 2)
    own_top = results[0]
    tops = [rotated(own_top, "grp", turn) for turn in range(1, groups)]
    (potential,) = call(
        functools.partial(last_terms_kernel, sides, levels),
        [node_sums],
        [transfer] + history[-4:] + terms,
        flops=8 * dimension * count * count,
        exps=count * count,
        name="last_terms",
    )
    (here,) = call(
        functools.partial(far_kernel, len(tops)),
        [block_sums],
        [own_top, potential, product, leaf_interp, near, side] + tops,
        flops=4 * sides * rows * count,
        name="far_field",
    )
    (out,) = call(total_kernel, [block_sums], [here, back], flops=2 * sides * rows, name="total")
    return out


def solution(mesh):
    in_specs = (
        P(None, ("leaf", "grp")),
        P(None, ("leaf", "grp")),
        P(("leaf", "grp")),
        P(("leaf", "grp"), None),
        P(("leaf", "grp"), None, None),
        P(None, ("leaf", "grp")),
        P(("leaf", "grp"), None, None, None),
    )
    out_specs = P(None, ("leaf", "grp"))
    return jax.shard_map(local, mesh=mesh, in_specs=in_specs, out_specs=out_specs, check_vma=False)
```

```python
import functools

import jax
import jax.numpy as jnp
from jax import lax
from jax.experimental import pallas as pl
from jax.experimental.pallas import tpu as pltpu
from jax.sharding import PartitionSpec as P

REACH = 2
BF16 = jnp.bfloat16
F32 = jnp.float32
LOG2E = 1.4426950408889634
PAD = 16
JOIN_FLOPS = 500
VMEM_LIMIT = 40 * 1024 * 1024
START_VMEM = 56 * 1024 * 1024

NN = ((1,), (0,))
NT = ((1,), (1,))
TN = ((0,), (0,))


def dot(left, right, contract=NN, precision=None):
    return lax.dot_general(
        left, right, (contract, ((), ())), preferred_element_type=F32, precision=precision
    )


def halves(value):
    high = value.astype(BF16)
    return high, (value - high.astype(F32)).astype(BF16)


def dot_split(left, right, contract=NN):
    rows = left.shape[0]
    both = dot(jnp.concatenate(halves(left), axis=0), right, contract)
    return both[:rows] + both[rows:]


def dot_parts(left, right):
    rows, columns = left.shape[0], right.shape[1]
    if left.dtype != BF16:
        left = jnp.concatenate(halves(left), axis=0)
    both = dot(left, jnp.concatenate(halves(right), axis=1))
    total = both[:rows, :columns] + both[:rows, columns:]
    if left.shape[0] > rows:
        total = total + (both[rows:, :columns] + both[rows:, columns:])
    return total


def row_norms(points):
    wide = points.astype(F32)
    return jnp.sum(wide * wide, axis=0, keepdims=True)


def column_norms(points):
    wide = points.astype(F32)
    high, low = halves(wide * wide)
    ones = jnp.ones((points.shape[0], 128), BF16)
    return dot(high, ones, TN) + dot(low, ones, TN)


def one_hot(index, rows, first):
    place = lax.broadcasted_iota(jnp.int32, (rows, index.shape[1]), 0) + first
    return jnp.where(place == index, 1.0, 0.0).astype(BF16)


def small_kernel(source, target):
    scale = 2.0 * LOG2E / source.shape[0]
    inner = dot(source, target, TN)
    squares = column_norms(source)[:, : target.shape[1]] + row_norms(target)
    return jnp.exp2(scale * (2.0 * inner - squares))


def pick(first, second, index, bit):
    count = first.shape[1]
    table = jnp.concatenate(
        [one_hot(index, count, count * bit), one_hot(index, count, count * (1 - bit))], axis=0
    )
    return dot(jnp.concatenate([first, second], axis=1), table).astype(BF16)


def write_message(weights, coords, matrix, message_ref, passed_ref):
    dimension, sides = coords.shape[0], weights.shape[0]
    passed = dot_split(weights, matrix, NT)
    message_ref[:dimension] = coords
    message_ref[dimension : dimension + sides] = weights.astype(BF16)
    message_ref[dimension + sides : dimension + 2 * sides] = passed.astype(BF16)
    passed_ref[...] = passed


def start_kernel(*refs):
    inputs, outs, held = refs[:7], refs[7:12], refs[12:19]
    made, sems, out_sems = refs[19:24], refs[24], refs[25]
    copies = [
        pltpu.make_async_copy(source, target, sems.at[number])
        for number, (source, target) in enumerate(zip(inputs, held))
    ]
    for copy in copies:
        copy.start()
    stores = [
        pltpu.make_async_copy(source, target, out_sems.at[number])
        for number, (source, target) in enumerate(zip(made, outs))
    ]
    order, skeletons, mask, charges, points, interp, transfer = held
    ordered_ref, coords_ref, marks_ref, message_ref, passed_ref = made
    dimension, rows = points.shape
    sides, count = passed_ref.shape
    for copy in copies[:4]:
        copy.wait()
    width = rows // 4
    for column in range(0, rows, width):
        table = one_hot(order[:, column : column + width], rows, 0)
        ordered_ref[:, column : column + width] = dot(charges[...], table).astype(BF16)
    stores[0].start()
    copies[4].wait()
    coords = dot(points[...], one_hot(skeletons[0], rows, 0)).astype(BF16)
    coords_ref[...] = coords
    stores[1].start()
    lane = lax.broadcasted_iota(jnp.int32, (1, count), 1)
    pattern = jnp.zeros((1, count), jnp.int32)
    for offset in range(mask.shape[1]):
        pattern = jnp.where(lane == offset, mask[:, offset : offset + 1], pattern)
    marks = jnp.broadcast_to(pattern.astype(F32), (PAD, count)).astype(BF16)
    marks_ref[...] = marks
    message_ref[dimension + 2 * sides :] = marks
    stores[2].start()
    copies[5].wait()
    weights = dot(ordered_ref[...], interp[...], NT)
    copies[6].wait()
    write_message(weights, coords, transfer[0], message_ref, passed_ref)
    stores[3].start()
    stores[4].start()
    for store in stores:
        store.wait()


def marked(marks, offset):
    rows = marks.astype(F32)
    lane = lax.broadcasted_iota(jnp.int32, rows.shape, 1)
    return jnp.max(jnp.where(lane == REACH + offset, rows, 0.0)) > 0.5


def round_kernel(level, last, skeletons, transfer, coords, passed, message, *outs):
    dimension = coords.shape[0]
    sides = passed.shape[0]
    bit = (lax.axis_index("leaf") >> level) & 1
    joined = pick(coords[...], message[:dimension], skeletons[level + 1], bit)
    span = slice(dimension + sides, dimension + 2 * sides)
    weights = passed[...] + message[span].astype(F32)
    if last:
        outs[0][:dimension] = joined
        outs[0][dimension:] = weights.astype(BF16)
        return
    outs[0][...] = joined
    write_message(weights, joined, transfer[level + 1], outs[1], outs[2])


def sibling_term(coords, message, sides):
    dimension = coords.shape[0]
    weights = message[dimension : dimension + sides]
    return dot_parts(weights, small_kernel(message[:dimension], coords[...]))


def term_kernel(sides, levels, transfer, coords, message, term_ref, *product_ref):
    term_ref[...] = sibling_term(coords, message, sides)
    if product_ref:
        product = transfer[levels - 1].astype(F32)
        for level in range(levels - 2, -1, -1):
            product = dot_split(product, transfer[level])
        product_ref[0][...] = product


def last_terms_kernel(sides, levels, transfer, *refs):
    pairs, terms, potential_ref = refs[:4], refs[4:-1], refs[-1]
    late = [sibling_term(pairs[0], pairs[1], sides), sibling_term(pairs[2], pairs[3], sides)]
    terms = [ref[...] for ref in terms] + late
    potential = terms[-1]
    for level in range(levels - 2, -1, -1):
        potential = dot_split(potential, transfer[level]) + terms[level]
    potential_ref[...] = potential


def lane_norms(tall):
    square = jnp.square(tall.astype(F32))
    norms = jnp.sum(square, axis=1, keepdims=True) * (2.0 * LOG2E / tall.shape[1])
    return jnp.broadcast_to(norms, (tall.shape[0], 128))


def turn_kernel(points, ordered, tall_ref, norms_ref):
    dimension, rows = points.shape
    sides = ordered.shape[0]
    tall_ref[:rows] = jnp.transpose(points[...])
    norms_ref[...] = lane_norms(tall_ref[:rows])
    for number in range(rows // dimension):
        first = rows + number * sides
        tall_ref[first : first + sides] = ordered[:, number * dimension : (number + 1) * dimension]


def bands(tall, norms, wide):
    dimension, rows = wide.shape
    scale = 2.0 * LOG2E / dimension
    target_norms = row_norms(wide[...]) * scale
    for row in range(0, rows, dimension):
        band = slice(row, row + dimension)
        source = tall[band]
        inner = dot(source, wide[...])
        own = lane_norms(source) if norms is None else norms[band]
        squares = jnp.tile(own, (1, rows // 128)) + target_norms
        yield band, jnp.exp2((2.0 * scale) * inner - squares).astype(BF16)


def self_kernel(tall, norms, wide, ordered, near_ref):
    for band, tile in bands(tall, norms, wide):
        near_ref[:, band] = dot(ordered[...], tile, NT)


def back_kernel(tall, norms, ordered, back_wide, back_ordered, marks, near, near_ref, held_ref):
    near_ref[...] = near[...]
    used = marked(marks[...], -2)

    @pl.when(used)
    def _():
        for band, tile in bands(tall, norms, back_wide):
            near_ref[:, band] += dot(back_ordered[...], tile, NT)
            part = dot(ordered[:, band], tile)
            if band.start:
                held_ref[...] += part
            else:
                held_ref[...] = part

    @pl.when(jnp.logical_not(used))
    def _():
        held_ref[...] = jnp.zeros_like(held_ref)


def pair_kernel(wide, ordered, side_tall, back_wide, back_ordered, marks, message, near, held,
                near_ref, back_ref, side_ref, sum_ref):
    dimension, rows = wide.shape
    sides = ordered.shape[0]
    odd = lax.rem(lax.axis_index("leaf"), 2)
    go_odd = jnp.logical_and(odd == 1, marked(message[message.shape[0] - PAD :], -1))
    go_even = jnp.logical_and(odd == 0, marked(marks[...], 1))

    def pair(other_wide, other_ordered):
        for band, tile in bands(side_tall, None, other_wide):
            side_ref[:, band] = dot(other_ordered[...], tile, NT).astype(BF16)
            first = rows + band.start // dimension * sides
            part = dot(side_tall[first : first + sides], tile)
            if band.start:
                sum_ref[...] += part
            else:
                sum_ref[...] = part

    @pl.when(go_odd)
    def _():
        pair(back_wide, back_ordered)
        back_ref[...] = (held[...] + sum_ref[...]).astype(BF16)
        near_ref[...] = near[...]

    @pl.when(go_even)
    def _():
        pair(wide, ordered)
        back_ref[...] = held[...].astype(BF16)
        near_ref[...] = near[...] + sum_ref[...]

    @pl.when(jnp.logical_not(jnp.logical_or(go_odd, go_even)))
    def _():
        back_ref[...] = held[...].astype(BF16)
        near_ref[...] = near[...]
        side_ref[...] = jnp.zeros_like(side_ref)


def far_kernel(others, own_top, potential, product, interp, near, side, *refs):
    tops, out_ref = refs[:others], refs[-1]
    sides = out_ref.shape[0]
    dimension = own_top.shape[0] - sides
    total = potential[...]
    above = None
    for top in tops:
        part = dot_parts(top[dimension:], small_kernel(top[:dimension], own_top[:dimension]))
        above = part if above is None else above + part
    if above is not None:
        total = total + dot_parts(above, product[...])
    out_ref[...] = (near[...] + side[...].astype(F32)) + dot_split(total, interp[...])


def total_kernel(here, back, out_ref):
    out_ref[...] = here[...] + back[...].astype(F32)


def call(kernel, outs, args, scratch=(), anywhere=False, flops=0, exps=0, name=None):
    vmem = pl.BlockSpec(memory_space=pltpu.VMEM)
    rest = pl.BlockSpec(memory_space=pl.ANY) if anywhere else vmem
    moved = 0 if anywhere or flops == 0 else sum(a.size * a.dtype.itemsize for a in list(args) + list(outs))
    return pl.pallas_call(
        kernel,
        out_shape=outs,
        in_specs=[rest] * len(args),
        out_specs=[rest if anywhere else vmem] * len(outs),
        scratch_shapes=list(scratch),
        compiler_params=pltpu.CompilerParams(
            vmem_limit_bytes=START_VMEM if anywhere else VMEM_LIMIT
        ),
        cost_estimate=pl.CostEstimate(flops=flops, bytes_accessed=moved, transcendentals=exps),
        name=name,
    )(*args)


def swapped(value, axis, flip):
    count = lax.axis_size(axis)
    return lax.ppermute(value, axis, [(place, place ^ flip) for place in range(count)])


def rotated(value, axis, turn):
    count = lax.axis_size(axis)
    return lax.ppermute(value, axis, [(place, (place + turn) % count) for place in range(count)])


def shifted(value, axis, step):
    places = range(lax.axis_size(axis))
    return lax.ppermute(
        value, axis, [(place, place + step) for place in places if place + step in places]
    )


def shape(dims, dtype):
    return jax.ShapeDtypeStruct(dims, dtype)


def local(points, charges, order, near_mask, skeletons, leaf_interp, transfer):
    dimension, rows = points.shape
    sides, count = charges.shape[0], leaf_interp.shape[0]
    leaves, groups = lax.axis_size("leaf"), lax.axis_size("grp")
    levels = leaves.bit_length() - 1
    skeletons = jnp.transpose(skeletons, (1, 0, 2))
    transfer = transfer[0]
    block_sums = shape((sides, rows), F32)
    block_values = shape((sides, rows), BF16)
    node_points = shape((dimension, count), BF16)
    node_sums = shape((sides, count), F32)
    tile_flops = 2 * rows * rows * (dimension + 2 * sides)

    back_points = rotated(points, "leaf", 2)

    inputs = [order.reshape(1, rows), skeletons, near_mask, charges, points, leaf_interp, transfer]
    made = [
        block_values,
        node_points,
        shape((PAD, count), BF16),
        shape((dimension + 2 * sides + PAD, count), BF16),
        node_sums,
    ]
    ordered, coords, marks, message, passed = call(
        start_kernel,
        made,
        inputs,
        scratch=[pltpu.VMEM(value.shape, value.dtype) for value in inputs + made]
        + [pltpu.SemaphoreType.DMA((len(inputs),)), pltpu.SemaphoreType.DMA((len(made),))],
        anywhere=True,
        name="start",
    )
    tall, norms = call(
        turn_kernel,
        [shape((rows + sides * rows // dimension, dimension), BF16), shape((rows, 128), F32)],
        [points, ordered],
        name="turn",
    )
    history, terms = [], []
    for level in range(levels):
        received = swapped(message, "leaf", 1 << level)
        if level == 0:
            first_received = received
            side_tall = swapped(tall, "leaf", 1)
        if level == 1:
            received, back_points = lax.optimization_barrier((received, back_points))
        last = level == levels - 1
        if level and not last:
            made = call(
                functools.partial(term_kernel, sides, levels),
                [node_sums] + [shape((count, count), F32)] * (level == 1),
                [transfer] + history[-2:],
                flops=8 * dimension * count * count,
                name="sibling_term",
            )
            terms.append(made[0])
            if level == 1:
                product = made[1]
            passed = lax.optimization_barrier((passed, made[0]))[0]
        history += [coords, received]
        if level == levels - 2:
            near, held = call(
                back_kernel,
                [block_sums, block_sums],
                [tall, norms, ordered, back_points, back_ordered, marks]
                + [lax.optimization_barrier((near, passed))[0]],
                flops=tile_flops,
                exps=rows * rows,
                name="back_tile",
            )
            passed, held = lax.optimization_barrier((passed, held))
        if last:
            near, back, side = call(
                pair_kernel,
                [block_sums, block_values, block_values],
                [points, ordered, side_tall, back_points, back_ordered, marks, first_received]
                + [lax.optimization_barrier((near, passed))[0], held],
                scratch=[pltpu.VMEM((sides, rows), F32)],
                flops=tile_flops,
                exps=rows * rows,
                name="pair_tile",
            )
            passed, near = lax.optimization_barrier((passed, near))
            back = shifted(back, "leaf", -2)
            side = swapped(side, "leaf", 1)
        if last:
            outs = [shape((dimension + sides, count), BF16)]
        else:
            outs = [node_points, shape((dimension + 2 * sides, count), BF16), node_sums]
        results = call(
            functools.partial(round_kernel, level, last),
            outs,
            [skeletons, transfer, coords, passed, received],
            flops=(JOIN_FLOPS if level < 2 else 8) * dimension * count * count,
            name="join_level",
        )
        if not last:
            coords, message, passed = results
        if level == 0:
            (near,) = call(
                self_kernel,
                [block_sums],
                [tall, norms, points, lax.optimization_barrier((ordered, results[-1]))[0]],
                name="self_tile",
            )
            sent = lax.optimization_barrier((ordered, near))[0]
            back_ordered = shifted(sent, "leaf", 2)
    own_top = results[0]
    tops = [rotated(own_top, "grp", turn) for turn in range(1, groups)]
    (potential,) = call(
        functools.partial(last_terms_kernel, sides, levels),
        [node_sums],
        [transfer] + history[-4:] + terms,
        flops=8 * dimension * count * count,
        exps=count * count,
        name="last_terms",
    )
    (here,) = call(
        functools.partial(far_kernel, len(tops)),
        [block_sums],
        [own_top, potential, product, leaf_interp, near, side] + tops,
        flops=4 * sides * rows * count,
        name="far_field",
    )
    (out,) = call(total_kernel, [block_sums], [here, back], flops=2 * sides * rows, name="total")
    return out


def solution(mesh):
    in_specs = (
        P(None, ("leaf", "grp")),
        P(None, ("leaf", "grp")),
        P(("leaf", "grp")),
        P(("leaf", "grp"), None),
        P(("leaf", "grp"), None, None),
        P(None, ("leaf", "grp")),
        P(("leaf", "grp"), None, None, None),
    )
    out_specs = P(None, ("leaf", "grp"))
    return jax.shard_map(local, mesh=mesh, in_specs=in_specs, out_specs=out_specs, check_vma=False)
```

```python
import functools

import jax
import jax.numpy as jnp
from jax import lax
from jax.experimental import pallas as pl
from jax.experimental.pallas import tpu as pltpu
from jax.sharding import PartitionSpec as P

REACH = 2
BF16 = jnp.bfloat16
F32 = jnp.float32
LOG2E = 1.4426950408889634
PAD = 16
JOIN_FLOPS = 500
VMEM_LIMIT = 40 * 1024 * 1024
START_VMEM = 56 * 1024 * 1024

NN = ((1,), (0,))
NT = ((1,), (1,))
TN = ((0,), (0,))


def dot(left, right, contract=NN, precision=None):
    return lax.dot_general(
        left, right, (contract, ((), ())), preferred_element_type=F32, precision=precision
    )


def halves(value):
    high = value.astype(BF16)
    return high, (value - high.astype(F32)).astype(BF16)


def dot_split(left, right, contract=NN):
    rows = left.shape[0]
    both = dot(jnp.concatenate(halves(left), axis=0), right, contract)
    return both[:rows] + both[rows:]


def dot_parts(left, right):
    rows, columns = left.shape[0], right.shape[1]
    if left.dtype != BF16:
        left = jnp.concatenate(halves(left), axis=0)
    both = dot(left, jnp.concatenate(halves(right), axis=1))
    total = both[:rows, :columns] + both[:rows, columns:]
    if left.shape[0] > rows:
        total = total + (both[rows:, :columns] + both[rows:, columns:])
    return total


def row_norms(points):
    wide = points.astype(F32)
    return jnp.sum(wide * wide, axis=0, keepdims=True)


def column_norms(points):
    wide = points.astype(F32)
    high, low = halves(wide * wide)
    ones = jnp.ones((points.shape[0], 128), BF16)
    return dot(high, ones, TN) + dot(low, ones, TN)


def one_hot(index, rows, first):
    place = lax.broadcasted_iota(jnp.int32, (rows, index.shape[1]), 0) + first
    return jnp.where(place == index, 1.0, 0.0).astype(BF16)


def small_kernel(source, target):
    scale = 2.0 * LOG2E / source.shape[0]
    inner = dot(source, target, TN)
    squares = column_norms(source)[:, : target.shape[1]] + row_norms(target)
    return jnp.exp2(scale * (2.0 * inner - squares))


def pick(first, second, index, bit):
    count = first.shape[1]
    table = jnp.concatenate(
        [one_hot(index, count, count * bit), one_hot(index, count, count * (1 - bit))], axis=0
    )
    return dot(jnp.concatenate([first, second], axis=1), table).astype(BF16)


def write_message(weights, coords, matrix, message_ref, passed_ref):
    dimension, sides = coords.shape[0], weights.shape[0]
    passed = dot_split(weights, matrix, NT)
    message_ref[:dimension] = coords
    message_ref[dimension : dimension + sides] = weights.astype(BF16)
    message_ref[dimension + sides : dimension + 2 * sides] = passed.astype(BF16)
    passed_ref[...] = passed


def start_kernel(*refs):
    inputs, outs, held = refs[:7], refs[7:12], refs[12:19]
    made, sems, out_sems = refs[19:24], refs[24], refs[25]
    copies = [
        pltpu.make_async_copy(source, target, sems.at[number])
        for number, (source, target) in enumerate(zip(inputs, held))
    ]
    for copy in copies:
        copy.start()
    stores = [
        pltpu.make_async_copy(source, target, out_sems.at[number])
        for number, (source, target) in enumerate(zip(made, outs))
    ]
    order, skeletons, mask, charges, points, interp, transfer = held
    ordered_ref, coords_ref, marks_ref, message_ref, passed_ref = made
    dimension, rows = points.shape
    sides, count = passed_ref.shape
    for copy in copies[:4]:
        copy.wait()
    width = rows // 4
    for column in range(0, rows, width):
        table = one_hot(order[:, column : column + width], rows, 0)
        ordered_ref[:, column : column + width] = dot(charges[...], table).astype(BF16)
    stores[0].start()
    copies[4].wait()
    coords = dot(points[...], one_hot(skeletons[0], rows, 0)).astype(BF16)
    coords_ref[...] = coords
    stores[1].start()
    lane = lax.broadcasted_iota(jnp.int32, (1, count), 1)
    pattern = jnp.zeros((1, count), jnp.int32)
    for offset in range(mask.shape[1]):
        pattern = jnp.where(lane == offset, mask[:, offset : offset + 1], pattern)
    marks = jnp.broadcast_to(pattern.astype(F32), (PAD, count)).astype(BF16)
    marks_ref[...] = marks
    message_ref[dimension + 2 * sides :] = marks
    stores[2].start()
    copies[5].wait()
    weights = dot(ordered_ref[...], interp[...], NT)
    copies[6].wait()
    write_message(weights, coords, transfer[0], message_ref, passed_ref)
    stores[3].start()
    stores[4].start()
    for store in stores:
        store.wait()


def marked(marks, offset):
    rows = marks.astype(F32)
    lane = lax.broadcasted_iota(jnp.int32, rows.shape, 1)
    return jnp.max(jnp.where(lane == REACH + offset, rows, 0.0)) > 0.5


def round_kernel(level, last, skeletons, transfer, coords, passed, message, *outs):
    dimension = coords.shape[0]
    sides = passed.shape[0]
    bit = (lax.axis_index("leaf") >> level) & 1
    joined = pick(coords[...], message[:dimension], skeletons[level + 1], bit)
    span = slice(dimension + sides, dimension + 2 * sides)
    weights = passed[...] + message[span].astype(F32)
    if last:
        outs[0][:dimension] = joined
        outs[0][dimension:] = weights.astype(BF16)
        return
    outs[0][...] = joined
    write_message(weights, joined, transfer[level + 1], outs[1], outs[2])


def sibling_term(coords, message, sides):
    dimension = coords.shape[0]
    weights = message[dimension : dimension + sides]
    return dot_parts(weights, small_kernel(message[:dimension], coords[...]))


def term_kernel(sides, levels, transfer, coords, message, term_ref, *product_ref):
    term_ref[...] = sibling_term(coords, message, sides)
    if product_ref:
        product = transfer[levels - 1].astype(F32)
        for level in range(levels - 2, -1, -1):
            product = dot_split(product, transfer[level])
        product_ref[0][...] = product


def last_terms_kernel(sides, levels, transfer, *refs):
    pairs, terms, potential_ref = refs[:4], refs[4:-1], refs[-1]
    late = [sibling_term(pairs[0], pairs[1], sides), sibling_term(pairs[2], pairs[3], sides)]
    terms = [ref[...] for ref in terms] + late
    potential = terms[-1]
    for level in range(levels - 2, -1, -1):
        potential = dot_split(potential, transfer[level]) + terms[level]
    potential_ref[...] = potential


def lane_norms(tall):
    square = jnp.square(tall.astype(F32))
    norms = jnp.sum(square, axis=1, keepdims=True) * (2.0 * LOG2E / tall.shape[1])
    return jnp.broadcast_to(norms, (tall.shape[0], 128))


def turn_kernel(points, ordered, tall_ref, norms_ref):
    dimension, rows = points.shape
    sides = ordered.shape[0]
    tall_ref[:rows] = jnp.transpose(points[...])
    norms_ref[...] = lane_norms(tall_ref[:rows])
    for number in range(rows // dimension):
        first = rows + number * sides
        tall_ref[first : first + sides] = ordered[:, number * dimension : (number + 1) * dimension]


def bands(tall, norms, wide):
    dimension, rows = wide.shape
    scale = 2.0 * LOG2E / dimension
    target_norms = row_norms(wide[...]) * scale
    for row in range(0, rows, dimension):
        band = slice(row, row + dimension)
        source = tall[band]
        inner = dot(source, wide[...])
        own = lane_norms(source) if norms is None else norms[band]
        squares = jnp.tile(own, (1, rows // 128)) + target_norms
        yield band, jnp.exp2((2.0 * scale) * inner - squares).astype(BF16)


def gathered(tile, turned):
    return jnp.transpose(dot(tile, turned))


def self_kernel(tall, norms, wide, ordered, near_ref):
    turned = jnp.transpose(ordered[...])
    for band, tile in bands(tall, norms, wide):
        near_ref[:, band] = gathered(tile, turned)


def back_kernel(tall, norms, ordered, back_wide, back_ordered, marks, near, near_ref, held_ref):
    near_ref[...] = near[...]
    used = marked(marks[...], -2)

    @pl.when(used)
    def _():
        turned = jnp.transpose(back_ordered[...])
        for band, tile in bands(tall, norms, back_wide):
            near_ref[:, band] += gathered(tile, turned)
            part = dot(ordered[:, band], tile)
            if band.start:
                held_ref[...] += part
            else:
                held_ref[...] = part

    @pl.when(jnp.logical_not(used))
    def _():
        held_ref[...] = jnp.zeros_like(held_ref)


def pair_kernel(wide, ordered, side_tall, back_wide, back_ordered, marks, message, near, held,
                near_ref, back_ref, side_ref, sum_ref):
    dimension, rows = wide.shape
    sides = ordered.shape[0]
    odd = lax.rem(lax.axis_index("leaf"), 2)
    go_odd = jnp.logical_and(odd == 1, marked(message[message.shape[0] - PAD :], -1))
    go_even = jnp.logical_and(odd == 0, marked(marks[...], 1))

    def pair(other_wide, other_ordered):
        turned = jnp.transpose(other_ordered[...])
        for band, tile in bands(side_tall, None, other_wide):
            side_ref[:, band] = gathered(tile, turned).astype(BF16)
            first = rows + band.start // dimension * sides
            part = dot(side_tall[first : first + sides], tile)
            if band.start:
                sum_ref[...] += part
            else:
                sum_ref[...] = part

    @pl.when(go_odd)
    def _():
        pair(back_wide, back_ordered)
        back_ref[...] = (held[...] + sum_ref[...]).astype(BF16)
        near_ref[...] = near[...]

    @pl.when(go_even)
    def _():
        pair(wide, ordered)
        back_ref[...] = held[...].astype(BF16)
        near_ref[...] = near[...] + sum_ref[...]

    @pl.when(jnp.logical_not(jnp.logical_or(go_odd, go_even)))
    def _():
        back_ref[...] = held[...].astype(BF16)
        near_ref[...] = near[...]
        side_ref[...] = jnp.zeros_like(side_ref)


def far_kernel(others, own_top, potential, product, interp, near, side, *refs):
    tops, out_ref = refs[:others], refs[-1]
    sides = out_ref.shape[0]
    dimension = own_top.shape[0] - sides
    total = potential[...]
    above = None
    for top in tops:
        part = dot_parts(top[dimension:], small_kernel(top[:dimension], own_top[:dimension]))
        above = part if above is None else above + part
    if above is not None:
        total = total + dot_parts(above, product[...])
    out_ref[...] = (near[...] + side[...].astype(F32)) + dot_split(total, interp[...])


def total_kernel(here, back, out_ref):
    out_ref[...] = here[...] + back[...].astype(F32)


def call(kernel, outs, args, scratch=(), anywhere=False, flops=0, exps=0, name=None):
    vmem = pl.BlockSpec(memory_space=pltpu.VMEM)
    rest = pl.BlockSpec(memory_space=pl.ANY) if anywhere else vmem
    moved = 0 if anywhere or flops == 0 else sum(a.size * a.dtype.itemsize for a in list(args) + list(outs))
    return pl.pallas_call(
        kernel,
        out_shape=outs,
        in_specs=[rest] * len(args),
        out_specs=[rest if anywhere else vmem] * len(outs),
        scratch_shapes=list(scratch),
        compiler_params=pltpu.CompilerParams(
            vmem_limit_bytes=START_VMEM if anywhere else VMEM_LIMIT
        ),
        cost_estimate=pl.CostEstimate(flops=flops, bytes_accessed=moved, transcendentals=exps),
        name=name,
    )(*args)


def swapped(value, axis, flip):
    count = lax.axis_size(axis)
    return lax.ppermute(value, axis, [(place, place ^ flip) for place in range(count)])


def rotated(value, axis, turn):
    count = lax.axis_size(axis)
    return lax.ppermute(value, axis, [(place, (place + turn) % count) for place in range(count)])


def shifted(value, axis, step):
    places = range(lax.axis_size(axis))
    return lax.ppermute(
        value, axis, [(place, place + step) for place in places if place + step in places]
    )


def shape(dims, dtype):
    return jax.ShapeDtypeStruct(dims, dtype)


def local(points, charges, order, near_mask, skeletons, leaf_interp, transfer):
    dimension, rows = points.shape
    sides, count = charges.shape[0], leaf_interp.shape[0]
    leaves, groups = lax.axis_size("leaf"), lax.axis_size("grp")
    levels = leaves.bit_length() - 1
    skeletons = jnp.transpose(skeletons, (1, 0, 2))
    transfer = transfer[0]
    block_sums = shape((sides, rows), F32)
    block_values = shape((sides, rows), BF16)
    node_points = shape((dimension, count), BF16)
    node_sums = shape((sides, count), F32)
    tile_flops = 2 * rows * rows * (dimension + 2 * sides)

    back_points = rotated(points, "leaf", 2)

    inputs = [order.reshape(1, rows), skeletons, near_mask, charges, points, leaf_interp, transfer]
    made = [
        block_values,
        node_points,
        shape((PAD, count), BF16),
        shape((dimension + 2 * sides + PAD, count), BF16),
        node_sums,
    ]
    ordered, coords, marks, message, passed = call(
        start_kernel,
        made,
        inputs,
        scratch=[pltpu.VMEM(value.shape, value.dtype) for value in inputs + made]
        + [pltpu.SemaphoreType.DMA((len(inputs),)), pltpu.SemaphoreType.DMA((len(made),))],
        anywhere=True,
        name="start",
    )
    tall, norms = call(
        turn_kernel,
        [shape((rows + sides * rows // dimension, dimension), BF16), shape((rows, 128), F32)],
        [points, ordered],
        name="turn",
    )
    history, terms = [], []
    for level in range(levels):
        received = swapped(message, "leaf", 1 << level)
        if level == 0:
            first_received = received
            side_tall = swapped(tall, "leaf", 1)
        if level == 1:
            received, back_points = lax.optimization_barrier((received, back_points))
        last = level == levels - 1
        if level and not last:
            made = call(
                functools.partial(term_kernel, sides, levels),
                [node_sums] + [shape((count, count), F32)] * (level == 1),
                [transfer] + history[-2:],
                flops=8 * dimension * count * count,
                name="sibling_term",
            )
            terms.append(made[0])
            if level == 1:
                product = made[1]
            passed = lax.optimization_barrier((passed, made[0]))[0]
        history += [coords, received]
        if level == levels - 2:
            near, held = call(
                back_kernel,
                [block_sums, block_sums],
                [tall, norms, ordered, back_points, back_ordered, marks]
                + [lax.optimization_barrier((near, passed))[0]],
                flops=tile_flops,
                exps=rows * rows,
                name="back_tile",
            )
            passed, held = lax.optimization_barrier((passed, held))
        if last:
            near, back, side = call(
                pair_kernel,
                [block_sums, block_values, block_values],
                [points, ordered, side_tall, back_points, back_ordered, marks, first_received]
                + [lax.optimization_barrier((near, passed))[0], held],
                scratch=[pltpu.VMEM((sides, rows), F32)],
                flops=tile_flops,
                exps=rows * rows,
                name="pair_tile",
            )
            passed, near = lax.optimization_barrier((passed, near))
            back = rotated(back, "leaf", -2)
            side = swapped(side, "leaf", 1)
        if last:
            outs = [shape((dimension + sides, count), BF16)]
        else:
            outs = [node_points, shape((dimension + 2 * sides, count), BF16), node_sums]
        results = call(
            functools.partial(round_kernel, level, last),
            outs,
            [skeletons, transfer, coords, passed, received],
            flops=(JOIN_FLOPS if level < 2 else 8) * dimension * count * count,
            name="join_level",
        )
        if not last:
            coords, message, passed = results
        if level == 0:
            (near,) = call(
                self_kernel,
                [block_sums],
                [tall, norms, points, lax.optimization_barrier((ordered, results[-1]))[0]],
                name="self_tile",
            )
            sent = lax.optimization_barrier((ordered, near))[0]
            back_ordered = shifted(sent, "leaf", 2)
    own_top = results[0]
    tops = [rotated(own_top, "grp", turn) for turn in range(1, groups)]
    (potential,) = call(
        functools.partial(last_terms_kernel, sides, levels),
        [node_sums],
        [transfer] + history[-4:] + terms,
        flops=8 * dimension * count * count,
        exps=count * count,
        name="last_terms",
    )
    (here,) = call(
        functools.partial(far_kernel, len(tops)),
        [block_sums],
        [own_top, potential, product, leaf_interp, near, side] + tops,
        flops=4 * sides * rows * count,
        name="far_field",
    )
    (out,) = call(total_kernel, [block_sums], [here, back], flops=2 * sides * rows, name="total")
    return out


def solution(mesh):
    in_specs = (
        P(None, ("leaf", "grp")),
        P(None, ("leaf", "grp")),
        P(("leaf", "grp")),
        P(("leaf", "grp"), None),
        P(("leaf", "grp"), None, None),
        P(None, ("leaf", "grp")),
        P(("leaf", "grp"), None, None, None),
    )
    out_specs = P(None, ("leaf", "grp"))
    return jax.shard_map(local, mesh=mesh, in_specs=in_specs, out_specs=out_specs, check_vma=False)
```

```python
import functools

import jax
import jax.numpy as jnp
from jax import lax
from jax.experimental import pallas as pl
from jax.experimental.pallas import tpu as pltpu
from jax.sharding import PartitionSpec as P

REACH = 2
BF16 = jnp.bfloat16
F32 = jnp.float32
LOG2E = 1.4426950408889634
PAD = 16
JOIN_FLOPS = 500
VMEM_LIMIT = 40 * 1024 * 1024
START_VMEM = 56 * 1024 * 1024

NN = ((1,), (0,))
NT = ((1,), (1,))
TN = ((0,), (0,))


def dot(left, right, contract=NN, precision=None):
    return lax.dot_general(
        left, right, (contract, ((), ())), preferred_element_type=F32, precision=precision
    )


def halves(value):
    high = value.astype(BF16)
    return high, (value - high.astype(F32)).astype(BF16)


def dot_split(left, right, contract=NN):
    rows = left.shape[0]
    both = dot(jnp.concatenate(halves(left), axis=0), right, contract)
    return both[:rows] + both[rows:]


def dot_parts(left, right):
    rows, columns = left.shape[0], right.shape[1]
    if left.dtype != BF16:
        left = jnp.concatenate(halves(left), axis=0)
    both = dot(left, jnp.concatenate(halves(right), axis=1))
    total = both[:rows, :columns] + both[:rows, columns:]
    if left.shape[0] > rows:
        total = total + (both[rows:, :columns] + both[rows:, columns:])
    return total


def row_norms(points):
    wide = points.astype(F32)
    return jnp.sum(wide * wide, axis=0, keepdims=True)


def column_norms(points):
    wide = points.astype(F32)
    high, low = halves(wide * wide)
    ones = jnp.ones((points.shape[0], 128), BF16)
    return dot(high, ones, TN) + dot(low, ones, TN)


def one_hot(index, rows, first):
    place = lax.broadcasted_iota(jnp.int32, (rows, index.shape[1]), 0) + first
    return jnp.where(place == index, 1.0, 0.0).astype(BF16)


def small_kernel(source, target):
    scale = 2.0 * LOG2E / source.shape[0]
    inner = dot(source, target, TN)
    squares = column_norms(source)[:, : target.shape[1]] + row_norms(target)
    return jnp.exp2(scale * (2.0 * inner - squares))


def pick(first, second, index, bit):
    count = first.shape[1]
    table = jnp.concatenate(
        [one_hot(index, count, count * bit), one_hot(index, count, count * (1 - bit))], axis=0
    )
    return dot(jnp.concatenate([first, second], axis=1), table).astype(BF16)


def write_message(weights, coords, matrix, message_ref, passed_ref):
    dimension, sides = coords.shape[0], weights.shape[0]
    passed = dot_split(weights, matrix, NT)
    message_ref[:dimension] = coords
    message_ref[dimension : dimension + sides] = weights.astype(BF16)
    message_ref[dimension + sides : dimension + 2 * sides] = passed.astype(BF16)
    passed_ref[...] = passed


def start_kernel(*refs):
    inputs, outs, held = refs[:7], refs[7:12], refs[12:19]
    made, sems, out_sems = refs[19:24], refs[24], refs[25]
    copies = [
        pltpu.make_async_copy(source, target, sems.at[number])
        for number, (source, target) in enumerate(zip(inputs, held))
    ]
    for copy in copies:
        copy.start()
    stores = [
        pltpu.make_async_copy(source, target, out_sems.at[number])
        for number, (source, target) in enumerate(zip(made, outs))
    ]
    order, skeletons, mask, charges, points, interp, transfer = held
    ordered_ref, coords_ref, marks_ref, message_ref, passed_ref = made
    dimension, rows = points.shape
    sides, count = passed_ref.shape
    for copy in copies[:4]:
        copy.wait()
    width = rows // 4
    for column in range(0, rows, width):
        table = one_hot(order[:, column : column + width], rows, 0)
        ordered_ref[:, column : column + width] = dot(charges[...], table).astype(BF16)
    stores[0].start()
    copies[4].wait()
    coords = dot(points[...], one_hot(skeletons[0], rows, 0)).astype(BF16)
    coords_ref[...] = coords
    stores[1].start()
    lane = lax.broadcasted_iota(jnp.int32, (1, count), 1)
    pattern = jnp.zeros((1, count), jnp.int32)
    for offset in range(mask.shape[1]):
        pattern = jnp.where(lane == offset, mask[:, offset : offset + 1], pattern)
    marks = jnp.broadcast_to(pattern.astype(F32), (PAD, count)).astype(BF16)
    marks_ref[...] = marks
    message_ref[dimension + 2 * sides :] = marks
    stores[2].start()
    copies[5].wait()
    weights = dot(ordered_ref[...], interp[...], NT)
    copies[6].wait()
    write_message(weights, coords, transfer[0], message_ref, passed_ref)
    stores[3].start()
    stores[4].start()
    for store in stores:
        store.wait()


def marked(marks, offset):
    rows = marks.astype(F32)
    lane = lax.broadcasted_iota(jnp.int32, rows.shape, 1)
    return jnp.max(jnp.where(lane == REACH + offset, rows, 0.0)) > 0.5


def round_kernel(level, last, skeletons, transfer, coords, passed, message, *outs):
    dimension = coords.shape[0]
    sides = passed.shape[0]
    bit = (lax.axis_index("leaf") >> level) & 1
    joined = pick(coords[...], message[:dimension], skeletons[level + 1], bit)
    span = slice(dimension + sides, dimension + 2 * sides)
    weights = passed[...] + message[span].astype(F32)
    if last:
        outs[0][:dimension] = joined
        outs[0][dimension:] = weights.astype(BF16)
        return
    outs[0][...] = joined
    write_message(weights, joined, transfer[level + 1], outs[1], outs[2])


def sibling_term(coords, message, sides):
    dimension = coords.shape[0]
    weights = message[dimension : dimension + sides]
    return dot_parts(weights, small_kernel(message[:dimension], coords[...]))


def term_kernel(sides, levels, transfer, coords, message, term_ref, *product_ref):
    term_ref[...] = sibling_term(coords, message, sides)
    if product_ref:
        product = transfer[levels - 1].astype(F32)
        for level in range(levels - 2, -1, -1):
            product = dot_split(product, transfer[level])
        product_ref[0][...] = product


def last_terms_kernel(sides, levels, transfer, *refs):
    pairs, terms, potential_ref = refs[:4], refs[4:-1], refs[-1]
    late = [sibling_term(pairs[0], pairs[1], sides), sibling_term(pairs[2], pairs[3], sides)]
    terms = [ref[...] for ref in terms] + late
    potential = terms[-1]
    for level in range(levels - 2, -1, -1):
        potential = dot_split(potential, transfer[level]) + terms[level]
    potential_ref[...] = potential


def lane_norms(tall):
    square = jnp.square(tall.astype(F32))
    norms = jnp.sum(square, axis=1, keepdims=True) * (2.0 * LOG2E / tall.shape[1])
    return jnp.broadcast_to(norms, (tall.shape[0], 128))


def turn_kernel(points, ordered, tall_ref, norms_ref):
    dimension, rows = points.shape
    sides = ordered.shape[0]
    tall_ref[:rows] = jnp.transpose(points[...])
    norms_ref[...] = lane_norms(tall_ref[:rows])
    for number in range(rows // dimension):
        first = rows + number * sides
        tall_ref[first : first + sides] = ordered[:, number * dimension : (number + 1) * dimension]


def bands(tall, norms, wide):
    dimension, rows = wide.shape
    scale = 2.0 * LOG2E / dimension
    target_norms = row_norms(wide[...]) * scale
    for row in range(0, rows, dimension):
        band = slice(row, row + dimension)
        source = tall[band]
        inner = dot(source, wide[...])
        own = lane_norms(source) if norms is None else norms[band]
        squares = jnp.tile(own, (1, rows // 128)) + target_norms
        yield band, jnp.exp2((2.0 * scale) * inner - squares).astype(BF16)


def self_kernel(tall, norms, wide, ordered, near_ref):
    for band, tile in bands(tall, norms, wide):
        near_ref[:, band] = dot(ordered[...], tile, NT)


def back_kernel(tall, norms, ordered, back_wide, back_ordered, marks, near, near_ref, held_ref):
    near_ref[...] = near[...]
    used = marked(marks[...], -2)

    @pl.when(used)
    def _():
        for band, tile in bands(tall, norms, back_wide):
            near_ref[:, band] += dot(back_ordered[...], tile, NT)
            part = dot(ordered[:, band], tile)
            if band.start:
                held_ref[...] += part
            else:
                held_ref[...] = part

    @pl.when(jnp.logical_not(used))
    def _():
        held_ref[...] = jnp.zeros_like(held_ref)


def pair_kernel(wide, ordered, side_tall, back_wide, back_ordered, marks, message, near, held,
                near_ref, back_ref, side_ref, sum_ref):
    dimension, rows = wide.shape
    sides = ordered.shape[0]
    odd = lax.rem(lax.axis_index("leaf"), 2)
    go_odd = jnp.logical_and(odd == 1, marked(message[message.shape[0] - PAD :], -1))
    go_even = jnp.logical_and(odd == 0, marked(marks[...], 1))

    def pair(other_wide, other_ordered):
        for band, tile in bands(side_tall, None, other_wide):
            side_ref[:, band] = dot(other_ordered[...], tile, NT).astype(BF16)
            first = rows + band.start // dimension * sides
            part = dot(side_tall[first : first + sides], tile)
            if band.start:
                sum_ref[...] += part
            else:
                sum_ref[...] = part

    @pl.when(go_odd)
    def _():
        pair(back_wide, back_ordered)
        back_ref[...] = (held[...] + sum_ref[...]).astype(BF16)
        near_ref[...] = near[...]

    @pl.when(go_even)
    def _():
        pair(wide, ordered)
        back_ref[...] = held[...].astype(BF16)
        near_ref[...] = near[...] + sum_ref[...]

    @pl.when(jnp.logical_not(jnp.logical_or(go_odd, go_even)))
    def _():
        back_ref[...] = held[...].astype(BF16)
        near_ref[...] = near[...]
        side_ref[...] = jnp.zeros_like(side_ref)


def far_kernel(others, own_top, potential, product, interp, near, side, *refs):
    tops, out_ref = refs[:others], refs[-1]
    sides = out_ref.shape[0]
    dimension = own_top.shape[0] - sides
    total = potential[...]
    above = None
    for top in tops:
        part = dot_parts(top[dimension:], small_kernel(top[:dimension], own_top[:dimension]))
        above = part if above is None else above + part
    if above is not None:
        total = total + dot_parts(above, product[...])
    out_ref[...] = (near[...] + side[...].astype(F32)) + dot_split(total, interp[...])


def total_kernel(here, back, out_ref):
    out_ref[...] = here[...] + back[...].astype(F32)


def call(kernel, outs, args, scratch=(), anywhere=False, flops=0, exps=0, name=None):
    vmem = pl.BlockSpec(memory_space=pltpu.VMEM)
    rest = pl.BlockSpec(memory_space=pl.ANY) if anywhere else vmem
    moved = 0 if anywhere or flops == 0 else sum(a.size * a.dtype.itemsize for a in list(args) + list(outs))
    return pl.pallas_call(
        kernel,
        out_shape=outs,
        in_specs=[rest] * len(args),
        out_specs=[rest if anywhere else vmem] * len(outs),
        scratch_shapes=list(scratch),
        compiler_params=pltpu.CompilerParams(
            vmem_limit_bytes=START_VMEM if anywhere else VMEM_LIMIT
        ),
        cost_estimate=pl.CostEstimate(flops=flops, bytes_accessed=moved, transcendentals=exps),
        name=name,
    )(*args)


def swapped(value, axis, flip):
    count = lax.axis_size(axis)
    return lax.ppermute(value, axis, [(place, place ^ flip) for place in range(count)])


def rotated(value, axis, turn):
    count = lax.axis_size(axis)
    return lax.ppermute(value, axis, [(place, (place + turn) % count) for place in range(count)])


def shape(dims, dtype):
    return jax.ShapeDtypeStruct(dims, dtype)


def local(points, charges, order, near_mask, skeletons, leaf_interp, transfer):
    dimension, rows = points.shape
    sides, count = charges.shape[0], leaf_interp.shape[0]
    leaves, groups = lax.axis_size("leaf"), lax.axis_size("grp")
    levels = leaves.bit_length() - 1
    skeletons = jnp.transpose(skeletons, (1, 0, 2))
    transfer = transfer[0]
    block_sums = shape((sides, rows), F32)
    block_values = shape((sides, rows), BF16)
    node_points = shape((dimension, count), BF16)
    node_sums = shape((sides, count), F32)
    tile_flops = 2 * rows * rows * (dimension + 2 * sides)

    back_points = rotated(points, "leaf", 2)

    inputs = [order.reshape(1, rows), skeletons, near_mask, charges, points, leaf_interp, transfer]
    made = [
        block_values,
        node_points,
        shape((PAD, count), BF16),
        shape((dimension + 2 * sides + PAD, count), BF16),
        node_sums,
    ]
    ordered, coords, marks, message, passed = call(
        start_kernel,
        made,
        inputs,
        scratch=[pltpu.VMEM(value.shape, value.dtype) for value in inputs + made]
        + [pltpu.SemaphoreType.DMA((len(inputs),)), pltpu.SemaphoreType.DMA((len(made),))],
        anywhere=True,
        name="start",
    )
    tall, norms = call(
        turn_kernel,
        [shape((rows + sides * rows // dimension, dimension), BF16), shape((rows, 128), F32)],
        [points, ordered],
        name="turn",
    )
    history, terms = [], []
    for level in range(levels):
        received = swapped(message, "leaf", 1 << level)
        if level == 0:
            first_received = received
            side_tall = swapped(tall, "leaf", 1)
        if level == 1:
            received, back_points = lax.optimization_barrier((received, back_points))
        last = level == levels - 1
        if level and not last:
            made = call(
                functools.partial(term_kernel, sides, levels),
                [node_sums] + [shape((count, count), F32)] * (level == 1),
                [transfer] + history[-2:],
                flops=8 * dimension * count * count,
                name="sibling_term",
            )
            terms.append(made[0])
            if level == 1:
                product = made[1]
            passed = lax.optimization_barrier((passed, made[0]))[0]
        history += [coords, received]
        if level == levels - 2:
            near, held = call(
                back_kernel,
                [block_sums, block_sums],
                [tall, norms, ordered, back_points, back_ordered, marks]
                + [lax.optimization_barrier((near, passed))[0]],
                flops=tile_flops,
                exps=rows * rows,
                name="back_tile",
            )
            passed, held = lax.optimization_barrier((passed, held))
        if last:
            near, back, side = call(
                pair_kernel,
                [block_sums, block_values, block_values],
                [points, ordered, side_tall, back_points, back_ordered, marks, first_received]
                + [lax.optimization_barrier((near, passed))[0], held],
                scratch=[pltpu.VMEM((sides, rows), F32)],
                flops=tile_flops,
                exps=rows * rows,
                name="pair_tile",
            )
            passed, near = lax.optimization_barrier((passed, near))
            back = rotated(back, "leaf", -2)
            side = swapped(side, "leaf", 1)
        if last:
            outs = [shape((dimension + sides, count), BF16)]
        else:
            outs = [node_points, shape((dimension + 2 * sides, count), BF16), node_sums]
        results = call(
            functools.partial(round_kernel, level, last),
            outs,
            [skeletons, transfer, coords, passed, received],
            flops=(JOIN_FLOPS if level < 2 else 8) * dimension * count * count,
            name="join_level",
        )
        if not last:
            coords, message, passed = results
        if level == 0:
            (near,) = call(
                self_kernel,
                [block_sums],
                [tall, norms, points, lax.optimization_barrier((ordered, results[-1]))[0]],
                name="self_tile",
            )
            sent = lax.optimization_barrier((ordered, near))[0]
            back_ordered = rotated(sent, "leaf", 2)
    own_top = results[0]
    tops = [rotated(own_top, "grp", turn) for turn in range(1, groups)]
    (potential,) = call(
        functools.partial(last_terms_kernel, sides, levels),
        [node_sums],
        [transfer] + history[-4:] + terms,
        flops=8 * dimension * count * count,
        exps=count * count,
        name="last_terms",
    )
    (here,) = call(
        functools.partial(far_kernel, len(tops)),
        [block_sums],
        [own_top, potential, product, leaf_interp, near, side] + tops,
        flops=4 * sides * rows * count,
        name="far_field",
    )
    (out,) = call(total_kernel, [block_sums], [here, back], flops=2 * sides * rows, name="total")
    return out


def solution(mesh):
    in_specs = (
        P(None, ("leaf", "grp")),
        P(None, ("leaf", "grp")),
        P(("leaf", "grp")),
        P(("leaf", "grp"), None),
        P(("leaf", "grp"), None, None),
        P(None, ("leaf", "grp")),
        P(("leaf", "grp"), None, None, None),
    )
    out_specs = P(None, ("leaf", "grp"))
    return jax.shard_map(local, mesh=mesh, in_specs=in_specs, out_specs=out_specs, check_vma=False)
```

```python
import functools

import jax
import jax.numpy as jnp
from jax import lax
from jax.experimental import pallas as pl
from jax.experimental.pallas import tpu as pltpu
from jax.sharding import PartitionSpec as P

REACH = 2
BF16 = jnp.bfloat16
F32 = jnp.float32
LOG2E = 1.4426950408889634
PAD = 16
JOIN_FLOPS = 500
VMEM_LIMIT = 40 * 1024 * 1024
START_VMEM = 56 * 1024 * 1024

NN = ((1,), (0,))
NT = ((1,), (1,))
TN = ((0,), (0,))


def dot(left, right, contract=NN, precision=None):
    return lax.dot_general(
        left, right, (contract, ((), ())), preferred_element_type=F32, precision=precision
    )


def halves(value):
    high = value.astype(BF16)
    return high, (value - high.astype(F32)).astype(BF16)


def dot_split(left, right, contract=NN):
    rows = left.shape[0]
    both = dot(jnp.concatenate(halves(left), axis=0), right, contract)
    return both[:rows] + both[rows:]


def dot_parts(left, right):
    rows, columns = left.shape[0], right.shape[1]
    if left.dtype != BF16:
        left = jnp.concatenate(halves(left), axis=0)
    both = dot(left, jnp.concatenate(halves(right), axis=1))
    total = both[:rows, :columns] + both[:rows, columns:]
    if left.shape[0] > rows:
        total = total + (both[rows:, :columns] + both[rows:, columns:])
    return total


def row_norms(points):
    wide = points.astype(F32)
    return jnp.sum(wide * wide, axis=0, keepdims=True)


def column_norms(points):
    wide = points.astype(F32)
    high, low = halves(wide * wide)
    ones = jnp.ones((points.shape[0], 128), BF16)
    return dot(high, ones, TN) + dot(low, ones, TN)


def one_hot(index, rows, first):
    place = lax.broadcasted_iota(jnp.int32, (rows, index.shape[1]), 0) + first
    return jnp.where(place == index, 1.0, 0.0).astype(BF16)


def small_kernel(source, target):
    scale = 2.0 * LOG2E / source.shape[0]
    inner = dot(source, target, TN)
    squares = column_norms(source)[:, : target.shape[1]] + row_norms(target)
    return jnp.exp2(scale * (2.0 * inner - squares))


def pick(first, second, index, bit):
    count = first.shape[1]
    table = jnp.concatenate(
        [one_hot(index, count, count * bit), one_hot(index, count, count * (1 - bit))], axis=0
    )
    return dot(jnp.concatenate([first, second], axis=1), table).astype(BF16)


def write_message(weights, coords, matrix, message_ref, passed_ref):
    dimension, sides = coords.shape[0], weights.shape[0]
    passed = dot_split(weights, matrix, NT)
    message_ref[:dimension] = coords
    message_ref[dimension : dimension + sides] = weights.astype(BF16)
    message_ref[dimension + sides : dimension + 2 * sides] = passed.astype(BF16)
    passed_ref[...] = passed


def start_kernel(*refs):
    inputs, outs, held = refs[:7], refs[7:12], refs[12:19]
    made, sems, out_sems = refs[19:24], refs[24], refs[25]
    copies = [
        pltpu.make_async_copy(source, target, sems.at[number])
        for number, (source, target) in enumerate(zip(inputs, held))
    ]
    for copy in copies:
        copy.start()
    stores = [
        pltpu.make_async_copy(source, target, out_sems.at[number])
        for number, (source, target) in enumerate(zip(made, outs))
    ]
    order, skeletons, mask, charges, points, interp, transfer = held
    ordered_ref, coords_ref, marks_ref, message_ref, passed_ref = made
    dimension, rows = points.shape
    sides, count = passed_ref.shape
    for copy in copies[:4]:
        copy.wait()
    width = rows // 4
    for column in range(0, rows, width):
        table = one_hot(order[:, column : column + width], rows, 0)
        ordered_ref[:, column : column + width] = dot(charges[...], table).astype(BF16)
    stores[0].start()
    copies[4].wait()
    coords = dot(points[...], one_hot(skeletons[0], rows, 0)).astype(BF16)
    coords_ref[...] = coords
    stores[1].start()
    lane = lax.broadcasted_iota(jnp.int32, (1, count), 1)
    pattern = jnp.zeros((1, count), jnp.int32)
    for offset in range(mask.shape[1]):
        pattern = jnp.where(lane == offset, mask[:, offset : offset + 1], pattern)
    marks = jnp.broadcast_to(pattern.astype(F32), (PAD, count)).astype(BF16)
    marks_ref[...] = marks
    message_ref[dimension + 2 * sides :] = marks
    stores[2].start()
    copies[5].wait()
    weights = dot(ordered_ref[...], interp[...], NT)
    copies[6].wait()
    write_message(weights, coords, transfer[0], message_ref, passed_ref)
    stores[3].start()
    stores[4].start()
    for store in stores:
        store.wait()


def marked(marks, offset):
    rows = marks.astype(F32)
    lane = lax.broadcasted_iota(jnp.int32, rows.shape, 1)
    return jnp.max(jnp.where(lane == REACH + offset, rows, 0.0)) > 0.5


def round_kernel(level, last, skeletons, transfer, coords, passed, message, *outs):
    dimension = coords.shape[0]
    sides = passed.shape[0]
    bit = (lax.axis_index("leaf") >> level) & 1
    joined = pick(coords[...], message[:dimension], skeletons[level + 1], bit)
    span = slice(dimension + sides, dimension + 2 * sides)
    weights = passed[...] + message[span].astype(F32)
    if last:
        outs[0][:dimension] = joined
        outs[0][dimension:] = weights.astype(BF16)
        return
    outs[0][...] = joined
    write_message(weights, joined, transfer[level + 1], outs[1], outs[2])


def sibling_term(coords, message, sides):
    dimension = coords.shape[0]
    weights = message[dimension : dimension + sides]
    return dot_parts(weights, small_kernel(message[:dimension], coords[...]))


def term_kernel(sides, levels, transfer, coords, message, term_ref, *product_ref):
    term_ref[...] = sibling_term(coords, message, sides)
    if product_ref:
        product = transfer[levels - 1].astype(F32)
        for level in range(levels - 2, -1, -1):
            product = dot_split(product, transfer[level])
        product_ref[0][...] = product


def last_terms_kernel(sides, levels, transfer, *refs):
    pairs, terms, potential_ref = refs[:4], refs[4:-1], refs[-1]
    late = [sibling_term(pairs[0], pairs[1], sides), sibling_term(pairs[2], pairs[3], sides)]
    terms = [ref[...] for ref in terms] + late
    potential = terms[-1]
    for level in range(levels - 2, -1, -1):
        potential = dot_split(potential, transfer[level]) + terms[level]
    potential_ref[...] = potential


def lane_norms(tall):
    square = jnp.square(tall.astype(F32))
    norms = jnp.sum(square, axis=1, keepdims=True) * (2.0 * LOG2E / tall.shape[1])
    return jnp.broadcast_to(norms, (tall.shape[0], 128))


def turn_kernel(points, ordered, tall_ref, norms_ref):
    dimension, rows = points.shape
    sides = ordered.shape[0]
    tall_ref[:rows] = jnp.transpose(points[...])
    norms_ref[...] = lane_norms(tall_ref[:rows])
    for number in range(rows // dimension):
        first = rows + number * sides
        tall_ref[first : first + sides] = ordered[:, number * dimension : (number + 1) * dimension]


def bands(tall, norms, wide):
    dimension, rows = wide.shape
    scale = 2.0 * LOG2E / dimension
    target_norms = row_norms(wide[...]) * scale
    for row in range(0, rows, dimension):
        band = slice(row, row + dimension)
        source = tall[band]
        inner = dot(source, wide[...])
        own = lane_norms(source) if norms is None else norms[band]
        squares = jnp.tile(own, (1, rows // 128)) + target_norms
        yield band, jnp.exp2((2.0 * scale) * inner - squares).astype(BF16)


def self_kernel(tall, norms, wide, ordered, near_ref):
    for band, tile in bands(tall, norms, wide):
        near_ref[:, band] = dot(ordered[...], tile, NT)


def back_kernel(tall, norms, ordered, back_wide, back_ordered, marks, near, near_ref, held_ref):
    near_ref[...] = near[...]
    used = marked(marks[...], -2)

    @pl.when(used)
    def _():
        for band, tile in bands(tall, norms, back_wide):
            near_ref[:, band] += dot(back_ordered[...], tile, NT)
            part = dot(ordered[:, band], tile)
            if band.start:
                held_ref[...] += part
            else:
                held_ref[...] = part

    @pl.when(jnp.logical_not(used))
    def _():
        held_ref[...] = jnp.zeros_like(held_ref)


def pair_kernel(wide, ordered, side_tall, back_wide, back_ordered, marks, message, near, held,
                near_ref, back_ref, side_ref, sum_ref):
    dimension, rows = wide.shape
    sides = ordered.shape[0]
    odd = lax.rem(lax.axis_index("leaf"), 2)
    go_odd = jnp.logical_and(odd == 1, marked(message[message.shape[0] - PAD :], -1))
    go_even = jnp.logical_and(odd == 0, marked(marks[...], 1))

    def pair(other_wide, other_ordered):
        for band, tile in bands(side_tall, None, other_wide):
            side_ref[:, band] = dot(other_ordered[...], tile, NT).astype(BF16)
            first = rows + band.start // dimension * sides
            part = dot(side_tall[first : first + sides], tile)
            if band.start:
                sum_ref[...] += part
            else:
                sum_ref[...] = part

    @pl.when(go_odd)
    def _():
        pair(back_wide, back_ordered)
        back_ref[...] = (held[...] + sum_ref[...]).astype(BF16)
        near_ref[...] = near[...]

    @pl.when(go_even)
    def _():
        pair(wide, ordered)
        back_ref[...] = held[...].astype(BF16)
        near_ref[...] = near[...] + sum_ref[...]

    @pl.when(jnp.logical_not(jnp.logical_or(go_odd, go_even)))
    def _():
        back_ref[...] = held[...].astype(BF16)
        near_ref[...] = near[...]
        side_ref[...] = jnp.zeros_like(side_ref)


def far_kernel(others, own_top, potential, product, interp, near, side, back, *refs):
    tops, out_ref = refs[:others], refs[-1]
    sides = out_ref.shape[0]
    dimension = own_top.shape[0] - sides
    total = potential[...]
    above = None
    for top in tops:
        part = dot_parts(top[dimension:], small_kernel(top[:dimension], own_top[:dimension]))
        above = part if above is None else above + part
    if above is not None:
        total = total + dot_parts(above, product[...])
    here = near[...] + (side[...].astype(F32) + back[...].astype(F32))
    out_ref[...] = here + dot_split(total, interp[...])


def call(kernel, outs, args, scratch=(), anywhere=False, flops=0, exps=0, name=None):
    vmem = pl.BlockSpec(memory_space=pltpu.VMEM)
    rest = pl.BlockSpec(memory_space=pl.ANY) if anywhere else vmem
    moved = 0 if anywhere or flops == 0 else sum(a.size * a.dtype.itemsize for a in list(args) + list(outs))
    return pl.pallas_call(
        kernel,
        out_shape=outs,
        in_specs=[rest] * len(args),
        out_specs=[rest if anywhere else vmem] * len(outs),
        scratch_shapes=list(scratch),
        compiler_params=pltpu.CompilerParams(
            vmem_limit_bytes=START_VMEM if anywhere else VMEM_LIMIT
        ),
        cost_estimate=pl.CostEstimate(flops=flops, bytes_accessed=moved, transcendentals=exps),
        name=name,
    )(*args)


def swapped(value, axis, flip):
    count = lax.axis_size(axis)
    return lax.ppermute(value, axis, [(place, place ^ flip) for place in range(count)])


def rotated(value, axis, turn):
    count = lax.axis_size(axis)
    return lax.ppermute(value, axis, [(place, (place + turn) % count) for place in range(count)])


def shifted(value, axis, step):
    places = range(lax.axis_size(axis))
    return lax.ppermute(
        value, axis, [(place, place + step) for place in places if place + step in places]
    )


def shape(dims, dtype):
    return jax.ShapeDtypeStruct(dims, dtype)


def local(points, charges, order, near_mask, skeletons, leaf_interp, transfer):
    dimension, rows = points.shape
    sides, count = charges.shape[0], leaf_interp.shape[0]
    leaves, groups = lax.axis_size("leaf"), lax.axis_size("grp")
    levels = leaves.bit_length() - 1
    skeletons = jnp.transpose(skeletons, (1, 0, 2))
    transfer = transfer[0]
    block_sums = shape((sides, rows), F32)
    block_values = shape((sides, rows), BF16)
    node_points = shape((dimension, count), BF16)
    node_sums = shape((sides, count), F32)
    tile_flops = 2 * rows * rows * (dimension + 2 * sides)

    back_points = rotated(points, "leaf", 2)

    inputs = [order.reshape(1, rows), skeletons, near_mask, charges, points, leaf_interp, transfer]
    made = [
        block_values,
        node_points,
        shape((PAD, count), BF16),
        shape((dimension + 2 * sides + PAD, count), BF16),
        node_sums,
    ]
    ordered, coords, marks, message, passed = call(
        start_kernel,
        made,
        inputs,
        scratch=[pltpu.VMEM(value.shape, value.dtype) for value in inputs + made]
        + [pltpu.SemaphoreType.DMA((len(inputs),)), pltpu.SemaphoreType.DMA((len(made),))],
        anywhere=True,
        name="start",
    )
    tall, norms = call(
        turn_kernel,
        [shape((rows + sides * rows // dimension, dimension), BF16), shape((rows, 128), F32)],
        [points, ordered],
        name="turn",
    )
    history, terms = [], []
    for level in range(levels):
        received = swapped(message, "leaf", 1 << level)
        if level == 0:
            first_received = received
            side_tall = swapped(tall, "leaf", 1)
        if level == 1:
            received, back_points = lax.optimization_barrier((received, back_points))
        last = level == levels - 1
        if level and not last:
            made = call(
                functools.partial(term_kernel, sides, levels),
                [node_sums] + [shape((count, count), F32)] * (level == 1),
                [transfer] + history[-2:],
                flops=8 * dimension * count * count,
                name="sibling_term",
            )
            terms.append(made[0])
            if level == 1:
                product = made[1]
            passed = lax.optimization_barrier((passed, made[0]))[0]
        history += [coords, received]
        if level == levels - 2:
            near, held = call(
                back_kernel,
                [block_sums, block_sums],
                [tall, norms, ordered, back_points, back_ordered, marks]
                + [lax.optimization_barrier((near, passed))[0]],
                flops=tile_flops,
                exps=rows * rows,
                name="back_tile",
            )
            passed, held = lax.optimization_barrier((passed, held))
        if last:
            near, back, side = call(
                pair_kernel,
                [block_sums, block_values, block_values],
                [points, ordered, side_tall, back_points, back_ordered, marks, first_received]
                + [lax.optimization_barrier((near, passed))[0], held],
                scratch=[pltpu.VMEM((sides, rows), F32)],
                flops=tile_flops,
                exps=rows * rows,
                name="pair_tile",
            )
            passed, near = lax.optimization_barrier((passed, near))
            back = rotated(back, "leaf", -2)
            side = swapped(side, "leaf", 1)
        if last:
            outs = [shape((dimension + sides, count), BF16)]
        else:
            outs = [node_points, shape((dimension + 2 * sides, count), BF16), node_sums]
        results = call(
            functools.partial(round_kernel, level, last),
            outs,
            [skeletons, transfer, coords, passed, received],
            flops=(JOIN_FLOPS if level < 2 else 8) * dimension * count * count,
            name="join_level",
        )
        if not last:
            coords, message, passed = results
        if level == 0:
            (near,) = call(
                self_kernel,
                [block_sums],
                [tall, norms, points, lax.optimization_barrier((ordered, results[-1]))[0]],
                name="self_tile",
            )
            sent = lax.optimization_barrier((ordered, near))[0]
            back_ordered = shifted(sent, "leaf", 2)
    own_top = results[0]
    tops = [rotated(own_top, "grp", turn) for turn in range(1, groups)]
    (potential,) = call(
        functools.partial(last_terms_kernel, sides, levels),
        [node_sums],
        [transfer] + history[-4:] + terms,
        flops=8 * dimension * count * count,
        exps=count * count,
        name="last_terms",
    )
    (out,) = call(
        functools.partial(far_kernel, len(tops)),
        [block_sums],
        [own_top, potential, product, leaf_interp, near, side, back] + tops,
        flops=4 * sides * rows * count,
        name="far_field",
    )
    return out


def solution(mesh):
    in_specs = (
        P(None, ("leaf", "grp")),
        P(None, ("leaf", "grp")),
        P(("leaf", "grp")),
        P(("leaf", "grp"), None),
        P(("leaf", "grp"), None, None),
        P(None, ("leaf", "grp")),
        P(("leaf", "grp"), None, None, None),
    )
    out_specs = P(None, ("leaf", "grp"))
    return jax.shard_map(local, mesh=mesh, in_specs=in_specs, out_specs=out_specs, check_vma=False)
```

```python
import functools

import jax
import jax.numpy as jnp
from jax import lax
from jax.experimental import pallas as pl
from jax.experimental.pallas import tpu as pltpu
from jax.sharding import PartitionSpec as P

REACH = 2
BF16 = jnp.bfloat16
F32 = jnp.float32
LOG2E = 1.4426950408889634
PAD = 16
JOIN_FLOPS = 500
VMEM_LIMIT = 40 * 1024 * 1024
START_VMEM = 56 * 1024 * 1024

NN = ((1,), (0,))
NT = ((1,), (1,))
TN = ((0,), (0,))


def dot(left, right, contract=NN, precision=None):
    return lax.dot_general(
        left, right, (contract, ((), ())), preferred_element_type=F32, precision=precision
    )


def halves(value):
    high = value.astype(BF16)
    return high, (value - high.astype(F32)).astype(BF16)


def dot_split(left, right, contract=NN):
    rows = left.shape[0]
    both = dot(jnp.concatenate(halves(left), axis=0), right, contract)
    return both[:rows] + both[rows:]


def dot_parts(left, right):
    rows, columns = left.shape[0], right.shape[1]
    if left.dtype != BF16:
        left = jnp.concatenate(halves(left), axis=0)
    both = dot(left, jnp.concatenate(halves(right), axis=1))
    total = both[:rows, :columns] + both[:rows, columns:]
    if left.shape[0] > rows:
        total = total + (both[rows:, :columns] + both[rows:, columns:])
    return total


def row_norms(points):
    wide = points.astype(F32)
    return jnp.sum(wide * wide, axis=0, keepdims=True)


def column_norms(points):
    wide = points.astype(F32)
    high, low = halves(wide * wide)
    ones = jnp.ones((points.shape[0], 128), BF16)
    return dot(high, ones, TN) + dot(low, ones, TN)


def one_hot(index, rows, first):
    place = lax.broadcasted_iota(jnp.int32, (rows, index.shape[1]), 0) + first
    return jnp.where(place == index, 1.0, 0.0).astype(BF16)


def small_kernel(source, target):
    scale = 2.0 * LOG2E / source.shape[0]
    inner = dot(source, target, TN)
    squares = column_norms(source)[:, : target.shape[1]] + row_norms(target)
    return jnp.exp2(scale * (2.0 * inner - squares))


def pick(first, second, index, bit):
    count = first.shape[1]
    table = jnp.concatenate(
        [one_hot(index, count, count * bit), one_hot(index, count, count * (1 - bit))], axis=0
    )
    return dot(jnp.concatenate([first, second], axis=1), table).astype(BF16)


def write_message(weights, coords, matrix, message_ref, passed_ref):
    dimension, sides = coords.shape[0], weights.shape[0]
    passed = dot_split(weights, matrix, NT)
    message_ref[:dimension] = coords
    message_ref[dimension : dimension + sides] = weights.astype(BF16)
    message_ref[dimension + sides : dimension + 2 * sides] = passed.astype(BF16)
    passed_ref[...] = passed


def start_kernel(*refs):
    inputs, outs, held = refs[:7], refs[7:12], refs[12:19]
    made, sems, out_sems = refs[19:24], refs[24], refs[25]
    copies = [
        pltpu.make_async_copy(source, target, sems.at[number])
        for number, (source, target) in enumerate(zip(inputs, held))
    ]
    for copy in copies:
        copy.start()
    stores = [
        pltpu.make_async_copy(source, target, out_sems.at[number])
        for number, (source, target) in enumerate(zip(made, outs))
    ]
    order, skeletons, mask, charges, points, interp, transfer = held
    ordered_ref, coords_ref, marks_ref, message_ref, passed_ref = made
    dimension, rows = points.shape
    sides, count = passed_ref.shape
    for copy in copies[:4]:
        copy.wait()
    width = rows // 4
    for column in range(0, rows, width):
        table = one_hot(order[:, column : column + width], rows, 0)
        ordered_ref[:, column : column + width] = dot(charges[...], table).astype(BF16)
    stores[0].start()
    copies[4].wait()
    coords = dot(points[...], one_hot(skeletons[0], rows, 0)).astype(BF16)
    coords_ref[...] = coords
    stores[1].start()
    lane = lax.broadcasted_iota(jnp.int32, (1, count), 1)
    pattern = jnp.zeros((1, count), jnp.int32)
    for offset in range(mask.shape[1]):
        pattern = jnp.where(lane == offset, mask[:, offset : offset + 1], pattern)
    marks = jnp.broadcast_to(pattern.astype(F32), (PAD, count)).astype(BF16)
    marks_ref[...] = marks
    message_ref[dimension + 2 * sides :] = marks
    stores[2].start()
    copies[5].wait()
    weights = dot(ordered_ref[...], interp[...], NT)
    copies[6].wait()
    write_message(weights, coords, transfer[0], message_ref, passed_ref)
    stores[3].start()
    stores[4].start()
    for store in stores:
        store.wait()


def marked(marks, offset):
    rows = marks.astype(F32)
    lane = lax.broadcasted_iota(jnp.int32, rows.shape, 1)
    return jnp.max(jnp.where(lane == REACH + offset, rows, 0.0)) > 0.5


def round_kernel(level, last, skeletons, transfer, coords, passed, message, *outs):
    dimension = coords.shape[0]
    sides = passed.shape[0]
    bit = (lax.axis_index("leaf") >> level) & 1
    joined = pick(coords[...], message[:dimension], skeletons[level + 1], bit)
    span = slice(dimension + sides, dimension + 2 * sides)
    weights = passed[...] + message[span].astype(F32)
    if last:
        outs[0][:dimension] = joined
        outs[0][dimension:] = weights.astype(BF16)
        return
    outs[0][...] = joined
    write_message(weights, joined, transfer[level + 1], outs[1], outs[2])


def sibling_term(coords, message, sides):
    dimension = coords.shape[0]
    weights = message[dimension : dimension + sides]
    return dot_parts(weights, small_kernel(message[:dimension], coords[...]))


def term_kernel(sides, levels, transfer, coords, message, term_ref, *product_ref):
    term_ref[...] = sibling_term(coords, message, sides)
    if product_ref:
        product = transfer[levels - 1].astype(F32)
        for level in range(levels - 2, -1, -1):
            product = dot_split(product, transfer[level])
        product_ref[0][...] = product


def last_terms_kernel(sides, levels, transfer, *refs):
    pairs, terms, potential_ref = refs[:4], refs[4:-1], refs[-1]
    late = [sibling_term(pairs[0], pairs[1], sides), sibling_term(pairs[2], pairs[3], sides)]
    terms = [ref[...] for ref in terms] + late
    potential = terms[-1]
    for level in range(levels - 2, -1, -1):
        potential = dot_split(potential, transfer[level]) + terms[level]
    potential_ref[...] = potential


def lane_norms(tall):
    square = jnp.square(tall.astype(F32))
    norms = jnp.sum(square, axis=1, keepdims=True) * (2.0 * LOG2E / tall.shape[1])
    return jnp.broadcast_to(norms, (tall.shape[0], 128))


def turn_kernel(points, ordered, tall_ref, norms_ref):
    dimension, rows = points.shape
    sides = ordered.shape[0]
    tall_ref[:rows] = jnp.transpose(points[...])
    norms_ref[...] = lane_norms(tall_ref[:rows])
    for number in range(rows // dimension):
        first = rows + number * sides
        tall_ref[first : first + sides] = ordered[:, number * dimension : (number + 1) * dimension]


def bands(tall, norms, wide):
    dimension, rows = wide.shape
    scale = 2.0 * LOG2E / dimension
    target_norms = row_norms(wide[...]) * scale
    for row in range(0, rows, dimension):
        band = slice(row, row + dimension)
        source = tall[band]
        inner = dot(source, wide[...])
        own = lane_norms(source) if norms is None else norms[band]
        squares = jnp.tile(own, (1, rows // 128)) + target_norms
        yield band, jnp.exp2((2.0 * scale) * inner - squares).astype(BF16)


def self_kernel(tall, norms, wide, ordered, near_ref):
    for band, tile in bands(tall, norms, wide):
        near_ref[:, band] = dot(ordered[...], tile, NT)


def back_kernel(tall, norms, ordered, back_wide, back_ordered, marks, near, near_ref, held_ref):
    near_ref[...] = near[...]
    used = marked(marks[...], -2)

    @pl.when(used)
    def _():
        for band, tile in bands(tall, norms, back_wide):
            near_ref[:, band] += dot(back_ordered[...], tile, NT)
            part = dot(ordered[:, band], tile)
            if band.start:
                held_ref[...] += part
            else:
                held_ref[...] = part

    @pl.when(jnp.logical_not(used))
    def _():
        held_ref[...] = jnp.zeros_like(held_ref)


def pair_kernel(wide, ordered, side_tall, back_wide, back_ordered, marks, message, near, held,
                near_ref, back_ref, side_ref, sum_ref):
    dimension, rows = wide.shape
    sides = ordered.shape[0]
    odd = lax.rem(lax.axis_index("leaf"), 2)
    go_odd = jnp.logical_and(odd == 1, marked(message[message.shape[0] - PAD :], -1))
    go_even = jnp.logical_and(odd == 0, marked(marks[...], 1))

    def pair(other_wide, other_ordered):
        for band, tile in bands(side_tall, None, other_wide):
            side_ref[:, band] = dot(other_ordered[...], tile, NT).astype(BF16)
            first = rows + band.start // dimension * sides
            part = dot(side_tall[first : first + sides], tile)
            if band.start:
                sum_ref[...] += part
            else:
                sum_ref[...] = part

    @pl.when(go_odd)
    def _():
        pair(back_wide, back_ordered)
        back_ref[...] = (held[...] + sum_ref[...]).astype(BF16)
        near_ref[...] = near[...]

    @pl.when(go_even)
    def _():
        pair(wide, ordered)
        back_ref[...] = held[...].astype(BF16)
        near_ref[...] = near[...] + sum_ref[...]

    @pl.when(jnp.logical_not(jnp.logical_or(go_odd, go_even)))
    def _():
        back_ref[...] = held[...].astype(BF16)
        near_ref[...] = near[...]
        side_ref[...] = jnp.zeros_like(side_ref)


def far_kernel(others, own_top, potential, product, interp, near, side, *refs):
    tops, out_ref = refs[:others], refs[-1]
    sides = out_ref.shape[0]
    dimension = own_top.shape[0] - sides
    total = potential[...]
    above = None
    for top in tops:
        part = dot_parts(top[dimension:], small_kernel(top[:dimension], own_top[:dimension]))
        above = part if above is None else above + part
    if above is not None:
        total = total + dot_parts(above, product[...])
    out_ref[...] = (near[...] + side[...].astype(F32)) + dot_split(total, interp[...])


def total_kernel(here, back, out_ref):
    out_ref[...] = here[...] + back[...].astype(F32)


def call(kernel, outs, args, scratch=(), anywhere=False, flops=0, exps=0, name=None):
    vmem = pl.BlockSpec(memory_space=pltpu.VMEM)
    rest = pl.BlockSpec(memory_space=pl.ANY) if anywhere else vmem
    moved = 0 if anywhere or flops == 0 else sum(a.size * a.dtype.itemsize for a in list(args) + list(outs))
    return pl.pallas_call(
        kernel,
        out_shape=outs,
        in_specs=[rest] * len(args),
        out_specs=[rest if anywhere else vmem] * len(outs),
        scratch_shapes=list(scratch),
        compiler_params=pltpu.CompilerParams(
            vmem_limit_bytes=START_VMEM if anywhere else VMEM_LIMIT
        ),
        cost_estimate=pl.CostEstimate(flops=flops, bytes_accessed=moved, transcendentals=exps),
        name=name,
    )(*args)


def swapped(value, axis, flip):
    count = lax.axis_size(axis)
    return lax.ppermute(value, axis, [(place, place ^ flip) for place in range(count)])


def rotated(value, axis, turn):
    count = lax.axis_size(axis)
    return lax.ppermute(value, axis, [(place, (place + turn) % count) for place in range(count)])


def shifted(value, axis, step):
    places = range(lax.axis_size(axis))
    return lax.ppermute(
        value, axis, [(place, place + step) for place in places if place + step in places]
    )


def shape(dims, dtype):
    return jax.ShapeDtypeStruct(dims, dtype)


def local(points, charges, order, near_mask, skeletons, leaf_interp, transfer):
    dimension, rows = points.shape
    sides, count = charges.shape[0], leaf_interp.shape[0]
    leaves, groups = lax.axis_size("leaf"), lax.axis_size("grp")
    levels = leaves.bit_length() - 1
    skeletons = jnp.transpose(skeletons, (1, 0, 2))
    transfer = transfer[0]
    block_sums = shape((sides, rows), F32)
    block_values = shape((sides, rows), BF16)
    node_points = shape((dimension, count), BF16)
    node_sums = shape((sides, count), F32)
    tile_flops = 2 * rows * rows * (dimension + 2 * sides)

    back_points = rotated(points, "leaf", 2)

    inputs = [order.reshape(1, rows), skeletons, near_mask, charges, points, leaf_interp, transfer]
    made = [
        block_values,
        node_points,
        shape((PAD, count), BF16),
        shape((dimension + 2 * sides + PAD, count), BF16),
        node_sums,
    ]
    ordered, coords, marks, message, passed = call(
        start_kernel,
        made,
        inputs,
        scratch=[pltpu.VMEM(value.shape, value.dtype) for value in inputs + made]
        + [pltpu.SemaphoreType.DMA((len(inputs),)), pltpu.SemaphoreType.DMA((len(made),))],
        anywhere=True,
        name="start",
    )
    tall, norms = call(
        turn_kernel,
        [shape((rows + sides * rows // dimension, dimension), BF16), shape((rows, 128), F32)],
        [points, ordered],
        name="turn",
    )
    history, terms = [], []
    for level in range(levels):
        received = swapped(message, "leaf", 1 << level)
        if level == 0:
            first_received = received
            side_tall = swapped(tall, "leaf", 1)
        if level == 1:
            received, back_points = lax.optimization_barrier((received, back_points))
        last = level == levels - 1
        if level and not last:
            made = call(
                functools.partial(term_kernel, sides, levels),
                [node_sums] + [shape((count, count), F32)] * (level == 1),
                [transfer] + history[-2:],
                flops=8 * dimension * count * count,
                name="sibling_term",
            )
            terms.append(made[0])
            if level == 1:
                product = made[1]
                passed = lax.optimization_barrier((passed, made[0]))[0]
        history += [coords, received]
        if level == levels - 2:
            near, held = call(
                back_kernel,
                [block_sums, block_sums],
                [tall, norms, ordered, back_points, back_ordered, marks]
                + [lax.optimization_barrier((near, passed))[0]],
                flops=tile_flops,
                exps=rows * rows,
                name="back_tile",
            )
            passed, held = lax.optimization_barrier((passed, held))
        if last:
            near, back, side = call(
                pair_kernel,
                [block_sums, block_values, block_values],
                [points, ordered, side_tall, back_points, back_ordered, marks, first_received]
                + [lax.optimization_barrier((near, passed))[0], held],
                scratch=[pltpu.VMEM((sides, rows), F32)],
                flops=tile_flops,
                exps=rows * rows,
                name="pair_tile",
            )
            passed, near, terms = lax.optimization_barrier((passed, near, terms))
            back = rotated(back, "leaf", -2)
            side = swapped(side, "leaf", 1)
        if last:
            outs = [shape((dimension + sides, count), BF16)]
        else:
            outs = [node_points, shape((dimension + 2 * sides, count), BF16), node_sums]
        results = call(
            functools.partial(round_kernel, level, last),
            outs,
            [skeletons, transfer, coords, passed, received],
            flops=(JOIN_FLOPS if level < 2 else 8) * dimension * count * count,
            name="join_level",
        )
        if not last:
            coords, message, passed = results
        if level == 0:
            (near,) = call(
                self_kernel,
                [block_sums],
                [tall, norms, points, lax.optimization_barrier((ordered, results[-1]))[0]],
                name="self_tile",
            )
            sent = lax.optimization_barrier((ordered, near))[0]
            back_ordered = shifted(sent, "leaf", 2)
    own_top = results[0]
    tops = [rotated(own_top, "grp", turn) for turn in range(1, groups)]
    (potential,) = call(
        functools.partial(last_terms_kernel, sides, levels),
        [node_sums],
        [transfer] + history[-4:] + terms,
        flops=8 * dimension * count * count,
        exps=count * count,
        name="last_terms",
    )
    (here,) = call(
        functools.partial(far_kernel, len(tops)),
        [block_sums],
        [own_top, potential, product, leaf_interp, near, side] + tops,
        flops=4 * sides * rows * count,
        name="far_field",
    )
    (out,) = call(total_kernel, [block_sums], [here, back], flops=2 * sides * rows, name="total")
    return out


def solution(mesh):
    in_specs = (
        P(None, ("leaf", "grp")),
        P(None, ("leaf", "grp")),
        P(("leaf", "grp")),
        P(("leaf", "grp"), None),
        P(("leaf", "grp"), None, None),
        P(None, ("leaf", "grp")),
        P(("leaf", "grp"), None, None, None),
    )
    out_specs = P(None, ("leaf", "grp"))
    return jax.shard_map(local, mesh=mesh, in_specs=in_specs, out_specs=out_specs, check_vma=False)
```
